32 devices in a mesh: grp: 2 (over x), orbit: 16 (over z, y, core).
Axes of the slice: x: 2, y: 2, z: 4, core: 2. Of those that a mesh axis runs over, the one named last changes fastest.
Arguments:
- solution: float32 [256, 8, 16, 128], P(('grp', 'orbit')), parts along dimension 0, may hold values from -6 to 6
- residual: float32 [256, 8, 16, 128], P(('grp', 'orbit')), parts along dimension 0, may hold values from -9 to 9
- direction: float32 [256, 8, 16, 128], P(('grp', 'orbit')), parts along dimension 0, may hold values from -9 to 9
- jacobian: bfloat16 [256, 24, 128, 128], P(('grp', 'orbit')), parts along dimension 0, may hold values from -0.109375 to 0.109375
- crossing: int32 [256, 24], P(('grp', 'orbit')), parts along dimension 0, may hold values from 0 to 127
- tile_count: int32 [32], P(('grp', 'orbit')), parts along dimension 0, may hold values from 1 to 8, as said below
- sightline_weight: float32 [256, 128], P(('grp', 'orbit')), parts along dimension 0, may hold values from 1 to 8
- length_class: int32 [256], P('grp'), parts along dimension 0, may hold values from 0 to 3
- smooth_weight: float32 [8, 128], replicated, may hold values from 0.2 to 2
Outputs:
- solution_next: float32 [256, 8, 16, 128], P(('grp', 'orbit')), parts along dimension 0
- residual_next: float32 [256, 8, 16, 128], P(('grp', 'orbit')), parts along dimension 0
- step_length: float32 [32], P('grp'), parts along dimension 0
The draws below stay inside these ranges and needn't reach their ends.
There are 2 independent parts, one for each index of `grp`. The reference program is written for one: setup_inputs(seed, part) draws one part's arguments, and reference() takes and returns one part's arrays. A program takes and returns all parts, laid end to end along the dimension named above; an argument that names none is the same for every part. Nothing has to cross between parts.
Inputs may be any that keep to these rules, and one draw needn't show every extreme that they name: `tile_count`: slots at or above this count hold padding that carries no weight; in every draw some device has 8 live tiles. `crossing`: the window of a device starts 4 columns before its own block and covers 2 * 8 columns.
All inputs are finite; a program needn't handle non-finite values.
Results may differ from the reference program's by a relative error of at most 0.00075.
Values may be sent and summed in bfloat16 or wider, within the bound.
No kernel may reach another device: no remote copies, remote signals or barrier semaphores. Data moves between devices by JAX's collectives and lax.ppermute only.
A program may use at most 64 MiB of HBM per device.

```python
import math
import jax
import jax.numpy as jnp
from jax import lax

GAS_SPECIES = 8
LEVELS = 120
TILE_SIZE = 128
NRHS = 16
CROSSED_TILES = 24
CLASSES = 4
COLUMNS_PER_UNIT = 8
MT_CAP = 8
COLS = 128
MEASURE_TILES = 128
REACH = 8
RIM = 4
N_ORBIT = 16


def expanding(sampled, power):
    column_pos = jnp.arange(COLS).astype(jnp.float32)
    growth = (1.0 + 2.0 * column_pos / COLS) ** power
    return sampled * growth[:, None, None, None]


def draw_residual(key, part):
    key = jax.random.fold_in(key, 21)
    sampled = jnp.clip(jax.random.normal(key, (COLS, GAS_SPECIES, NRHS, TILE_SIZE), jnp.float32), -5.0, 5.0)
    return expanding(sampled, 0.5)


def draw_direction(key, part):
    key = jax.random.fold_in(key, 33)
    sampled = jnp.clip(jax.random.normal(key, (COLS, GAS_SPECIES, NRHS, TILE_SIZE), jnp.float32), -5.0, 5.0)
    return expanding(sampled, 0.5)


def draw_tile_count(key, part):
    key = jax.random.fold_in(key, 47)
    first_key, second_key, third_key = jax.random.split(key, 3)
    first_draw = jax.random.randint(first_key, (N_ORBIT,), 1, MT_CAP + 1)
    second_draw = jax.random.randint(second_key, (N_ORBIT,), 1, MT_CAP + 1)
    busiest = jax.random.randint(third_key, (), 0, N_ORBIT)
    counts = jnp.minimum(first_draw, second_draw)
    return jnp.where(jnp.arange(N_ORBIT) == busiest, MT_CAP, counts).astype(jnp.int32)


def set_ends(entries, own_key, low, largest):
    longest = entries.shape.index(max(entries.shape))
    spots = []
    for shift in (0, 1):
        where = [jax.random.randint(jax.random.fold_in(own_key, axis), (), 0, length) for axis, length in enumerate(entries.shape)]
        where[longest] = (where[longest] + shift) % entries.shape[longest]
        spots.append(tuple(where))
    return entries.at[spots[0]].set(low).at[spots[1]].set(largest)


def block_scale(key, extent, cuts, low, high):
    level, own = 1.0, jax.random.fold_in(key, 6)
    for position, blocks in cuts:
        draws = jnp.exp(jax.random.uniform(jax.random.fold_in(own, position), (blocks,), jnp.float32, low / len(cuts), high / len(cuts)))
        level = level * jnp.repeat(draws, extent[position] // blocks).reshape([-1 if axis == position else 1 for axis in range(len(extent))])
    return level


def centred(own_key, dims, width, bound, cuts=(), kind=jnp.bfloat16):
    drawn = jax.random.normal(own_key, dims, jnp.float32) * width
    if len(cuts) > 0:
        drawn = block_scale(own_key, dims, cuts, -0.22, 0.18) * drawn
    return jnp.clip(drawn, min=-bound, max=bound).astype(kind)


def setup_inputs(seed: int = 0, part: int = 0) -> dict:
    keys = jax.random.split(jax.random.key(seed), 10)
    part_splits = jax.random.split(jax.random.fold_in(keys[9], part), 10)
    return {
        "solution": centred(part_splits[0], (COLS, GAS_SPECIES, NRHS, TILE_SIZE), 1.0, 6.0, ((0, 16),), jnp.float32),
        "residual": draw_residual(jax.random.fold_in(jax.random.fold_in(keys[9], part), 71), part),
        "direction": draw_direction(jax.random.fold_in(jax.random.fold_in(keys[9], part), 71), part),
        "jacobian": centred(part_splits[3], (MEASURE_TILES, CROSSED_TILES, TILE_SIZE, TILE_SIZE), (CROSSED_TILES * TILE_SIZE) ** -0.5, 0.109375, ((0, 16),)),
        "crossing": set_ends(jax.random.randint(part_splits[4], (MEASURE_TILES, CROSSED_TILES), 0, 2 * COLUMNS_PER_UNIT * GAS_SPECIES), jax.random.fold_in(part_splits[4], 1), 0, (2 * COLUMNS_PER_UNIT * GAS_SPECIES) - 1).astype(jnp.int32),
        "tile_count": draw_tile_count(jax.random.fold_in(jax.random.fold_in(keys[9], part), 71), part),
        "sightline_weight": jnp.clip(jnp.exp(math.log(8.0) - 2.0794415 * jax.random.uniform(part_splits[6], (MEASURE_TILES, TILE_SIZE), jnp.float32) ** block_scale(part_splits[6], (MEASURE_TILES, TILE_SIZE), ((0, 16),), -0.2, 0.2)), 1.0, 8.0),
        "length_class": set_ends(jax.random.randint(part_splits[7], (COLS,), 0, CLASSES), jax.random.fold_in(part_splits[7], 1), 0, CLASSES - 1).astype(jnp.int32),
        "smooth_weight": jnp.clip(jnp.exp(jax.random.uniform(keys[8], (GAS_SPECIES, TILE_SIZE), jnp.float32, math.log(0.2), math.log(2.0))), 0.2, 2.0),
    }


epsilon = 1e-6


def regularize(values, length_class, reach):
    lengths = (length_class + 1) * reach // CLASSES
    broadcast = (-1,) + (1,) * (values.ndim - 1)

    def add_offset(distance, ongoing_total):
        reciprocal = 1.0 / (distance * distance).astype(jnp.float32)
        weight = jnp.where(distance <= lengths, reciprocal, 0.0).astype(jnp.float32).reshape(broadcast)
        edge_flux = weight * (values - jnp.roll(values, -distance, axis=0))
        return ongoing_total + edge_flux - jnp.roll(edge_flux, distance, axis=0)

    return lax.fori_loop(1, reach + 1, add_offset, jnp.zeros_like(values))


def reference(solution, residual, direction, jacobian, crossing, tile_count, sightline_weight, length_class, smooth_weight):
    level_mask = (jnp.arange(TILE_SIZE) < LEVELS).astype(jnp.float32)
    masked_dir = direction * level_mask
    masked_res = residual * level_mask
    rounded_dir = masked_dir.astype(jnp.bfloat16)
    window_cols = 2 * COLUMNS_PER_UNIT
    devices = jnp.arange(N_ORBIT).astype(jnp.int32)
    blocks = (devices, jacobian.reshape(N_ORBIT, MT_CAP, CROSSED_TILES, TILE_SIZE, TILE_SIZE), crossing.reshape(N_ORBIT, MT_CAP, CROSSED_TILES), tile_count, sightline_weight.reshape(N_ORBIT, MT_CAP, TILE_SIZE))

    def one_device(projected, block):
        device, block_jacobian, block_cross, live_count, block_noise = block
        columns = ((device * COLUMNS_PER_UNIT - RIM + jnp.arange(window_cols).astype(jnp.int32)) % COLS).astype(jnp.int32)
        window = rounded_dir[columns].reshape(window_cols * GAS_SPECIES, NRHS, TILE_SIZE)
        gathered = window[block_cross].astype(jnp.float32)
        wide_jacobian = block_jacobian.astype(jnp.float32)
        integrals = jnp.einsum("tjrl,tjnl->tnr", wide_jacobian, gathered, precision=lax.Precision.HIGHEST)
        alive = (jnp.arange(MT_CAP) < live_count).astype(jnp.float32)
        row_weight = alive[:, None] * block_noise
        weighted = (row_weight[:, None, :] * integrals).astype(jnp.bfloat16)
        contribution = jnp.einsum("tjrl,tnr->tjnl", wide_jacobian, weighted.astype(jnp.float32), precision=lax.Precision.HIGHEST)
        tile_sums = jnp.zeros((window_cols * GAS_SPECIES, NRHS, TILE_SIZE), jnp.float32).at[block_cross.reshape(-1)].add(contribution.reshape(MT_CAP * CROSSED_TILES, NRHS, TILE_SIZE))
        projected = projected.at[columns].add(tile_sums.reshape(window_cols, GAS_SPECIES, NRHS, TILE_SIZE))
        return projected, None

    projected, unused = lax.scan(one_device, jnp.zeros((COLS, GAS_SPECIES, NRHS, TILE_SIZE), jnp.float32), blocks)
    smoothing = regularize(masked_dir, length_class, REACH)
    image = level_mask * (projected + smooth_weight[None, :, None, :] * (masked_dir + smoothing))
    residual_norm = jnp.sum(masked_res * masked_res, axis=(0, 1, 3))
    curvature = jnp.sum(masked_dir * image, axis=(0, 1, 3))
    step_length = residual_norm / (curvature + epsilon)
    expand = step_length[None, None, :, None]
    solution_next = level_mask * (solution + expand * masked_dir)
    residual_next = masked_res - expand * image
    return (solution_next, residual_next, step_length)
```

```python
import functools

import jax
import jax.numpy as jnp
from jax import lax
from jax.experimental import pallas as pl
from jax.experimental.pallas import tpu as pltpu
from jax.sharding import PartitionSpec as P

LEVELS = 120
CLASSES = 4
REACH = 8
EPSILON = 1e-06
VMEM_LIMIT = 40 * 1024 * 1024

SMEM = functools.partial(pl.BlockSpec, memory_space=pltpu.SMEM)
VMEM = functools.partial(pl.BlockSpec, memory_space=pltpu.VMEM)
ANY = functools.partial(pl.BlockSpec, memory_space=pl.ANY)


def live_lanes(shape):
    return lax.broadcasted_iota(jnp.int32, shape, len(shape) - 1) < LEVELS


def masked(values):
    return jnp.where(live_lanes(values.shape), values, 0.0)


def call(kernel, out_shape, in_specs, flops, moved, scratch=()):
    return pl.pallas_call(
        kernel,
        out_shape=out_shape,
        in_specs=in_specs,
        out_specs=jax.tree.map(lambda _: VMEM(), out_shape),
        scratch_shapes=list(scratch),
        compiler_params=pltpu.CompilerParams(vmem_limit_bytes=VMEM_LIMIT),
        cost_estimate=pl.CostEstimate(flops=flops, bytes_accessed=moved, transcendentals=0),
    )


def rounding_kernel(rim, direction, near_low, near_high, far_up, far_down):
    cols = direction.shape[0]
    for c in range(cols):
        value = masked(direction[c])
        high = value.astype(jnp.bfloat16)
        if c < rim:
            near_low[c] = high
            far_up[c] = high
        else:
            near_high[c - rim] = high
            far_down[c - rim] = high
        if c == 0:
            far_down[rim] = (value - high.astype(jnp.float32)).astype(jnp.bfloat16)
        if c == cols - 1:
            far_up[rim] = (value - high.astype(jnp.float32)).astype(jnp.bfloat16)


def coupling(classes, cols):
    total = classes.shape[0]
    first = lax.axis_index("orbit") * cols
    table = {}
    for c in range(-REACH, cols):
        length = (classes[lax.rem(first + c + total, total)] + 1) * REACH // CLASSES
        for k in range(1, REACH + 1):
            table[c, k] = jnp.where(k <= length, jnp.float32(1.0 / (k * k)), jnp.float32(0.0))
    return table


def between(table, c, other):
    return table[c, other - c] if other > c else table[other, c - other]


def inner_kernel(direction, residual, classes, inner, norm):
    cols = direction.shape[0]
    table = coupling(classes, cols)
    squares = jnp.zeros(norm.shape, jnp.float32)
    for c in range(cols):
        centre = jnp.float32(0.0)
        for k in range(1, REACH + 1):
            centre = centre + (table[c, k] + table[c - k, k])
        result = centre * masked(direction[c])
        for other in range(cols):
            if other != c and abs(other - c) <= REACH:
                result = result - between(table, c, other) * masked(direction[other])
        inner[c] = result
        mres = masked(residual[c])
        squares = squares + jnp.sum(mres * mres, axis=0)
    norm[...] = squares


def outer_kernel(
    rim, direction, inner, left_near, right_near, left_far, right_far, classes, smooth, norm, curved,
    base, sums, sides,
):
    cols = direction.shape[0]
    table = coupling(classes, cols)
    for c in range(rim):
        sides[c] = left_far[c].astype(jnp.float32)
        sides[rim + c] = left_near[c].astype(jnp.float32)
        sides[cols + c] = right_near[c].astype(jnp.float32)
        sides[cols + rim + c] = right_far[c].astype(jnp.float32)
    sides[cols - 1] += left_far[rim].astype(jnp.float32)
    sides[cols] += right_far[rim].astype(jnp.float32)
    total = curved[...]
    weight = smooth[...][:, None, :]
    for c in range(cols):
        result = inner[c]
        for other in list(range(-cols, 0)) + list(range(cols, 2 * cols)):
            if abs(other - c) <= REACH:
                place = other + cols if other < 0 else other
                result = result - between(table, c, other) * sides[place]
        value = masked(direction[c])
        result = weight * (value + result)
        base[c] = result
        total = total + jnp.sum(value * result, axis=0)
    lane = lax.broadcasted_iota(jnp.int32, sums.shape, 1)
    sums[...] = jnp.where(
        lane == 0,
        jnp.sum(norm[...], axis=1, keepdims=True),
        jnp.where(lane == 1, jnp.sum(total, axis=1, keepdims=True), 0.0),
    )


def forward_kernel(
    crossing, count, sight, left, low, high, right, jac_hbm, weighted, curved, window, jac, sems
):
    slots, crossings = crossing.shape
    copies = [pltpu.make_async_copy(jac_hbm.at[i], jac.at[i], sems.at[i]) for i in range(slots)]
    for copy in copies:
        copy.start()
    rim_tiles = left.shape[0]
    for place, part in enumerate((left, low, high, right)):
        window[pl.ds(place * rim_tiles, rim_tiles)] = part[...]
    total = jnp.zeros(curved.shape, jnp.float32)
    for i in range(slots):
        copies[i].wait()
        picked = jnp.concatenate([window[crossing[i, j]] for j in range(crossings)], axis=1)
        tiles = jnp.concatenate([jac[i, j] for j in range(crossings)], axis=1)
        integrals = lax.dot_general(
            picked, tiles, (((1,), (1,)), ((), ())), preferred_element_type=jnp.float32
        )
        row = sight[pl.ds(i, 1), :] * jnp.where(i < count[0], 1.0, 0.0)
        product = (row * integrals).astype(jnp.bfloat16)
        weighted[i] = product
        total = total + product.astype(jnp.float32) * integrals
    curved[...] = total


def backward_kernel(crossing, weighted, jac_hbm, own, left, right, sums, jac, sems):
    slots, crossings = crossing.shape
    copies = [pltpu.make_async_copy(jac_hbm.at[i], jac.at[i], sems.at[i]) for i in range(slots)]
    for copy in copies:
        copy.start()
    sums[...] = jnp.zeros(sums.shape, jnp.float32)
    tile = jac.shape[-1]
    for i in range(slots):
        copies[i].wait()
        tiles = jnp.concatenate([jac[i, j] for j in range(crossings)], axis=1)
        terms = jnp.dot(weighted[i], tiles, preferred_element_type=jnp.float32)
        for j in range(crossings):
            sums[crossing[i, j]] += terms[:, j * tile : (j + 1) * tile]
    rim_tiles, own_tiles = left.shape[0], own.shape[0]
    left[...] = sums[pl.ds(0, rim_tiles)].astype(left.dtype)
    right[...] = sums[pl.ds(rim_tiles + own_tiles, rim_tiles)].astype(right.dtype)
    own[...] = sums[pl.ds(rim_tiles, own_tiles)]


def final_kernel(
    rim, solution, residual, direction, base, own, from_left, from_right, sums,
    solution_next, residual_next, step_length,
):
    norm = sums[:, 0:1]
    curvature = sums[:, 1:2]
    step = norm / (curvature + EPSILON)
    step_length[...] = step
    cols = direction.shape[0]
    wide = jnp.broadcast_to(step, direction.shape[2:])[None]
    for c in range(cols):
        arrived = from_left[c] if c < rim else from_right[c - rim]
        image = masked(base[c] + (own[c] + arrived.astype(jnp.float32)))
        solution_next[c] = masked(solution[c] + wide * direction[c])
        residual_next[c] = masked(residual[c]) - wide * image


def shifted(array, by):
    count = lax.axis_size("orbit")
    return lax.ppermute(array, "orbit", [(i, (i + by) % count) for i in range(count)])


def summed(array):
    count = lax.axis_size("orbit")
    if count & (count - 1):
        return lax.psum(array, "orbit")
    bit = 1
    while bit < count:
        array = array + lax.ppermute(array, "orbit", [(i, i ^ bit) for i in range(count)])
        bit *= 2
    return array


def local(
    solution, residual, direction, jacobian, crossing, tile_count, sightline_weight,
    length_class, smooth_weight,
):
    cols, species, probes, width = direction.shape
    rim = cols // 2
    slots, crossings = crossing.shape
    f32, bf16 = jnp.float32, jnp.bfloat16
    shape = jax.ShapeDtypeStruct
    column = (species, probes, width)
    elements = direction.size
    scratch_jac = [pltpu.VMEM(jacobian.shape, bf16), pltpu.SemaphoreType.DMA((slots,))]
    dot_flops = 2 * jacobian.size * probes

    near = shape((rim,) + column, bf16)
    far = shape((rim + 1,) + column, bf16)
    near_low, near_high, far_up, far_down = call(
        functools.partial(rounding_kernel, rim),
        (near, near, far, far),
        [VMEM()],
        2 * elements,
        9 * elements,
    )(direction)
    left_near = shifted(near_high, 1)
    right_near = shifted(near_low, -1)
    left_far = shifted(far_up, 1)
    right_far = shifted(far_down, -1)

    inner, norm = call(
        inner_kernel,
        (shape(direction.shape, f32), shape((probes, width), f32)),
        [VMEM(), VMEM(), SMEM()],
        20 * elements,
        12 * elements,
    )(direction, residual, length_class)

    flat = (rim * species, probes, width)
    weighted, curved = call(
        forward_kernel,
        (shape((slots, probes, width), bf16), shape((probes, width), f32)),
        [SMEM(), SMEM()] + [VMEM()] * 5 + [ANY()],
        dot_flops,
        2 * jacobian.size,
        [pltpu.VMEM((4 * rim * species, probes, width), bf16)] + scratch_jac,
    )(
        crossing, tile_count, sightline_weight, left_near.reshape(flat), near_low.reshape(flat),
        near_high.reshape(flat), right_near.reshape(flat), jacobian,
    )

    base, sums = call(
        functools.partial(outer_kernel, rim),
        (shape(direction.shape, f32), shape((probes, width), f32)),
        [VMEM()] * 6 + [SMEM()] + [VMEM()] * 3,
        20 * elements,
        16 * elements,
        [pltpu.VMEM((2 * cols,) + column, f32)],
    )(
        direction, inner, left_near, right_near, left_far, right_far, length_class, smooth_weight,
        norm, curved,
    )
    sums = summed(sums)

    own, to_left, to_right = call(
        backward_kernel,
        (
            shape((cols * species, probes, width), f32),
            shape(flat, bf16),
            shape(flat, bf16),
        ),
        [SMEM(), VMEM(), ANY()],
        dot_flops,
        2 * jacobian.size,
        [pltpu.VMEM((4 * rim * species, probes, width), f32)] + scratch_jac,
    )(crossing, weighted, jacobian)
    from_left = shifted(to_right, 1)
    from_right = shifted(to_left, -1)

    solution_next, residual_next, step_length = call(
        functools.partial(final_kernel, rim),
        (
            shape(direction.shape, f32),
            shape(direction.shape, f32),
            shape((probes, 1), f32),
        ),
        [VMEM()] * 8,
        8 * elements,
        28 * elements,
    )(
        solution, residual, direction, base, own.reshape(direction.shape),
        from_left.reshape(near.shape), from_right.reshape(near.shape), sums,
    )
    return solution_next, residual_next, step_length.reshape(probes)


def solution(mesh):
    wide = P(("grp", "orbit"), None, None, None)
    placed = (
        wide, wide, wide, wide,
        P(("grp", "orbit"), None),
        P(("grp", "orbit")),
        P(("grp", "orbit"), None),
        P("grp"),
        P(),
    )
    return jax.shard_map(
        local, mesh=mesh, in_specs=placed, out_specs=(wide, wide, P("grp")), check_vma=False
    )
```

```python
import functools

import jax
import jax.numpy as jnp
from jax import lax
from jax.experimental import pallas as pl
from jax.experimental.pallas import tpu as pltpu
from jax.sharding import PartitionSpec as P

LEVELS = 120
CLASSES = 4
REACH = 8
EPSILON = 1e-06
VMEM_LIMIT = 24 * 1024 * 1024

SMEM = functools.partial(pl.BlockSpec, memory_space=pltpu.SMEM)
VMEM = functools.partial(pl.BlockSpec, memory_space=pltpu.VMEM)
HBM = functools.partial(pl.BlockSpec, memory_space=pltpu.HBM)


def in_hbm(array):
    return pltpu.with_memory_space_constraint(array, pltpu.HBM)


def live_lanes(shape):
    return lax.broadcasted_iota(jnp.int32, shape, len(shape) - 1) < LEVELS


def masked(values):
    return jnp.where(live_lanes(values.shape), values, 0.0)


def call(kernel, out_shape, in_specs, flops, moved, scratch=()):
    return pl.pallas_call(
        kernel,
        out_shape=out_shape,
        in_specs=in_specs,
        out_specs=jax.tree.map(lambda _: VMEM(), out_shape),
        scratch_shapes=list(scratch),
        compiler_params=pltpu.CompilerParams(vmem_limit_bytes=VMEM_LIMIT),
        cost_estimate=pl.CostEstimate(flops=flops, bytes_accessed=moved, transcendentals=0),
    )


def rounding_kernel(direction, low, high):
    rim = low.shape[0]
    for c in range(rim):
        low[c] = masked(direction[c]).astype(jnp.bfloat16)
        high[c] = masked(direction[rim + c]).astype(jnp.bfloat16)


def coupling(classes, cols, columns):
    total = classes.shape[0]
    first = lax.axis_index("orbit") * cols
    table = {}
    for c in columns:
        length = (classes[lax.rem(first + c + total, total)] + 1) * REACH // CLASSES
        for k in range(1, REACH + 1):
            table[c, k] = jnp.where(k <= length, jnp.float32(1.0 / (k * k)), jnp.float32(0.0))
    return table


def pull(table, to, values):
    result = None
    for c, value in values.items():
        if c != to and abs(c - to) <= REACH:
            term = table[min(c, to), abs(c - to)] * value
            result = term if result is None else result + term
    return -result


def inner_kernel(
    direction, residual_hbm, classes_hbm, smooth_hbm, jac_hbm, begun, norm, curved, jac,
    residual, classes, smooth, sems,
):
    pairs = (classes_hbm, classes), (smooth_hbm, smooth), (residual_hbm, residual), (jac_hbm, jac)
    copies = [pltpu.make_async_copy(*pair, sems.at[i]) for i, pair in enumerate(pairs)]
    for copy in copies:
        copy.start()
    copies[0].wait()
    copies[1].wait()
    cols = direction.shape[0]
    rim = cols // 2
    table = coupling(classes, cols, range(-REACH, cols))
    weight = smooth[...][:, None, :]
    total = jnp.zeros(norm.shape, jnp.float32)
    values = {c: masked(direction[c]) for c in range(cols)}
    rests = {c: v - v.astype(jnp.bfloat16).astype(jnp.float32) for c, v in values.items()}
    for c in range(cols):
        centre = jnp.float32(1.0)
        for k in range(1, REACH + 1):
            centre = centre + (table[c, k] + table[c - k, k])
        result = weight * (centre * values[c] + pull(table, c, values))
        begun[rim + c] = result
        total = total + jnp.sum(values[c] * result, axis=0)
    for q in range(rim):
        to_left = {c: values[c] if c >= rim else rests[c] for c in range(cols)}
        to_right = {c: values[c] if c < rim else rests[c] for c in range(cols)}
        begun[q] = weight * pull(table, q - rim, to_left)
        begun[rim + cols + q] = weight * pull(table, q + cols, to_right)
    curved[...] = total
    copies[2].wait()
    squares = jnp.zeros(norm.shape, jnp.float32)
    for c in range(cols):
        mres = masked(residual[c])
        squares = squares + jnp.sum(mres * mres, axis=0)
    norm[...] = squares
    copies[3].wait()


def forward_kernel(
    crossing, count, classes, sight, direction, smooth, left, low, high, right, begun, norm, curved,
    jac, weighted, own, sums, window,
):
    slots, crossings = crossing.shape
    cols, species = direction.shape[:2]
    rim = left.shape[0]
    rim_tiles = rim * species
    for place, part in enumerate((left, low, high, right)):
        window[pl.ds(place * rim_tiles, rim_tiles)] = part[...].reshape(rim_tiles, *part.shape[2:])
    total = curved[...]
    for i in range(slots):
        picked = jnp.concatenate([window[crossing[i, j]] for j in range(crossings)], axis=1)
        tiles = jnp.concatenate([jac[i, j] for j in range(crossings)], axis=1)
        integrals = lax.dot_general(
            tiles, picked, (((1,), (1,)), ((), ())), preferred_element_type=jnp.float32
        )
        integrals = jnp.transpose(integrals)
        row = sight[pl.ds(i, 1), :] * jnp.where(i < count[0], 1.0, 0.0)
        product = (row * integrals).astype(jnp.bfloat16)
        weighted[i] = product
        total = total + product.astype(jnp.float32) * integrals
    table = coupling(classes, cols, range(-rim, cols))
    weight = smooth[...][:, None, :]
    before = {c - rim: left[c].astype(jnp.float32) for c in range(rim)}
    after = {c + cols: right[c].astype(jnp.float32) for c in range(rim)}
    for c in range(cols):
        from_before = weight * pull(table, c, before)
        from_after = weight * pull(table, c, after)
        own[c] = begun[rim + c] + (from_before + from_after)
        edges = from_after if c < rim else from_after + from_before
        total = total + 2.0 * jnp.sum(masked(direction[c]) * edges, axis=0)
    lane = lax.broadcasted_iota(jnp.int32, sums.shape, 1)
    sums[...] = jnp.where(
        lane == 0,
        jnp.sum(norm[...], axis=1, keepdims=True),
        jnp.where(lane == 1, jnp.sum(total, axis=1, keepdims=True), 0.0),
    )


def backward_kernel(crossing, weighted, jac, begun, own, image, left, right, sums):
    slots, crossings = crossing.shape
    cols, species, probes, tile = own.shape
    rim = left.shape[0]
    rim_tiles, own_tiles = rim * species, cols * species
    spans = (pl.ds(0, rim_tiles), pl.ds(rim_tiles, own_tiles), pl.ds(rim_tiles + own_tiles, rim_tiles))
    sums[spans[0]] = begun[pl.ds(0, rim)].reshape(rim_tiles, probes, tile)
    sums[spans[1]] = own[...].reshape(own_tiles, probes, tile)
    sums[spans[2]] = begun[pl.ds(rim + cols, rim)].reshape(rim_tiles, probes, tile)
    for i in range(slots):
        tiles = jnp.concatenate([jac[i, j] for j in range(crossings)], axis=1)
        terms = jnp.dot(weighted[i], tiles, preferred_element_type=jnp.float32)
        for j in range(crossings):
            sums[crossing[i, j]] += terms[:, j * tile : (j + 1) * tile]
    left[...] = sums[spans[0]].astype(left.dtype).reshape(left.shape)
    right[...] = sums[spans[2]].astype(right.dtype).reshape(right.shape)
    image[...] = sums[spans[1]].reshape(image.shape)


def final_kernel(
    solution, residual, direction, image, from_left, from_right, sums,
    solution_next, residual_next, step_length,
):
    step = sums[:, 0:1] / (sums[:, 1:2] + EPSILON)
    cols = direction.shape[0]
    rim = from_left.shape[0]
    wide = jnp.broadcast_to(step, direction.shape[2:])
    step_length[...] = jnp.transpose(wide)[0:1]
    wide = wide[None]
    for c in range(cols):
        arrived = from_left[c] if c < rim else from_right[c - rim]
        whole = masked(image[c] + arrived.astype(jnp.float32))
        solution_next[c] = masked(solution[c] + wide * direction[c])
        residual_next[c] = masked(residual[c]) - wide * whole


def shifted(array, by):
    count = lax.axis_size("orbit")
    return lax.ppermute(array, "orbit", [(i, (i + by) % count) for i in range(count)])


def summed(array):
    count = lax.axis_size("orbit")
    if count & (count - 1):
        return lax.psum(array, "orbit")
    bits = [1 << b for b in range(count.bit_length() - 1)]
    for bit in bits[1:] + bits[:1]:
        array = array + lax.ppermute(array, "orbit", [(i, i ^ bit) for i in range(count)])
    return array


def local(
    solution, residual, direction, jacobian, crossing, tile_count, sightline_weight,
    length_class, smooth_weight,
):
    cols, species, probes, width = direction.shape
    assert REACH <= cols
    rim = cols // 2
    slots = crossing.shape[0]
    f32, bf16 = jnp.float32, jnp.bfloat16
    shape = jax.ShapeDtypeStruct
    column = (species, probes, width)
    elements = direction.size
    dot_flops = 2 * jacobian.size * probes
    near = shape((rim,) + column, bf16)
    whole = shape(direction.shape, f32)
    small = shape((probes, width), f32)

    low, high = call(rounding_kernel, (near, near), [VMEM()], 2 * elements, 6 * elements)(direction)
    left = shifted(high, 1)
    right = shifted(low, -1)

    begun, norm, curved, jac = call(
        inner_kernel,
        (shape((2 * cols,) + column, f32), small, small, shape(jacobian.shape, bf16)),
        [VMEM()] + [HBM()] * 4,
        60 * elements,
        4 * jacobian.size,
        [
            pltpu.VMEM(direction.shape, f32),
            pltpu.SMEM(length_class.shape, jnp.int32),
            pltpu.VMEM(smooth_weight.shape, f32),
            pltpu.SemaphoreType.DMA((4,)),
        ],
    )(direction, *map(in_hbm, (residual, length_class, smooth_weight, jacobian)))

    weighted, own, sums = call(
        forward_kernel,
        (shape((slots, probes, width), bf16), whole, small),
        [SMEM()] * 3 + [VMEM()] * 11,
        dot_flops,
        2 * jacobian.size,
        [pltpu.VMEM((2 * cols * species, probes, width), bf16)],
    )(
        crossing, tile_count, length_class, sightline_weight, direction, smooth_weight,
        left, low, high, right, begun, norm, curved, jac,
    )
    sums = summed(sums)

    image, to_left, to_right = call(
        backward_kernel,
        (whole, near, near),
        [SMEM()] + [VMEM()] * 4,
        dot_flops,
        2 * jacobian.size,
        [pltpu.VMEM((2 * cols * species, probes, width), f32)],
    )(crossing, weighted, jac, begun, own)
    from_left = shifted(to_right, 1)
    from_right = shifted(to_left, -1)

    solution_next, residual_next, step_length = call(
        final_kernel,
        (whole, whole, shape((1, probes), f32)),
        [VMEM()] * 7,
        8 * elements,
        28 * elements,
    )(solution, residual, direction, image, from_left, from_right, sums)
    return solution_next, residual_next, step_length.reshape(probes)


def solution(mesh):
    wide = P(("grp", "orbit"), None, None, None)
    placed = (
        wide, wide, wide, wide,
        P(("grp", "orbit"), None),
        P(("grp", "orbit")),
        P(("grp", "orbit"), None),
        P("grp"),
        P(),
    )
    return jax.shard_map(
        local, mesh=mesh, in_specs=placed, out_specs=(wide, wide, P("grp")), check_vma=False
    )
```

```python
import functools

import jax
import jax.numpy as jnp
from jax import lax
from jax.experimental import pallas as pl
from jax.experimental.pallas import tpu as pltpu
from jax.sharding import PartitionSpec as P

LEVELS = 120
CLASSES = 4
REACH = 8
EPSILON = 1e-06
VMEM_LIMIT = 24 * 1024 * 1024

SMEM = functools.partial(pl.BlockSpec, memory_space=pltpu.SMEM)
VMEM = functools.partial(pl.BlockSpec, memory_space=pltpu.VMEM)
HBM = functools.partial(pl.BlockSpec, memory_space=pltpu.HBM)


def in_hbm(array):
    return pltpu.with_memory_space_constraint(array, pltpu.HBM)


def live_lanes(shape):
    return lax.broadcasted_iota(jnp.int32, shape, len(shape) - 1) < LEVELS


def masked(values):
    return jnp.where(live_lanes(values.shape), values, 0.0)


def call(kernel, out_shape, in_specs, flops, moved, scratch=()):
    return pl.pallas_call(
        kernel,
        out_shape=out_shape,
        in_specs=in_specs,
        out_specs=jax.tree.map(lambda _: VMEM(), out_shape),
        scratch_shapes=list(scratch),
        compiler_params=pltpu.CompilerParams(vmem_limit_bytes=VMEM_LIMIT),
        cost_estimate=pl.CostEstimate(flops=flops, bytes_accessed=moved, transcendentals=0),
    )


def parity():
    return lax.rem(lax.axis_index("orbit"), 2)


def rounding_kernel(direction, across, within):
    rim = across.shape[0]
    odd = parity()
    for c in range(rim):
        across[c] = masked(direction[odd * rim + c]).astype(jnp.bfloat16)
        within[c] = masked(direction[(1 - odd) * rim + c]).astype(jnp.bfloat16)


def coupling(classes, cols, columns):
    total = classes.shape[0]
    first = lax.axis_index("orbit") * cols
    table = {}
    for c in columns:
        length = (classes[lax.rem(first + c + total, total)] + 1) * REACH // CLASSES
        for k in range(1, REACH + 1):
            table[c, k] = jnp.where(k <= length, jnp.float32(1.0 / (k * k)), jnp.float32(0.0))
    return table


def pull(table, to, values):
    result = None
    for c, value in values.items():
        if c != to and abs(c - to) <= REACH:
            term = table[min(c, to), abs(c - to)] * value
            result = term if result is None else result + term
    return -result


def inner_kernel(
    direction, count, residual_hbm, classes_hbm, smooth_hbm, sight_hbm, jac_hbm,
    begun, norm, curved, rows, jac, residual, classes, smooth, sight, sems,
):
    pairs = (
        (classes_hbm, classes), (smooth_hbm, smooth), (sight_hbm, sight),
        (residual_hbm, residual), (jac_hbm, jac),
    )
    copies = [pltpu.make_async_copy(*pair, sems.at[i]) for i, pair in enumerate(pairs)]
    for copy in copies:
        copy.start()
    copies[0].wait()
    copies[1].wait()
    cols = direction.shape[0]
    rim = cols // 2
    table = coupling(classes, cols, range(-REACH, cols))
    weight = smooth[...][:, None, :]
    total = jnp.zeros(norm.shape, jnp.float32)
    values = {c: masked(direction[c]) for c in range(cols)}
    rests = {c: v - v.astype(jnp.bfloat16).astype(jnp.float32) for c, v in values.items()}
    for c in range(cols):
        centre = jnp.float32(1.0)
        for k in range(1, REACH + 1):
            centre = centre + (table[c, k] + table[c - k, k])
        result = weight * (centre * values[c] + pull(table, c, values))
        begun[rim + c] = result
        total = total + jnp.sum(values[c] * result, axis=0)
    for q in range(rim):
        to_left = {c: values[c] if c >= rim else rests[c] for c in range(cols)}
        to_right = {c: values[c] if c < rim else rests[c] for c in range(cols)}
        begun[q] = weight * pull(table, q - rim, to_left)
        begun[rim + cols + q] = weight * pull(table, q + cols, to_right)
    curved[...] = total
    copies[2].wait()
    slot = lax.broadcasted_iota(jnp.int32, rows.shape, 0)
    rows[...] = jnp.where(slot < count[0], sight[...], 0.0)
    copies[3].wait()
    squares = jnp.zeros(norm.shape, jnp.float32)
    for c in range(cols):
        mres = masked(residual[c])
        squares = squares + jnp.sum(mres * mres, axis=0)
    norm[...] = squares
    copies[4].wait()


def forward_kernel(
    crossing, classes, rows, direction, smooth, across, within, from_across, from_within,
    begun, norm, curved, jac, weighted, own, sums, window,
):
    slots, crossings = crossing.shape
    cols, species = direction.shape[:2]
    rim = across.shape[0]
    span = rim * species
    odd = parity()
    places = (1 + odd, across), (2 - odd, within), (3 * odd, from_across), (3 - 3 * odd, from_within)
    for place, part in places:
        window[pl.ds(place * span, span)] = part[...].reshape(span, *part.shape[2:])
    total = curved[...]
    for i in range(slots):
        picked = jnp.concatenate([window[crossing[i, j]] for j in range(crossings)], axis=1)
        tiles = jnp.concatenate([jac[i, j] for j in range(crossings)], axis=1)
        integrals = lax.dot_general(
            tiles, picked, (((1,), (1,)), ((), ())), preferred_element_type=jnp.float32
        )
        integrals = jnp.transpose(integrals)
        product = (rows[pl.ds(i, 1), :] * integrals).astype(jnp.bfloat16)
        weighted[i] = product
        total = total + product.astype(jnp.float32) * integrals
    table = coupling(classes, cols, range(-rim, cols))
    weight = smooth[...][:, None, :]
    before, after = {}, {}
    for c in range(rim):
        before[c - rim] = window[pl.ds(c * species, species)].astype(jnp.float32)
        after[c + cols] = window[pl.ds(3 * span + c * species, species)].astype(jnp.float32)
    for c in range(cols):
        from_before = weight * pull(table, c, before)
        from_after = weight * pull(table, c, after)
        own[c] = begun[rim + c] + (from_before + from_after)
        edges = from_after if c < rim else from_after + from_before
        total = total + 2.0 * jnp.sum(masked(direction[c]) * edges, axis=0)
    half = sums.shape[1]
    parts = [jnp.sum(x, axis=1, keepdims=True) for x in (norm[...], total)]
    parts = [part[h * half : (h + 1) * half] for h in range(2) for part in parts]
    lane = lax.broadcasted_iota(jnp.int32, sums.shape[1:], 1)
    block = jnp.zeros(sums.shape[1:], jnp.float32)
    for k, part in enumerate(parts):
        block = jnp.where(lane == k, part, block)
    sums[...] = jnp.broadcast_to(block[None], sums.shape)


def backward_kernel(crossing, weighted, jac, begun, own, image, across, within, sums):
    slots, crossings = crossing.shape
    cols, species, probes, tile = own.shape
    rim = across.shape[0]
    span = rim * species
    middle = pl.ds(span, 2 * span)
    sums[pl.ds(0, span)] = begun[pl.ds(0, rim)].reshape(span, probes, tile)
    sums[middle] = own[...].reshape(2 * span, probes, tile)
    sums[pl.ds(3 * span, span)] = begun[pl.ds(rim + cols, rim)].reshape(span, probes, tile)
    for i in range(slots):
        tiles = jnp.concatenate([jac[i, j] for j in range(crossings)], axis=1)
        terms = jnp.dot(weighted[i], tiles, preferred_element_type=jnp.float32)
        for j in range(crossings):
            sums[crossing[i, j]] += terms[:, j * tile : (j + 1) * tile]
    odd = parity()
    for part, place in (across, 3 * odd), (within, 3 - 3 * odd):
        part[...] = sums[pl.ds(place * span, span)].astype(part.dtype).reshape(part.shape)
    image[...] = sums[middle].reshape(image.shape)


def final_kernel(
    solution, residual, direction, image, from_across, from_within, sums,
    solution_next, residual_next, step_length,
):
    whole = jnp.sum(sums[...], axis=0)
    norm = jnp.concatenate([whole[:, 0:1], whole[:, 2:3]], axis=0)
    curvature = jnp.concatenate([whole[:, 1:2], whole[:, 3:4]], axis=0)
    step = norm / (curvature + EPSILON)
    rim = from_across.shape[0]
    wide = jnp.broadcast_to(step, direction.shape[2:])
    step_length[...] = jnp.transpose(wide)[0:1]
    wide = wide[None]
    odd = parity()
    for q in range(rim):
        for c, part in (odd * rim + q, from_across), ((1 - odd) * rim + q, from_within):
            total = masked(image[c] + part[q].astype(jnp.float32))
            solution_next[c] = masked(solution[c] + wide * direction[c])
            residual_next[c] = masked(residual[c]) - wide * total


def swapped(across, within):
    count = lax.axis_size("orbit")
    assert count % 2 == 0
    outer = [(i, (i + 2 * (i % 2) - 1) % count) for i in range(count)]
    inner = [(i, i ^ 1) for i in range(count)]
    return lax.ppermute(across, "orbit", outer), lax.ppermute(within, "orbit", inner)


def local(
    solution, residual, direction, jacobian, crossing, tile_count, sightline_weight,
    length_class, smooth_weight,
):
    cols, species, probes, width = direction.shape
    assert REACH <= cols
    rim = cols // 2
    slots = crossing.shape[0]
    f32, bf16 = jnp.float32, jnp.bfloat16
    shape = jax.ShapeDtypeStruct
    column = (species, probes, width)
    elements = direction.size
    dot_flops = 2 * jacobian.size * probes
    near = shape((rim,) + column, bf16)
    whole = shape(direction.shape, f32)
    small = shape((probes, width), f32)

    across, within = call(
        rounding_kernel, (near, near), [VMEM()], 2 * elements, 6 * elements
    )(direction)
    from_across, from_within = swapped(across, within)

    begun, norm, curved, rows, jac = call(
        inner_kernel,
        (
            shape((2 * cols,) + column, f32), small, small,
            shape(sightline_weight.shape, f32), shape(jacobian.shape, bf16),
        ),
        [VMEM(), SMEM()] + [HBM()] * 5,
        60 * elements,
        4 * jacobian.size,
        [
            pltpu.VMEM(direction.shape, f32),
            pltpu.SMEM(length_class.shape, jnp.int32),
            pltpu.VMEM(smooth_weight.shape, f32),
            pltpu.VMEM(sightline_weight.shape, f32),
            pltpu.SemaphoreType.DMA((5,)),
        ],
    )(
        direction, tile_count,
        *map(in_hbm, (residual, length_class, smooth_weight, sightline_weight, jacobian)),
    )

    devices = lax.axis_size("orbit")
    weighted, own, sums = call(
        forward_kernel,
        (
            shape((slots, probes, width), bf16), whole,
            shape((devices, probes // 2, width), f32),
        ),
        [SMEM()] * 2 + [VMEM()] * 11,
        dot_flops,
        2 * jacobian.size,
        [pltpu.VMEM((2 * cols * species, probes, width), bf16)],
    )(
        crossing, length_class, rows, direction, smooth_weight,
        across, within, from_across, from_within, begun, norm, curved, jac,
    )
    sums = lax.all_to_all(sums, "orbit", 0, 0)

    image, across, within = call(
        backward_kernel,
        (whole, near, near),
        [SMEM()] + [VMEM()] * 4,
        dot_flops,
        2 * jacobian.size,
        [pltpu.VMEM((2 * cols * species, probes, width), f32)],
    )(crossing, weighted, jac, begun, own)
    from_across, from_within = swapped(across, within)

    solution_next, residual_next, step_length = call(
        final_kernel,
        (whole, whole, shape((1, probes), f32)),
        [VMEM()] * 7,
        8 * elements,
        28 * elements,
    )(solution, residual, direction, image, from_across, from_within, sums)
    return solution_next, residual_next, step_length.reshape(probes)


def solution(mesh):
    wide = P(("grp", "orbit"), None, None, None)
    placed = (
        wide, wide, wide, wide,
        P(("grp", "orbit"), None),
        P(("grp", "orbit")),
        P(("grp", "orbit"), None),
        P("grp"),
        P(),
    )
    return jax.shard_map(
        local, mesh=mesh, in_specs=placed, out_specs=(wide, wide, P("grp")), check_vma=False
    )
```

```python
import functools

import jax
import jax.numpy as jnp
from jax import lax
from jax.experimental import pallas as pl
from jax.experimental.pallas import tpu as pltpu
from jax.sharding import PartitionSpec as P

LEVELS = 120
CLASSES = 4
REACH = 8
EPSILON = 1e-06
VMEM_LIMIT = 24 * 1024 * 1024

SMEM = functools.partial(pl.BlockSpec, memory_space=pltpu.SMEM)
VMEM = functools.partial(pl.BlockSpec, memory_space=pltpu.VMEM)
HBM = functools.partial(pl.BlockSpec, memory_space=pltpu.HBM)


def in_hbm(array):
    return pltpu.with_memory_space_constraint(array, pltpu.HBM)


def live_lanes(shape):
    return lax.broadcasted_iota(jnp.int32, shape, len(shape) - 1) < LEVELS


def masked(values):
    return jnp.where(live_lanes(values.shape), values, 0.0)


def call(kernel, out_shape, in_specs, flops, moved, scratch=()):
    return pl.pallas_call(
        kernel,
        out_shape=out_shape,
        in_specs=in_specs,
        out_specs=jax.tree.map(lambda _: VMEM(), out_shape),
        scratch_shapes=list(scratch),
        compiler_params=pltpu.CompilerParams(vmem_limit_bytes=VMEM_LIMIT),
        cost_estimate=pl.CostEstimate(flops=flops, bytes_accessed=moved, transcendentals=0),
    )


def parity():
    return lax.rem(lax.axis_index("orbit"), 2)


def rounding_kernel(direction, across, within):
    rim = across.shape[0]
    odd = parity()
    for c in range(rim):
        across[c] = masked(direction[odd * rim + c]).astype(jnp.bfloat16)
        within[c] = masked(direction[(1 - odd) * rim + c]).astype(jnp.bfloat16)


def coupling(classes, cols, columns):
    total = classes.shape[0]
    first = lax.axis_index("orbit") * cols
    table = {}
    for c in columns:
        length = (classes[lax.rem(first + c + total, total)] + 1) * REACH // CLASSES
        for k in range(1, REACH + 1):
            table[c, k] = jnp.where(k <= length, jnp.float32(1.0 / (k * k)), jnp.float32(0.0))
    return table


def pull(table, to, values):
    result = None
    for c, value in values.items():
        if c != to and abs(c - to) <= REACH:
            term = table[min(c, to), abs(c - to)] * value
            result = term if result is None else result + term
    return -result


def inner_kernel(
    direction, count, residual_hbm, classes_hbm, smooth_hbm, sight_hbm, jac_hbm,
    begun, norm, curved, rows, jac, residual, classes, smooth, sight, sems,
):
    pairs = (
        (classes_hbm, classes), (smooth_hbm, smooth), (sight_hbm, sight),
        (residual_hbm, residual), (jac_hbm, jac),
    )
    copies = [pltpu.make_async_copy(*pair, sems.at[i]) for i, pair in enumerate(pairs)]
    for copy in copies:
        copy.start()
    copies[0].wait()
    copies[1].wait()
    cols = direction.shape[0]
    rim = cols // 2
    table = coupling(classes, cols, range(-REACH, cols))
    weight = smooth[...][:, None, :]
    total = jnp.zeros(norm.shape, jnp.float32)
    values = {c: masked(direction[c]) for c in range(cols)}
    rests = {c: v - v.astype(jnp.bfloat16).astype(jnp.float32) for c, v in values.items()}
    for c in range(cols):
        centre = jnp.float32(1.0)
        for k in range(1, REACH + 1):
            centre = centre + (table[c, k] + table[c - k, k])
        result = weight * (centre * values[c] + pull(table, c, values))
        begun[rim + c] = result
        total = total + jnp.sum(values[c] * result, axis=0)
    for q in range(rim):
        to_left = {c: values[c] if c >= rim else rests[c] for c in range(cols)}
        to_right = {c: values[c] if c < rim else rests[c] for c in range(cols)}
        begun[q] = weight * pull(table, q - rim, to_left)
        begun[rim + cols + q] = weight * pull(table, q + cols, to_right)
    curved[...] = total
    copies[2].wait()
    slot = lax.broadcasted_iota(jnp.int32, rows.shape, 0)
    rows[...] = jnp.where(slot < count[0], sight[...], 0.0)
    copies[3].wait()
    squares = jnp.zeros(norm.shape, jnp.float32)
    for c in range(cols):
        mres = masked(residual[c])
        squares = squares + jnp.sum(mres * mres, axis=0)
    norm[...] = squares
    copies[4].wait()


def forward_kernel(
    crossing, classes, rows, direction, smooth, across, within, from_across, from_within,
    begun, norm, curved, jac, weighted, own, sums, window,
):
    slots, crossings = crossing.shape
    cols, species = direction.shape[:2]
    rim = across.shape[0]
    span = rim * species
    odd = parity()
    places = (1 + odd, across), (2 - odd, within), (3 * odd, from_across), (3 - 3 * odd, from_within)
    for place, part in places:
        window[pl.ds(place * span, span)] = part[...].reshape(span, *part.shape[2:])
    total = curved[...]
    for i in range(slots):
        picked = jnp.concatenate([window[crossing[i, j]] for j in range(crossings)], axis=1)
        tiles = jnp.concatenate([jac[i, j] for j in range(crossings)], axis=1)
        integrals = lax.dot_general(
            tiles, picked, (((1,), (1,)), ((), ())), preferred_element_type=jnp.float32
        )
        integrals = jnp.transpose(integrals)
        product = (rows[pl.ds(i, 1), :] * integrals).astype(jnp.bfloat16)
        weighted[i] = product
        total = total + product.astype(jnp.float32) * integrals
    table = coupling(classes, cols, range(-rim, cols))
    weight = smooth[...][:, None, :]
    before, after = {}, {}
    for c in range(rim):
        before[c - rim] = window[pl.ds(c * species, species)].astype(jnp.float32)
        after[c + cols] = window[pl.ds(3 * span + c * species, species)].astype(jnp.float32)
    for c in range(cols):
        from_before = weight * pull(table, c, before)
        from_after = weight * pull(table, c, after)
        own[c] = begun[rim + c] + (from_before + from_after)
        edges = from_after if c < rim else from_after + from_before
        total = total + 2.0 * jnp.sum(masked(direction[c]) * edges, axis=0)
    half = sums.shape[0]
    parts = [jnp.sum(x, axis=1, keepdims=True) for x in (norm[...], total)]
    parts = [part[h * half : (h + 1) * half] for h in range(2) for part in parts]
    lane = lax.broadcasted_iota(jnp.int32, sums.shape, 1)
    block = jnp.zeros(sums.shape, jnp.float32)
    for k, part in enumerate(parts):
        block = jnp.where(lane == k, part, block)
    sums[...] = block


def backward_kernel(crossing, weighted, jac, begun, own, image, across, within, sums):
    slots, crossings = crossing.shape
    cols, species, probes, tile = own.shape
    rim = across.shape[0]
    span = rim * species
    middle = pl.ds(span, 2 * span)
    sums[pl.ds(0, span)] = begun[pl.ds(0, rim)].reshape(span, probes, tile)
    sums[middle] = own[...].reshape(2 * span, probes, tile)
    sums[pl.ds(3 * span, span)] = begun[pl.ds(rim + cols, rim)].reshape(span, probes, tile)
    for i in range(slots):
        tiles = jnp.concatenate([jac[i, j] for j in range(crossings)], axis=1)
        terms = jnp.dot(weighted[i], tiles, preferred_element_type=jnp.float32)
        for j in range(crossings):
            sums[crossing[i, j]] += terms[:, j * tile : (j + 1) * tile]
    odd = parity()
    for part, place in (across, 3 * odd), (within, 3 - 3 * odd):
        part[...] = sums[pl.ds(place * span, span)].astype(part.dtype).reshape(part.shape)
    image[...] = sums[middle].reshape(image.shape)


def final_kernel(
    solution, residual, direction, image, from_across, from_within, sums,
    solution_next, residual_next, step_length,
):
    whole = jnp.sum(sums[...], axis=0)
    norm = jnp.concatenate([whole[:, 0:1], whole[:, 2:3]], axis=0)
    curvature = jnp.concatenate([whole[:, 1:2], whole[:, 3:4]], axis=0)
    step = norm / (curvature + EPSILON)
    rim = from_across.shape[0]
    wide = jnp.broadcast_to(step, direction.shape[2:])
    step_length[...] = jnp.transpose(wide)[0:1]
    wide = wide[None]
    odd = parity()
    for q in range(rim):
        for c, part in (odd * rim + q, from_across), ((1 - odd) * rim + q, from_within):
            total = masked(image[c] + part[q].astype(jnp.float32))
            solution_next[c] = masked(solution[c] + wide * direction[c])
            residual_next[c] = masked(residual[c]) - wide * total


def swapped(across, within):
    count = lax.axis_size("orbit")
    assert count % 2 == 0
    outer = [(i, (i + 2 * (i % 2) - 1) % count) for i in range(count)]
    inner = [(i, i ^ 1) for i in range(count)]
    return lax.ppermute(across, "orbit", outer), lax.ppermute(within, "orbit", inner)


def local(
    solution, residual, direction, jacobian, crossing, tile_count, sightline_weight,
    length_class, smooth_weight,
):
    cols, species, probes, width = direction.shape
    assert REACH <= cols
    rim = cols // 2
    slots = crossing.shape[0]
    f32, bf16 = jnp.float32, jnp.bfloat16
    shape = jax.ShapeDtypeStruct
    column = (species, probes, width)
    elements = direction.size
    dot_flops = 2 * jacobian.size * probes
    near = shape((rim,) + column, bf16)
    whole = shape(direction.shape, f32)
    small = shape((probes, width), f32)

    across, within = call(
        rounding_kernel, (near, near), [VMEM()], 2 * elements, 6 * elements
    )(direction)
    from_across, from_within = swapped(across, within)

    begun, norm, curved, rows, jac = call(
        inner_kernel,
        (
            shape((2 * cols,) + column, f32), small, small,
            shape(sightline_weight.shape, f32), shape(jacobian.shape, bf16),
        ),
        [VMEM(), SMEM()] + [HBM()] * 5,
        60 * elements,
        4 * jacobian.size,
        [
            pltpu.VMEM(direction.shape, f32),
            pltpu.SMEM(length_class.shape, jnp.int32),
            pltpu.VMEM(smooth_weight.shape, f32),
            pltpu.VMEM(sightline_weight.shape, f32),
            pltpu.SemaphoreType.DMA((5,)),
        ],
    )(
        direction, tile_count,
        *map(in_hbm, (residual, length_class, smooth_weight, sightline_weight, jacobian)),
    )

    weighted, own, sums = call(
        forward_kernel,
        (
            shape((slots, probes, width), bf16), whole,
            shape((probes // 2, width), f32),
        ),
        [SMEM()] * 2 + [VMEM()] * 11,
        dot_flops,
        2 * jacobian.size,
        [pltpu.VMEM((2 * cols * species, probes, width), bf16)],
    )(
        crossing, length_class, rows, direction, smooth_weight,
        across, within, from_across, from_within, begun, norm, curved, jac,
    )
    sums = lax.all_gather(sums, "orbit")

    image, across, within = call(
        backward_kernel,
        (whole, near, near),
        [SMEM()] + [VMEM()] * 4,
        dot_flops,
        2 * jacobian.size,
        [pltpu.VMEM((2 * cols * species, probes, width), f32)],
    )(crossing, weighted, jac, begun, own)
    from_across, from_within = swapped(across, within)

    solution_next, residual_next, step_length = call(
        final_kernel,
        (whole, whole, shape((1, probes), f32)),
        [VMEM()] * 7,
        8 * elements,
        28 * elements,
    )(solution, residual, direction, image, from_across, from_within, sums)
    return solution_next, residual_next, step_length.reshape(probes)


def solution(mesh):
    wide = P(("grp", "orbit"), None, None, None)
    placed = (
        wide, wide, wide, wide,
        P(("grp", "orbit"), None),
        P(("grp", "orbit")),
        P(("grp", "orbit"), None),
        P("grp"),
        P(),
    )
    return jax.shard_map(
        local, mesh=mesh, in_specs=placed, out_specs=(wide, wide, P("grp")), check_vma=False
    )
```

```python
import functools

import jax
import jax.numpy as jnp
from jax import lax
from jax.experimental import pallas as pl
from jax.experimental.pallas import tpu as pltpu
from jax.sharding import PartitionSpec as P

LEVELS = 120
CLASSES = 4
REACH = 8
EPSILON = 1e-06
VMEM_LIMIT = 24 * 1024 * 1024

SMEM = functools.partial(pl.BlockSpec, memory_space=pltpu.SMEM)
VMEM = functools.partial(pl.BlockSpec, memory_space=pltpu.VMEM)
HBM = functools.partial(pl.BlockSpec, memory_space=pltpu.HBM)


def in_hbm(array):
    return pltpu.with_memory_space_constraint(array, pltpu.HBM)


def live_lanes(shape):
    return lax.broadcasted_iota(jnp.int32, shape, len(shape) - 1) < LEVELS


def masked(values):
    return jnp.where(live_lanes(values.shape), values, 0.0)


def call(kernel, out_shape, in_specs, flops, moved, scratch=()):
    return pl.pallas_call(
        kernel,
        out_shape=out_shape,
        in_specs=in_specs,
        out_specs=jax.tree.map(lambda _: VMEM(), out_shape),
        scratch_shapes=list(scratch),
        compiler_params=pltpu.CompilerParams(vmem_limit_bytes=VMEM_LIMIT),
        cost_estimate=pl.CostEstimate(flops=flops, bytes_accessed=moved, transcendentals=0),
    )


def parity():
    return lax.rem(lax.axis_index("orbit"), 2)


def rounding_kernel(direction, across, within):
    rim = across.shape[0]
    odd = parity()
    for c in range(rim):
        across[c] = masked(direction[odd * rim + c]).astype(jnp.bfloat16)
        within[c] = masked(direction[(1 - odd) * rim + c]).astype(jnp.bfloat16)


def coupling(classes, cols, columns):
    total = classes.shape[0]
    first = lax.axis_index("orbit") * cols
    table = {}
    for c in columns:
        length = (classes[lax.rem(first + c + total, total)] + 1) * REACH // CLASSES
        for k in range(1, REACH + 1):
            table[c, k] = jnp.where(k <= length, jnp.float32(1.0 / (k * k)), jnp.float32(0.0))
    return table


def pull(table, to, values):
    result = None
    for c, value in values.items():
        if c != to and abs(c - to) <= REACH:
            term = table[min(c, to), abs(c - to)] * value
            result = term if result is None else result + term
    return -result


def inner_kernel(
    direction, count, residual_hbm, classes_hbm, smooth_hbm, sight_hbm, jac_hbm,
    begun, norm, curved, rows, jac, residual, classes, smooth, sight, sems,
):
    pairs = (
        (classes_hbm, classes), (smooth_hbm, smooth), (sight_hbm, sight),
        (residual_hbm, residual), (jac_hbm, jac),
    )
    copies = [pltpu.make_async_copy(*pair, sems.at[i]) for i, pair in enumerate(pairs)]
    for copy in copies:
        copy.start()
    copies[0].wait()
    copies[1].wait()
    cols = direction.shape[0]
    rim = cols // 2
    table = coupling(classes, cols, range(-REACH, cols))
    weight = smooth[...][:, None, :]
    total = jnp.zeros(norm.shape, jnp.float32)
    values = {c: masked(direction[c]) for c in range(cols)}
    rests = {c: v - v.astype(jnp.bfloat16).astype(jnp.float32) for c, v in values.items()}
    for c in range(cols):
        centre = jnp.float32(1.0)
        for k in range(1, REACH + 1):
            centre = centre + (table[c, k] + table[c - k, k])
        result = weight * (centre * values[c] + pull(table, c, values))
        begun[rim + c] = result
        total = total + jnp.sum(values[c] * result, axis=0)
    for q in range(rim):
        to_left = {c: values[c] if c >= rim else rests[c] for c in range(cols)}
        to_right = {c: values[c] if c < rim else rests[c] for c in range(cols)}
        begun[q] = weight * pull(table, q - rim, to_left)
        begun[rim + cols + q] = weight * pull(table, q + cols, to_right)
    curved[...] = total
    copies[2].wait()
    slot = lax.broadcasted_iota(jnp.int32, rows.shape, 0)
    rows[...] = jnp.where(slot < count[0], sight[...], 0.0)
    copies[3].wait()
    squares = jnp.zeros(norm.shape, jnp.float32)
    for c in range(cols):
        mres = masked(residual[c])
        squares = squares + jnp.sum(mres * mres, axis=0)
    norm[...] = squares
    copies[4].wait()


def forward_kernel(
    crossing, classes, rows, direction, smooth, across, within, from_across, from_within,
    begun, norm, curved, jac, weighted, own, sums, window,
):
    slots, crossings = crossing.shape
    cols, species = direction.shape[:2]
    rim = across.shape[0]
    span = rim * species
    odd = parity()
    places = (1 + odd, across), (2 - odd, within), (3 * odd, from_across), (3 - 3 * odd, from_within)
    for place, part in places:
        window[pl.ds(place * span, span)] = part[...].reshape(span, *part.shape[2:])
    total = curved[...]
    for i in range(slots):
        picked = jnp.concatenate([window[crossing[i, j]] for j in range(crossings)], axis=1)
        tiles = jnp.concatenate([jac[i, j] for j in range(crossings)], axis=1)
        integrals = lax.dot_general(
            tiles, picked, (((1,), (1,)), ((), ())), preferred_element_type=jnp.float32
        )
        integrals = jnp.transpose(integrals)
        product = (rows[pl.ds(i, 1), :] * integrals).astype(jnp.bfloat16)
        weighted[i] = product
        total = total + product.astype(jnp.float32) * integrals
    table = coupling(classes, cols, range(-rim, cols))
    weight = smooth[...][:, None, :]
    before, after = {}, {}
    for c in range(rim):
        before[c - rim] = window[pl.ds(c * species, species)].astype(jnp.float32)
        after[c + cols] = window[pl.ds(3 * span + c * species, species)].astype(jnp.float32)
    for c in range(cols):
        from_before = weight * pull(table, c, before)
        from_after = weight * pull(table, c, after)
        own[c] = begun[rim + c] + (from_before + from_after)
        edges = from_after if c < rim else from_after + from_before
        total = total + 2.0 * jnp.sum(masked(direction[c]) * edges, axis=0)
    half = sums.shape[0]
    parts = [jnp.sum(x, axis=1, keepdims=True) for x in (norm[...], total)]
    parts = [part[h * half : (h + 1) * half] for h in range(2) for part in parts]
    lane = lax.broadcasted_iota(jnp.int32, sums.shape, 1)
    block = jnp.zeros(sums.shape, jnp.float32)
    for k, part in enumerate(parts):
        block = jnp.where(lane == k, part, block)
    sums[...] = block


def backward_kernel(crossing, weighted, jac, begun, own, image, across, within, sums):
    slots, crossings = crossing.shape
    cols, species, probes, tile = own.shape
    rim = across.shape[0]
    span = rim * species
    middle = pl.ds(span, 2 * span)
    sums[pl.ds(0, span)] = begun[pl.ds(0, rim)].reshape(span, probes, tile)
    sums[middle] = own[...].reshape(2 * span, probes, tile)
    sums[pl.ds(3 * span, span)] = begun[pl.ds(rim + cols, rim)].reshape(span, probes, tile)
    for i in range(slots):
        tiles = jnp.concatenate([jac[i, j] for j in range(crossings)], axis=1)
        terms = jnp.dot(weighted[i], tiles, preferred_element_type=jnp.float32)
        for j in range(crossings):
            sums[crossing[i, j]] += terms[:, j * tile : (j + 1) * tile]
    odd = parity()
    for part, place in (across, 3 * odd), (within, 3 - 3 * odd):
        part[...] = sums[pl.ds(place * span, span)].astype(part.dtype).reshape(part.shape)
    image[...] = sums[middle].reshape(image.shape)


def final_kernel(
    solution, residual, direction, image, from_across, from_within, sums,
    solution_next, residual_next, step_length,
):
    whole = jnp.sum(sums[...], axis=0)
    norm = jnp.concatenate([whole[:, 0:1], whole[:, 2:3]], axis=0)
    curvature = jnp.concatenate([whole[:, 1:2], whole[:, 3:4]], axis=0)
    step = norm / (curvature + EPSILON)
    rim = from_across.shape[0]
    wide = jnp.broadcast_to(step, direction.shape[2:])
    step_length[...] = jnp.transpose(wide)[0:1]
    wide = wide[None]
    odd = parity()
    for q in range(rim):
        for c, part in (odd * rim + q, from_across), ((1 - odd) * rim + q, from_within):
            total = masked(image[c] + part[q].astype(jnp.float32))
            solution_next[c] = masked(solution[c] + wide * direction[c])
            residual_next[c] = masked(residual[c]) - wide * total


def swapped(across, within):
    count = lax.axis_size("orbit")
    assert count % 2 == 0
    outer = [(i, (i + 2 * (i % 2) - 1) % count) for i in range(count)]
    inner = [(i, i ^ 1) for i in range(count)]
    return lax.ppermute(across, "orbit", outer), lax.ppermute(within, "orbit", inner)


def local(
    solution, residual, direction, jacobian, crossing, tile_count, sightline_weight,
    length_class, smooth_weight,
):
    cols, species, probes, width = direction.shape
    assert REACH <= cols
    rim = cols // 2
    slots = crossing.shape[0]
    f32, bf16 = jnp.float32, jnp.bfloat16
    shape = jax.ShapeDtypeStruct
    column = (species, probes, width)
    elements = direction.size
    dot_flops = 2 * jacobian.size * probes
    near = shape((rim,) + column, bf16)
    whole = shape(direction.shape, f32)
    small = shape((probes, width), f32)

    across, within = call(
        rounding_kernel, (near, near), [VMEM()], 2 * elements, 6 * elements
    )(direction)
    from_across, from_within = swapped(across, within)

    begun, norm, curved, rows, jac = call(
        inner_kernel,
        (
            shape((2 * cols,) + column, f32), small, small,
            shape(sightline_weight.shape, f32), shape(jacobian.shape, bf16),
        ),
        [VMEM(), SMEM()] + [HBM()] * 5,
        60 * elements,
        4 * jacobian.size,
        [
            pltpu.VMEM(direction.shape, f32),
            pltpu.SMEM(length_class.shape, jnp.int32),
            pltpu.VMEM(smooth_weight.shape, f32),
            pltpu.VMEM(sightline_weight.shape, f32),
            pltpu.SemaphoreType.DMA((5,)),
        ],
    )(
        direction, tile_count,
        *map(in_hbm, (residual, length_class, smooth_weight, sightline_weight, jacobian)),
    )

    devices = lax.axis_size("orbit")
    chips = devices // 2
    weighted, own, sums = call(
        forward_kernel,
        (
            shape((slots, probes, width), bf16), whole,
            shape((probes // 2, width), f32),
        ),
        [SMEM()] * 2 + [VMEM()] * 11,
        dot_flops,
        2 * jacobian.size,
        [pltpu.VMEM((2 * cols * species, probes, width), bf16)],
    )(
        crossing, length_class, rows, direction, smooth_weight,
        across, within, from_across, from_within, begun, norm, curved, jac,
    )
    twin = lax.ppermute(sums, "orbit", [(i, i ^ 1) for i in range(devices)])

    image, across, within = call(
        backward_kernel,
        (whole, near, near),
        [SMEM()] + [VMEM()] * 4,
        dot_flops,
        2 * jacobian.size,
        [pltpu.VMEM((2 * cols * species, probes, width), f32)],
    )(crossing, weighted, jac, begun, own)
    across, within, twin = lax.optimization_barrier((across, within, twin))
    from_across, from_within = swapped(across, within)
    alike = [[2 * i + core for i in range(chips)] for core in range(2)]
    sums = jnp.broadcast_to((sums + twin)[None], (chips,) + sums.shape)
    sums = lax.all_to_all(sums, "orbit", 0, 0, axis_index_groups=alike)

    solution_next, residual_next, step_length = call(
        final_kernel,
        (whole, whole, shape((1, probes), f32)),
        [VMEM()] * 7,
        8 * elements,
        28 * elements,
    )(solution, residual, direction, image, from_across, from_within, sums)
    return solution_next, residual_next, step_length.reshape(probes)


def solution(mesh):
    wide = P(("grp", "orbit"), None, None, None)
    placed = (
        wide, wide, wide, wide,
        P(("grp", "orbit"), None),
        P(("grp", "orbit")),
        P(("grp", "orbit"), None),
        P("grp"),
        P(),
    )
    return jax.shard_map(
        local, mesh=mesh, in_specs=placed, out_specs=(wide, wide, P("grp")), check_vma=False
    )
```

```python
import functools

import jax
import jax.numpy as jnp
from jax import lax
from jax.experimental import pallas as pl
from jax.experimental.pallas import tpu as pltpu
from jax.sharding import PartitionSpec as P

LEVELS = 120
CLASSES = 4
REACH = 8
EPSILON = 1e-06
VMEM_LIMIT = 24 * 1024 * 1024

SMEM = functools.partial(pl.BlockSpec, memory_space=pltpu.SMEM)
VMEM = functools.partial(pl.BlockSpec, memory_space=pltpu.VMEM)
HBM = functools.partial(pl.BlockSpec, memory_space=pltpu.HBM)


def in_hbm(array):
    return pltpu.with_memory_space_constraint(array, pltpu.HBM)


def live_lanes(shape):
    return lax.broadcasted_iota(jnp.int32, shape, len(shape) - 1) < LEVELS


def masked(values):
    return jnp.where(live_lanes(values.shape), values, 0.0)


def call(kernel, out_shape, in_specs, flops, moved, scratch=()):
    return pl.pallas_call(
        kernel,
        out_shape=out_shape,
        in_specs=in_specs,
        out_specs=jax.tree.map(lambda _: VMEM(), out_shape),
        scratch_shapes=list(scratch),
        compiler_params=pltpu.CompilerParams(vmem_limit_bytes=VMEM_LIMIT),
        cost_estimate=pl.CostEstimate(flops=flops, bytes_accessed=moved, transcendentals=0),
    )


def parity():
    return lax.rem(lax.axis_index("orbit"), 2)


def rounding_kernel(direction, across, within):
    rim = across.shape[0]
    odd = parity()
    for c in range(rim):
        across[c] = masked(direction[odd * rim + c]).astype(jnp.bfloat16)
        within[c] = masked(direction[(1 - odd) * rim + c]).astype(jnp.bfloat16)


def coupling(classes, cols, columns):
    total = classes.shape[0]
    first = lax.axis_index("orbit") * cols
    table = {}
    for c in columns:
        length = (classes[lax.rem(first + c + total, total)] + 1) * REACH // CLASSES
        for k in range(1, REACH + 1):
            table[c, k] = jnp.where(k <= length, jnp.float32(1.0 / (k * k)), jnp.float32(0.0))
    return table


def pull(table, to, values):
    result = None
    for c, value in values.items():
        if c != to and abs(c - to) <= REACH:
            term = table[min(c, to), abs(c - to)] * value
            result = term if result is None else result + term
    return -result


def inner_kernel(
    direction, count, residual_hbm, classes_hbm, smooth_hbm, sight_hbm, jac_hbm,
    begun, norm, curved, rows, jac, residual, classes, smooth, sight, sems,
):
    pairs = (
        (classes_hbm, classes), (smooth_hbm, smooth), (sight_hbm, sight),
        (residual_hbm, residual), (jac_hbm, jac),
    )
    copies = [pltpu.make_async_copy(*pair, sems.at[i]) for i, pair in enumerate(pairs)]
    for copy in copies:
        copy.start()
    copies[0].wait()
    copies[1].wait()
    cols = direction.shape[0]
    rim = cols // 2
    table = coupling(classes, cols, range(-REACH, cols))
    weight = smooth[...][:, None, :]
    total = jnp.zeros(norm.shape, jnp.float32)
    values = {c: masked(direction[c]) for c in range(cols)}
    rests = {c: v - v.astype(jnp.bfloat16).astype(jnp.float32) for c, v in values.items()}
    for c in range(cols):
        centre = jnp.float32(1.0)
        for k in range(1, REACH + 1):
            centre = centre + (table[c, k] + table[c - k, k])
        result = weight * (centre * values[c] + pull(table, c, values))
        begun[rim + c] = result
        total = total + jnp.sum(values[c] * result, axis=0)
    for q in range(rim):
        to_left = {c: values[c] if c >= rim else rests[c] for c in range(cols)}
        to_right = {c: values[c] if c < rim else rests[c] for c in range(cols)}
        begun[q] = weight * pull(table, q - rim, to_left)
        begun[rim + cols + q] = weight * pull(table, q + cols, to_right)
    curved[...] = total
    copies[2].wait()
    slot = lax.broadcasted_iota(jnp.int32, rows.shape, 0)
    rows[...] = jnp.where(slot < count[0], sight[...], 0.0)
    copies[3].wait()
    squares = jnp.zeros(norm.shape, jnp.float32)
    for c in range(cols):
        mres = masked(residual[c])
        squares = squares + jnp.sum(mres * mres, axis=0)
    norm[...] = squares
    copies[4].wait()


def forward_kernel(
    crossing, classes, rows, direction, smooth, across, within, from_across, from_within,
    begun, norm, curved, jac, weighted, own, sums, window,
):
    slots, crossings = crossing.shape
    cols, species = direction.shape[:2]
    rim = across.shape[0]
    span = rim * species
    odd = parity()
    places = (1 + odd, across), (2 - odd, within), (3 * odd, from_across), (3 - 3 * odd, from_within)
    for place, part in places:
        window[pl.ds(place * span, span)] = part[...].reshape(span, *part.shape[2:])
    total = curved[...]
    for i in range(slots):
        picked = jnp.concatenate([window[crossing[i, j]] for j in range(crossings)], axis=1)
        tiles = jnp.concatenate([jac[i, j] for j in range(crossings)], axis=1)
        integrals = lax.dot_general(
            tiles, picked, (((1,), (1,)), ((), ())), preferred_element_type=jnp.float32
        )
        integrals = jnp.transpose(integrals)
        product = (rows[pl.ds(i, 1), :] * integrals).astype(jnp.bfloat16)
        weighted[i] = product
        total = total + product.astype(jnp.float32) * integrals
    table = coupling(classes, cols, range(-rim, cols))
    weight = smooth[...][:, None, :]
    before, after = {}, {}
    for c in range(rim):
        before[c - rim] = window[pl.ds(c * species, species)].astype(jnp.float32)
        after[c + cols] = window[pl.ds(3 * span + c * species, species)].astype(jnp.float32)
    for c in range(cols):
        from_before = weight * pull(table, c, before)
        from_after = weight * pull(table, c, after)
        own[c] = begun[rim + c] + (from_before + from_after)
        edges = from_after if c < rim else from_after + from_before
        total = total + 2.0 * jnp.sum(masked(direction[c]) * edges, axis=0)
    half = sums.shape[0]
    parts = [jnp.sum(x, axis=1, keepdims=True) for x in (norm[...], total)]
    parts = [part[h * half : (h + 1) * half] for h in range(2) for part in parts]
    lane = lax.broadcasted_iota(jnp.int32, sums.shape, 1)
    block = jnp.zeros(sums.shape, jnp.float32)
    for k, part in enumerate(parts):
        block = jnp.where(lane == k, part, block)
    sums[...] = block


def backward_kernel(crossing, weighted, jac, begun, own, image, across, within, sums):
    slots, crossings = crossing.shape
    cols, species, probes, tile = own.shape
    rim = across.shape[0]
    span = rim * species
    middle = pl.ds(span, 2 * span)
    sums[pl.ds(0, span)] = begun[pl.ds(0, rim)].reshape(span, probes, tile)
    sums[middle] = own[...].reshape(2 * span, probes, tile)
    sums[pl.ds(3 * span, span)] = begun[pl.ds(rim + cols, rim)].reshape(span, probes, tile)
    for i in range(slots):
        tiles = jnp.concatenate([jac[i, j] for j in range(crossings)], axis=1)
        terms = jnp.dot(weighted[i], tiles, preferred_element_type=jnp.float32)
        for j in range(crossings):
            sums[crossing[i, j]] += terms[:, j * tile : (j + 1) * tile]
    odd = parity()
    for part, place in (across, 3 * odd), (within, 3 - 3 * odd):
        part[...] = sums[pl.ds(place * span, span)].astype(part.dtype).reshape(part.shape)
    image[...] = sums[middle].reshape(image.shape)


def final_kernel(
    solution, residual, direction, image, from_across, from_within, sums,
    solution_next, residual_next, step_length,
):
    whole = jnp.sum(sums[...], axis=0)
    norm = jnp.concatenate([whole[:, 0:1], whole[:, 2:3]], axis=0)
    curvature = jnp.concatenate([whole[:, 1:2], whole[:, 3:4]], axis=0)
    step = norm / (curvature + EPSILON)
    rim = from_across.shape[0]
    wide = jnp.broadcast_to(step, direction.shape[2:])
    step_length[...] = jnp.transpose(wide)[0:1]
    wide = wide[None]
    odd = parity()
    for q in range(rim):
        for c, part in (odd * rim + q, from_across), ((1 - odd) * rim + q, from_within):
            total = masked(image[c] + part[q].astype(jnp.float32))
            solution_next[c] = masked(solution[c] + wide * direction[c])
            residual_next[c] = masked(residual[c]) - wide * total


def swapped(across, within):
    count = lax.axis_size("orbit")
    assert count % 2 == 0
    outer = [(i, (i + 2 * (i % 2) - 1) % count) for i in range(count)]
    inner = [(i, i ^ 1) for i in range(count)]
    return lax.ppermute(across, "orbit", outer), lax.ppermute(within, "orbit", inner)


def local(
    solution, residual, direction, jacobian, crossing, tile_count, sightline_weight,
    length_class, smooth_weight,
):
    cols, species, probes, width = direction.shape
    assert REACH <= cols
    rim = cols // 2
    slots = crossing.shape[0]
    f32, bf16 = jnp.float32, jnp.bfloat16
    shape = jax.ShapeDtypeStruct
    column = (species, probes, width)
    elements = direction.size
    dot_flops = 2 * jacobian.size * probes
    near = shape((rim,) + column, bf16)
    whole = shape(direction.shape, f32)
    small = shape((probes, width), f32)

    across, within = call(
        rounding_kernel, (near, near), [VMEM()], 2 * elements, 6 * elements
    )(direction)
    from_across, from_within = swapped(across, within)

    begun, norm, curved, rows, jac = call(
        inner_kernel,
        (
            shape((2 * cols,) + column, f32), small, small,
            shape(sightline_weight.shape, f32), shape(jacobian.shape, bf16),
        ),
        [VMEM(), SMEM()] + [HBM()] * 5,
        60 * elements,
        4 * jacobian.size,
        [
            pltpu.VMEM(direction.shape, f32),
            pltpu.SMEM(length_class.shape, jnp.int32),
            pltpu.VMEM(smooth_weight.shape, f32),
            pltpu.VMEM(sightline_weight.shape, f32),
            pltpu.SemaphoreType.DMA((5,)),
        ],
    )(
        direction, tile_count,
        *map(in_hbm, (residual, length_class, smooth_weight, sightline_weight, jacobian)),
    )

    devices = lax.axis_size("orbit")
    peers = devices // 2
    weighted, own, sums = call(
        forward_kernel,
        (
            shape((slots, probes, width), bf16), whole,
            shape((probes // 2, width), f32),
        ),
        [SMEM()] * 2 + [VMEM()] * 11,
        dot_flops,
        2 * jacobian.size,
        [pltpu.VMEM((2 * cols * species, probes, width), bf16)],
    )(
        crossing, length_class, rows, direction, smooth_weight,
        across, within, from_across, from_within, begun, norm, curved, jac,
    )
    assert devices % 4 == 0
    twin = lax.ppermute(sums, "orbit", [(i, i ^ 2) for i in range(devices)])

    image, across, within = call(
        backward_kernel,
        (whole, near, near),
        [SMEM()] + [VMEM()] * 4,
        dot_flops,
        2 * jacobian.size,
        [pltpu.VMEM((2 * cols * species, probes, width), f32)],
    )(crossing, weighted, jac, begun, own)
    across, within, twin = lax.optimization_barrier((across, within, twin))
    from_across, from_within = swapped(across, within)
    alike = [[i for i in range(devices) if i & 2 == side] for side in (0, 2)]
    sums = jnp.broadcast_to((sums + twin)[None], (peers,) + sums.shape)
    sums = lax.all_to_all(sums, "orbit", 0, 0, axis_index_groups=alike)

    solution_next, residual_next, step_length = call(
        final_kernel,
        (whole, whole, shape((1, probes), f32)),
        [VMEM()] * 7,
        8 * elements,
        28 * elements,
    )(solution, residual, direction, image, from_across, from_within, sums)
    return solution_next, residual_next, step_length.reshape(probes)


def solution(mesh):
    wide = P(("grp", "orbit"), None, None, None)
    placed = (
        wide, wide, wide, wide,
        P(("grp", "orbit"), None),
        P(("grp", "orbit")),
        P(("grp", "orbit"), None),
        P("grp"),
        P(),
    )
    return jax.shard_map(
        local, mesh=mesh, in_specs=placed, out_specs=(wide, wide, P("grp")), check_vma=False
    )
```

```python
import functools

import jax
import jax.numpy as jnp
from jax import lax
from jax.experimental import pallas as pl
from jax.experimental.pallas import tpu as pltpu
from jax.sharding import PartitionSpec as P

LEVELS = 120
CLASSES = 4
REACH = 8
EPSILON = 1e-06
VMEM_LIMIT = 24 * 1024 * 1024

SMEM = functools.partial(pl.BlockSpec, memory_space=pltpu.SMEM)
VMEM = functools.partial(pl.BlockSpec, memory_space=pltpu.VMEM)
HBM = functools.partial(pl.BlockSpec, memory_space=pltpu.HBM)


def in_hbm(array):
    return pltpu.with_memory_space_constraint(array, pltpu.HBM)


def live_lanes(shape):
    return lax.broadcasted_iota(jnp.int32, shape, len(shape) - 1) < LEVELS


def masked(values):
    return jnp.where(live_lanes(values.shape), values, 0.0)


def call(kernel, out_shape, in_specs, flops, moved, scratch=(), out_specs=None):
    return pl.pallas_call(
        kernel,
        out_shape=out_shape,
        in_specs=in_specs,
        out_specs=tuple(out_specs or [VMEM()] * len(out_shape)),
        scratch_shapes=list(scratch),
        compiler_params=pltpu.CompilerParams(vmem_limit_bytes=VMEM_LIMIT),
        cost_estimate=pl.CostEstimate(flops=flops, bytes_accessed=moved, transcendentals=0),
    )


def parity():
    return lax.rem(lax.axis_index("orbit"), 2)


def rounding_kernel(direction, across, within):
    rim = across.shape[0]
    odd = parity()
    for c in range(rim):
        across[c] = masked(direction[odd * rim + c]).astype(jnp.bfloat16)
        within[c] = masked(direction[(1 - odd) * rim + c]).astype(jnp.bfloat16)


def coupling(classes, cols, columns):
    total = classes.shape[0]
    first = lax.axis_index("orbit") * cols
    table = {}
    for c in columns:
        length = (classes[lax.rem(first + c + total, total)] + 1) * REACH // CLASSES
        for k in range(1, REACH + 1):
            table[c, k] = jnp.where(k <= length, jnp.float32(1.0 / (k * k)), jnp.float32(0.0))
    return table


def pull(table, to, values):
    result = None
    for c, value in values.items():
        if c != to and abs(c - to) <= REACH:
            term = table[min(c, to), abs(c - to)] * value
            result = term if result is None else result + term
    return -result


def side_pulls(table, values, on_left, cols):
    rim = len(values)
    for c in range(cols):
        result = None
        for q, value in enumerate(values):
            before, after = c - q + rim, q + cols - c
            left = table[q - rim, before] if before <= REACH else jnp.float32(0.0)
            right = table[c, after] if after <= REACH else jnp.float32(0.0)
            term = jnp.where(on_left, left, right) * value
            result = term if result is None else result + term
        counted = jnp.where(on_left, jnp.float32(0.0 if c < rim else 2.0), jnp.float32(2.0))
        yield c, -result, counted


def early_positions(crossings):
    return 2 * (crossings * 7 // 24)


def shadow_kernel(
    count, direction, across, within, from_within,
    residual_hbm, classes_hbm, smooth_hbm, sight_hbm, crossing_hbm, jac_hbm,
    begun, norm, curved, rows, jac, partial, order,
    residual, classes, smooth, sight, crossing, window, sems,
):
    slots, crossings = crossing.shape
    pairs = (
        (classes_hbm, classes), (smooth_hbm, smooth), (sight_hbm, sight), (residual_hbm, residual),
        (crossing_hbm, crossing),
    )
    copies = [pltpu.make_async_copy(*pair, sems.at[i]) for i, pair in enumerate(pairs)]
    loads = [
        pltpu.make_async_copy(jac_hbm.at[i], jac.at[i], sems.at[len(pairs) + i]) for i in range(slots)
    ]
    for copy in copies + loads:
        copy.start()
    cols, species = direction.shape[:2]
    rim = cols // 2
    span = rim * species
    odd = parity()

    for place, part in (1 + odd, across), (2 - odd, within), (3 - 3 * odd, from_within):
        window[pl.ds(place * span, span)] = part[...].reshape(span, *part.shape[2:])
    window[4 * span] = jnp.zeros(window.shape[1:], window.dtype)

    copies[4].wait()
    known_from = (1 - odd) * span
    for i in range(slots):
        head, tail = jnp.int32(0), jnp.int32(crossings - 1)
        for j in range(crossings):
            tile = crossing[i, j]
            known = (tile >= known_from) & (tile < known_from + 3 * span)
            order[i, jnp.where(known, head, tail)] = j
            step = known.astype(jnp.int32)
            head, tail = head + step, tail + step - 1
        order[i, crossings] = head

    copies[0].wait()
    copies[1].wait()
    table = coupling(classes, cols, range(-REACH, cols))
    weight = smooth[...][:, None, :]
    total = jnp.zeros(norm.shape, jnp.float32)
    values = {c: masked(direction[c]) for c in range(cols)}
    rests = {c: v - v.astype(jnp.bfloat16).astype(jnp.float32) for c, v in values.items()}
    beside = [from_within[q].astype(jnp.float32) for q in range(rim)]
    for c, side, counted in side_pulls(table, beside, odd == 1, cols):
        centre = jnp.float32(1.0)
        for k in range(1, REACH + 1):
            centre = centre + (table[c, k] + table[c - k, k])
        inner = centre * values[c] + pull(table, c, values)
        begun[rim + c] = weight * (inner + side)
        total = total + jnp.sum(values[c] * (weight * (inner + counted * side)), axis=0)
    for q in range(rim):
        to_left = {c: values[c] if c >= rim else rests[c] for c in range(cols)}
        to_right = {c: values[c] if c < rim else rests[c] for c in range(cols)}
        begun[q] = weight * pull(table, q - rim, to_left)
        begun[rim + cols + q] = weight * pull(table, q + cols, to_right)
    curved[...] = total
    copies[2].wait()
    slot = lax.broadcasted_iota(jnp.int32, rows.shape, 0)
    rows[...] = jnp.where(slot < count[0], sight[...], 0.0)
    copies[3].wait()
    squares = jnp.zeros(norm.shape, jnp.float32)
    for c in range(cols):
        mres = masked(residual[c])
        squares = squares + jnp.sum(mres * mres, axis=0)
    norm[...] = squares

    for i in range(slots):
        loads[i].wait()
        picked, tiles = [], []
        for place in range(early_positions(crossings)):
            j = order[i, place]
            here = place < order[i, crossings]
            picked.append(window[jnp.where(here, crossing[i, j], 4 * span)])
            tiles.append(jac[i, j])
        partial[i] = jnp.transpose(project(tiles, picked))


def project(tiles, picked):
    return lax.dot_general(
        jnp.concatenate(tiles, axis=1), jnp.concatenate(picked, axis=1),
        (((1,), (1,)), ((), ())), preferred_element_type=jnp.float32,
    )


def forward_kernel(
    crossing, order, classes, rows, direction, smooth, across, within, from_across, from_within,
    begun, norm, curved, jac, partial, weighted, own, sums, window, integrals,
):
    slots, crossings = crossing.shape
    early = early_positions(crossings)
    cols, species = direction.shape[:2]
    rim = across.shape[0]
    span = rim * species
    odd = parity()
    places = (1 + odd, across), (2 - odd, within), (3 * odd, from_across), (3 - 3 * odd, from_within)
    for place, part in places:
        window[pl.ds(place * span, span)] = part[...].reshape(span, *part.shape[2:])
    for i in range(slots):
        picked, tiles = [], []
        for place in range(early, crossings):
            j = order[i, place]
            picked.append(window[crossing[i, j]])
            tiles.append(jac[i, j])
        integrals[i] = partial[i] + jnp.transpose(project(tiles, picked))

    fewest = order[0, crossings]
    for i in range(1, slots):
        fewest = jnp.minimum(fewest, order[i, crossings])

    @pl.when(fewest < early)
    def _():
        for i in range(slots):
            @pl.loop(order[i, crossings], early)
            def _(place):
                j = order[i, place]
                integrals[i] += jnp.transpose(project([jac[i, j]], [window[crossing[i, j]]]))

    total = curved[...]
    for i in range(slots):
        product = (rows[pl.ds(i, 1), :] * integrals[i]).astype(jnp.bfloat16)
        weighted[i] = product
        total = total + product.astype(jnp.float32) * integrals[i]
    table = coupling(classes, cols, range(-rim, cols))
    weight = smooth[...][:, None, :]
    beside = [from_across[q].astype(jnp.float32) for q in range(rim)]
    for c, side, counted in side_pulls(table, beside, odd == 0, cols):
        side = weight * side
        own[c] = begun[rim + c] + side
        total = total + counted * jnp.sum(masked(direction[c]) * side, axis=0)
    half = sums.shape[0]
    parts = [jnp.sum(x, axis=1, keepdims=True) for x in (norm[...], total)]
    parts = [part[h * half : (h + 1) * half] for h in range(2) for part in parts]
    lane = lax.broadcasted_iota(jnp.int32, sums.shape, 1)
    block = jnp.zeros(sums.shape, jnp.float32)
    for k, part in enumerate(parts):
        block = jnp.where(lane == k, part, block)
    sums[...] = block


def backward_kernel(crossing, weighted, jac, begun, own, image, across, within, sums):
    slots, crossings = crossing.shape
    cols, species, probes, tile = own.shape
    rim = across.shape[0]
    span = rim * species
    middle = pl.ds(span, 2 * span)
    sums[pl.ds(0, span)] = begun[pl.ds(0, rim)].reshape(span, probes, tile)
    sums[middle] = own[...].reshape(2 * span, probes, tile)
    sums[pl.ds(3 * span, span)] = begun[pl.ds(rim + cols, rim)].reshape(span, probes, tile)
    for i in range(slots):
        tiles = jnp.concatenate([jac[i, j] for j in range(crossings)], axis=1)
        terms = jnp.dot(weighted[i], tiles, preferred_element_type=jnp.float32)
        for j in range(crossings):
            sums[crossing[i, j]] += terms[:, j * tile : (j + 1) * tile]
    odd = parity()
    for part, place in (across, 3 * odd), (within, 3 - 3 * odd):
        part[...] = sums[pl.ds(place * span, span)].astype(part.dtype).reshape(part.shape)
    image[...] = sums[middle].reshape(image.shape)


def final_kernel(
    solution, residual, direction, image, from_across, from_within, sums,
    solution_next, residual_next, step_length,
):
    whole = jnp.sum(sums[...], axis=0)
    norm = jnp.concatenate([whole[:, 0:1], whole[:, 2:3]], axis=0)
    curvature = jnp.concatenate([whole[:, 1:2], whole[:, 3:4]], axis=0)
    step = norm / (curvature + EPSILON)
    rim = from_across.shape[0]
    wide = jnp.broadcast_to(step, direction.shape[2:])
    step_length[...] = jnp.transpose(wide)[0:1]
    wide = wide[None]
    odd = parity()
    for q in range(rim):
        for c, part in (odd * rim + q, from_across), ((1 - odd) * rim + q, from_within):
            total = masked(image[c] + part[q].astype(jnp.float32))
            solution_next[c] = masked(solution[c] + wide * direction[c])
            residual_next[c] = masked(residual[c]) - wide * total


def swapped(across, within):
    count = lax.axis_size("orbit")
    assert count % 2 == 0
    outer = [(i, (i + 2 * (i % 2) - 1) % count) for i in range(count)]
    inner = [(i, i ^ 1) for i in range(count)]
    from_within = lax.ppermute(within, "orbit", inner)
    return lax.ppermute(across, "orbit", outer), from_within


def local(
    solution, residual, direction, jacobian, crossing, tile_count, sightline_weight,
    length_class, smooth_weight,
):
    cols, species, probes, width = direction.shape
    assert REACH <= cols
    rim = cols // 2
    slots, crossings = crossing.shape
    f32, bf16 = jnp.float32, jnp.bfloat16
    shape = jax.ShapeDtypeStruct
    column = (species, probes, width)
    elements = direction.size
    dot_flops = 2 * jacobian.size * probes
    near = shape((rim,) + column, bf16)
    whole = shape(direction.shape, f32)
    small = shape((probes, width), f32)

    across, within = call(
        rounding_kernel, (near, near), [VMEM()], 2 * elements, 6 * elements
    )(direction)
    from_across, from_within = swapped(across, within)

    begun, norm, curved, rows, jac, partial, order = call(
        shadow_kernel,
        (
            shape((2 * cols,) + column, f32), small, small,
            shape(sightline_weight.shape, f32), shape(jacobian.shape, bf16),
            shape((slots, probes, width), f32), shape((slots, crossings + 1), jnp.int32),
        ),
        [SMEM()] + [VMEM()] * 4 + [HBM()] * 6,
        dot_flops,
        4 * jacobian.size,
        [
            pltpu.VMEM(direction.shape, f32),
            pltpu.SMEM(length_class.shape, jnp.int32),
            pltpu.VMEM(smooth_weight.shape, f32),
            pltpu.VMEM(sightline_weight.shape, f32),
            pltpu.SMEM(crossing.shape, jnp.int32),
            pltpu.VMEM((2 * cols * species + 1, probes, width), bf16),
            pltpu.SemaphoreType.DMA((5 + slots,)),
        ],
        [VMEM()] * 6 + [SMEM()],
    )(
        tile_count, direction, across, within, from_within,
        *map(in_hbm, (
            residual, length_class, smooth_weight, sightline_weight, crossing, jacobian,
        )),
    )

    devices = lax.axis_size("orbit")
    peers = devices // 2
    weighted, own, sums = call(
        forward_kernel,
        (
            shape((slots, probes, width), bf16), whole,
            shape((probes // 2, width), f32),
        ),
        [SMEM()] * 3 + [VMEM()] * 12,
        dot_flops,
        2 * jacobian.size,
        [
            pltpu.VMEM((2 * cols * species, probes, width), bf16),
            pltpu.VMEM((slots, probes, width), f32),
        ],
    )(
        crossing, order, length_class, rows, direction, smooth_weight,
        across, within, from_across, from_within, begun, norm, curved, jac, partial,
    )
    assert devices % 4 == 0
    twin = lax.ppermute(sums, "orbit", [(i, i ^ 2) for i in range(devices)])

    image, across, within = call(
        backward_kernel,
        (whole, near, near),
        [SMEM()] + [VMEM()] * 4,
        dot_flops,
        2 * jacobian.size,
        [pltpu.VMEM((2 * cols * species, probes, width), f32)],
    )(crossing, weighted, jac, begun, own)
    across, within, twin = lax.optimization_barrier((across, within, twin))
    from_across, from_within = swapped(across, within)
    alike = [[i for i in range(devices) if i & 2 == side] for side in (0, 2)]
    sums = jnp.broadcast_to((sums + twin)[None], (peers,) + sums.shape)
    sums = lax.all_to_all(sums, "orbit", 0, 0, axis_index_groups=alike)

    solution_next, residual_next, step_length = call(
        final_kernel,
        (whole, whole, shape((1, probes), f32)),
        [VMEM()] * 7,
        8 * elements,
        28 * elements,
    )(solution, residual, direction, image, from_across, from_within, sums)
    return solution_next, residual_next, step_length.reshape(probes)


def solution(mesh):
    wide = P(("grp", "orbit"), None, None, None)
    placed = (
        wide, wide, wide, wide,
        P(("grp", "orbit"), None),
        P(("grp", "orbit")),
        P(("grp", "orbit"), None),
        P("grp"),
        P(),
    )
    return jax.shard_map(
        local, mesh=mesh, in_specs=placed, out_specs=(wide, wide, P("grp")), check_vma=False
    )
```

```python
import functools

import jax
import jax.numpy as jnp
from jax import lax
from jax.experimental import pallas as pl
from jax.experimental.pallas import tpu as pltpu
from jax.sharding import PartitionSpec as P

LEVELS = 120
CLASSES = 4
REACH = 8
EPSILON = 1e-06
VMEM_LIMIT = 24 * 1024 * 1024

SMEM = functools.partial(pl.BlockSpec, memory_space=pltpu.SMEM)
VMEM = functools.partial(pl.BlockSpec, memory_space=pltpu.VMEM)
HBM = functools.partial(pl.BlockSpec, memory_space=pltpu.HBM)


def in_hbm(array):
    return pltpu.with_memory_space_constraint(array, pltpu.HBM)


def live_lanes(shape):
    return lax.broadcasted_iota(jnp.int32, shape, len(shape) - 1) < LEVELS


def masked(values):
    return jnp.where(live_lanes(values.shape), values, 0.0)


def call(kernel, out_shape, in_specs, flops, moved, scratch=(), out_specs=None):
    return pl.pallas_call(
        kernel,
        out_shape=out_shape,
        in_specs=in_specs,
        out_specs=tuple(out_specs or [VMEM()] * len(out_shape)),
        scratch_shapes=list(scratch),
        compiler_params=pltpu.CompilerParams(vmem_limit_bytes=VMEM_LIMIT),
        cost_estimate=pl.CostEstimate(flops=flops, bytes_accessed=moved, transcendentals=0),
    )


def parity():
    return lax.rem(lax.axis_index("orbit"), 2)


def rounding_kernel(direction, across, within):
    rim = across.shape[0]
    odd = parity()
    for c in range(rim):
        across[c] = masked(direction[odd * rim + c]).astype(jnp.bfloat16)
        within[c] = masked(direction[(1 - odd) * rim + c]).astype(jnp.bfloat16)


def coupling(classes, cols, columns):
    total = classes.shape[0]
    first = lax.axis_index("orbit") * cols
    table = {}
    for c in columns:
        length = (classes[lax.rem(first + c + total, total)] + 1) * REACH // CLASSES
        for k in range(1, REACH + 1):
            table[c, k] = jnp.where(k <= length, jnp.float32(1.0 / (k * k)), jnp.float32(0.0))
    return table


def pull(table, to, values):
    result = None
    for c, value in values.items():
        if c != to and abs(c - to) <= REACH:
            term = table[min(c, to), abs(c - to)] * value
            result = term if result is None else result + term
    return 0.0 if result is None else -result


def inner_kernel(
    direction, count, residual_hbm, classes_hbm, smooth_hbm, sight_hbm, jac_hbm,
    begun, faced, norm, curved, rows, jac, residual, classes, smooth, sight, sems,
):
    pairs = (
        (classes_hbm, classes), (smooth_hbm, smooth), (sight_hbm, sight),
        (residual_hbm, residual), (jac_hbm, jac),
    )
    copies = [pltpu.make_async_copy(*pair, sems.at[i]) for i, pair in enumerate(pairs)]
    for copy in copies:
        copy.start()
    copies[0].wait()
    copies[1].wait()
    cols = direction.shape[0]
    rim = cols // 2
    table = coupling(classes, cols, range(-REACH, cols))
    weight = smooth[...][:, None, :]
    total = jnp.zeros(norm.shape, jnp.float32)
    values = {c: masked(direction[c]) for c in range(cols)}
    rests = {c: v - v.astype(jnp.bfloat16).astype(jnp.float32) for c, v in values.items()}
    for c in range(cols):
        centre = jnp.float32(1.0)
        for k in range(1, REACH + 1):
            centre = centre + (table[c, k] + table[c - k, k])
        result = weight * (centre * values[c] + pull(table, c, values))
        begun[rim + c] = result
        total = total + jnp.sum(values[c] * result, axis=0)
    low = {c: values[c] for c in range(rim)}
    high = {c: values[c] for c in range(rim, cols)}
    low_rests = {c: rests[c] for c in range(rim)}
    high_rests = {c: rests[c] for c in range(rim, cols)}
    for q in range(rim):
        facing = weight * pull(table, q - rim, high)
        faced[0, q] = facing
        begun[q] = facing + weight * pull(table, q - rim, low_rests)
        facing = weight * pull(table, q + cols, low)
        faced[1, q] = facing + weight * pull(table, q + cols, high)
        begun[rim + cols + q] = facing + weight * pull(table, q + cols, high_rests)
    curved[...] = total
    copies[2].wait()
    slot = lax.broadcasted_iota(jnp.int32, rows.shape, 0)
    rows[...] = jnp.where(slot < count[0], sight[...], 0.0)
    copies[3].wait()
    squares = jnp.zeros(norm.shape, jnp.float32)
    for c in range(cols):
        mres = masked(residual[c])
        squares = squares + jnp.sum(mres * mres, axis=0)
    norm[...] = squares
    copies[4].wait()


def forward_kernel(
    crossing, rows, across, within, from_across, from_within, faced, norm, curved, jac,
    weighted, sums, window,
):
    slots, crossings = crossing.shape
    rim, species = across.shape[:2]
    span = rim * species
    odd = parity()
    places = (1 + odd, across), (2 - odd, within), (3 * odd, from_across), (3 - 3 * odd, from_within)
    for place, part in places:
        window[pl.ds(place * span, span)] = part[...].reshape(span, *part.shape[2:])
    total = curved[...]
    for q in range(rim):
        for side, part in (odd, from_across), (1 - odd, from_within):
            total = total + 2.0 * jnp.sum(faced[side, q] * part[q].astype(jnp.float32), axis=0)
    for i in range(slots):
        picked = jnp.concatenate([window[crossing[i, j]] for j in range(crossings)], axis=1)
        tiles = jnp.concatenate([jac[i, j] for j in range(crossings)], axis=1)
        integrals = lax.dot_general(
            tiles, picked, (((1,), (1,)), ((), ())), preferred_element_type=jnp.float32
        )
        integrals = jnp.transpose(integrals)
        product = (rows[pl.ds(i, 1), :] * integrals).astype(jnp.bfloat16)
        weighted[i] = product
        total = total + product.astype(jnp.float32) * integrals
    half = sums.shape[0]
    parts = [jnp.sum(x, axis=1, keepdims=True) for x in (norm[...], total)]
    parts = [part[h * half : (h + 1) * half] for h in range(2) for part in parts]
    lane = lax.broadcasted_iota(jnp.int32, sums.shape, 1)
    block = jnp.zeros(sums.shape, jnp.float32)
    for k, part in enumerate(parts):
        block = jnp.where(lane == k, part, block)
    sums[...] = block


def backward_kernel(
    crossing, classes, smooth, weighted, jac, begun, from_across, from_within,
    image, across, within, sums, near,
):
    slots, crossings = crossing.shape
    cols, species, probes, tile = image.shape
    rim = across.shape[0]
    span = rim * species
    odd = parity()
    near[odd] = from_across[...].astype(jnp.float32)
    near[1 - odd] = from_within[...].astype(jnp.float32)
    table = coupling(classes, cols, range(-rim, cols))
    weight = smooth[...][:, None, :]
    beside = {q - rim: near[0, q] for q in range(rim)} | {q + cols: near[1, q] for q in range(rim)}
    for c in range(cols):
        place = pl.ds(span + c * species, species)
        sums[place] = begun[rim + c] + weight * pull(table, c, beside)
    sums[pl.ds(0, span)] = begun[pl.ds(0, rim)].reshape(span, probes, tile)
    sums[pl.ds(3 * span, span)] = begun[pl.ds(rim + cols, rim)].reshape(span, probes, tile)
    for i in range(slots):
        tiles = jnp.concatenate([jac[i, j] for j in range(crossings)], axis=1)
        terms = jnp.dot(weighted[i], tiles, preferred_element_type=jnp.float32)
        for j in range(crossings):
            sums[crossing[i, j]] += terms[:, j * tile : (j + 1) * tile]
    for part, place in (across, 3 * odd), (within, 3 - 3 * odd):
        part[...] = sums[pl.ds(place * span, span)].astype(part.dtype).reshape(part.shape)
    image[...] = sums[pl.ds(span, 2 * span)].reshape(image.shape)


def final_kernel(
    solution, residual, direction, image, from_across, from_within, sums,
    solution_next, residual_next, step_length, made, sems,
):
    whole = jnp.sum(sums[...], axis=0)
    norm = jnp.concatenate([whole[:, 0:1], whole[:, 2:3]], axis=0)
    curvature = jnp.concatenate([whole[:, 1:2], whole[:, 3:4]], axis=0)
    step = norm / (curvature + EPSILON)
    rim = from_across.shape[0]
    wide = jnp.broadcast_to(step, direction.shape[2:])
    step_length[...] = jnp.transpose(wide)[0:1]
    wide = wide[None]
    odd = parity()
    copies = []
    for q in range(rim):
        for c, part in (odd * rim + q, from_across), ((1 - odd) * rim + q, from_within):
            k = len(copies) // 2
            made[0, k] = masked(solution[c] + wide * direction[c])
            made[1, k] = masked(residual[c]) - wide * masked(image[c] + part[q].astype(jnp.float32))
            for half, out in enumerate((solution_next, residual_next)):
                copy = pltpu.make_async_copy(made.at[half, k], out.at[c], sems.at[half, k])
                copy.start()
                copies.append(copy)
    for copy in copies:
        copy.wait()


def swapped(across, within):
    count = lax.axis_size("orbit")
    assert count % 2 == 0
    outer = [(i, (i + 2 * (i % 2) - 1) % count) for i in range(count)]
    inner = [(i, i ^ 1) for i in range(count)]
    return lax.ppermute(across, "orbit", outer), lax.ppermute(within, "orbit", inner)


def local(
    solution, residual, direction, jacobian, crossing, tile_count, sightline_weight,
    length_class, smooth_weight,
):
    cols, species, probes, width = direction.shape
    assert REACH <= cols
    rim = cols // 2
    slots = crossing.shape[0]
    f32, bf16 = jnp.float32, jnp.bfloat16
    shape = jax.ShapeDtypeStruct
    column = (species, probes, width)
    elements = direction.size
    dot_flops = 2 * jacobian.size * probes
    near = shape((rim,) + column, bf16)
    whole = shape(direction.shape, f32)
    small = shape((probes, width), f32)

    across, within = call(
        rounding_kernel, (near, near), [VMEM()], 2 * elements, 6 * elements
    )(direction)
    from_across, from_within = swapped(across, within)

    begun, faced, norm, curved, rows, jac = call(
        inner_kernel,
        (
            shape((2 * cols,) + column, f32), shape((2, rim) + column, f32), small, small,
            shape(sightline_weight.shape, f32), shape(jacobian.shape, bf16),
        ),
        [VMEM(), SMEM()] + [HBM()] * 5,
        60 * elements,
        4 * jacobian.size,
        [
            pltpu.VMEM(direction.shape, f32),
            pltpu.SMEM(length_class.shape, jnp.int32),
            pltpu.VMEM(smooth_weight.shape, f32),
            pltpu.VMEM(sightline_weight.shape, f32),
            pltpu.SemaphoreType.DMA((5,)),
        ],
    )(
        direction, tile_count,
        *map(in_hbm, (residual, length_class, smooth_weight, sightline_weight, jacobian)),
    )

    devices = lax.axis_size("orbit")
    peers = devices // 2
    weighted, sums = call(
        forward_kernel,
        (shape((slots, probes, width), bf16), shape((probes // 2, width), f32)),
        [SMEM()] + [VMEM()] * 9,
        dot_flops,
        2 * jacobian.size,
        [pltpu.VMEM((2 * cols * species, probes, width), bf16)],
    )(crossing, rows, across, within, from_across, from_within, faced, norm, curved, jac)
    assert devices % 4 == 0
    twin = lax.ppermute(sums, "orbit", [(i, i ^ 2) for i in range(devices)])

    image, across, within = call(
        backward_kernel,
        (whole, near, near),
        [SMEM()] * 2 + [VMEM()] * 6,
        dot_flops,
        2 * jacobian.size,
        [
            pltpu.VMEM((2 * cols * species, probes, width), f32),
            pltpu.VMEM((2, rim) + column, f32),
        ],
    )(crossing, length_class, smooth_weight, weighted, jac, begun, from_across, from_within)
    across, within, twin = lax.optimization_barrier((across, within, twin))
    from_across, from_within = swapped(across, within)
    alike = [[i for i in range(devices) if i & 2 == side] for side in (0, 2)]
    sums = jnp.broadcast_to((sums + twin)[None], (peers,) + sums.shape)
    sums = lax.all_to_all(sums, "orbit", 0, 0, axis_index_groups=alike)

    solution_next, residual_next, step_length = call(
        final_kernel,
        (whole, whole, shape((1, probes), f32)),
        [VMEM()] * 7,
        8 * elements,
        28 * elements,
        [pltpu.VMEM((2,) + direction.shape, f32), pltpu.SemaphoreType.DMA((2, cols))],
        [HBM()] * 2 + [VMEM()],
    )(solution, residual, direction, image, from_across, from_within, sums)
    return solution_next, residual_next, step_length.reshape(probes)


def solution(mesh):
    wide = P(("grp", "orbit"), None, None, None)
    placed = (
        wide, wide, wide, wide,
        P(("grp", "orbit"), None),
        P(("grp", "orbit")),
        P(("grp", "orbit"), None),
        P("grp"),
        P(),
    )
    return jax.shard_map(
        local, mesh=mesh, in_specs=placed, out_specs=(wide, wide, P("grp")), check_vma=False
    )
```

```python
import functools

import jax
import jax.numpy as jnp
from jax import lax
from jax.experimental import pallas as pl
from jax.experimental.pallas import tpu as pltpu
from jax.sharding import PartitionSpec as P

LEVELS = 120
CLASSES = 4
REACH = 8
EPSILON = 1e-06
VMEM_LIMIT = 24 * 1024 * 1024

SMEM = functools.partial(pl.BlockSpec, memory_space=pltpu.SMEM)
VMEM = functools.partial(pl.BlockSpec, memory_space=pltpu.VMEM)
HBM = functools.partial(pl.BlockSpec, memory_space=pltpu.HBM)


def in_hbm(array):
    return pltpu.with_memory_space_constraint(array, pltpu.HBM)


def live_lanes(shape):
    return lax.broadcasted_iota(jnp.int32, shape, len(shape) - 1) < LEVELS


def masked(values):
    return jnp.where(live_lanes(values.shape), values, 0.0)


def call(kernel, out_shape, in_specs, flops, moved, scratch=(), out_specs=None):
    return pl.pallas_call(
        kernel,
        out_shape=out_shape,
        in_specs=in_specs,
        out_specs=tuple(out_specs or [VMEM()] * len(out_shape)),
        scratch_shapes=list(scratch),
        compiler_params=pltpu.CompilerParams(vmem_limit_bytes=VMEM_LIMIT),
        cost_estimate=pl.CostEstimate(flops=flops, bytes_accessed=moved, transcendentals=0),
    )


def parity():
    return lax.rem(lax.axis_index("orbit"), 2)


def rounding_kernel(direction, across, within):
    rim = across.shape[0]
    odd = parity()
    for c in range(rim):
        across[c] = masked(direction[odd * rim + c]).astype(jnp.bfloat16)
        within[c] = masked(direction[(1 - odd) * rim + c]).astype(jnp.bfloat16)


def coupling(classes, cols, columns):
    total = classes.shape[0]
    first = lax.axis_index("orbit") * cols
    table = {}
    for c in columns:
        length = (classes[lax.rem(first + c + total, total)] + 1) * REACH // CLASSES
        for k in range(1, REACH + 1):
            table[c, k] = jnp.where(k <= length, jnp.float32(1.0 / (k * k)), jnp.float32(0.0))
    return table


def pull(table, to, values):
    result = None
    for c, value in values.items():
        if c != to and abs(c - to) <= REACH:
            term = table[min(c, to), abs(c - to)] * value
            result = term if result is None else result + term
    return 0.0 if result is None else -result


def inner_kernel(
    direction, count, residual_hbm, classes_hbm, smooth_hbm, sight_hbm, crossing_hbm, jac_hbm,
    begun, faced, norm, curved, rows, jac, crossing, classes, residual, smooth, sight, sems,
):
    pairs = (
        (classes_hbm, classes), (smooth_hbm, smooth), (sight_hbm, sight),
        (residual_hbm, residual), (crossing_hbm, crossing), (jac_hbm, jac),
    )
    copies = [pltpu.make_async_copy(*pair, sems.at[i]) for i, pair in enumerate(pairs)]
    for copy in copies:
        copy.start()
    copies[0].wait()
    copies[1].wait()
    cols = direction.shape[0]
    rim = cols // 2
    table = coupling(classes, cols, range(-REACH, cols))
    weight = smooth[...][:, None, :]
    total = jnp.zeros(norm.shape, jnp.float32)
    values = {c: masked(direction[c]) for c in range(cols)}
    rests = {c: v - v.astype(jnp.bfloat16).astype(jnp.float32) for c, v in values.items()}
    for c in range(cols):
        centre = jnp.float32(1.0)
        for k in range(1, REACH + 1):
            centre = centre + (table[c, k] + table[c - k, k])
        result = weight * (centre * values[c] + pull(table, c, values))
        begun[rim + c] = result
        total = total + jnp.sum(values[c] * result, axis=0)
    low = {c: values[c] for c in range(rim)}
    high = {c: values[c] for c in range(rim, cols)}
    low_rests = {c: rests[c] for c in range(rim)}
    high_rests = {c: rests[c] for c in range(rim, cols)}
    for q in range(rim):
        facing = weight * pull(table, q - rim, high)
        faced[0, q] = facing
        begun[q] = facing + weight * pull(table, q - rim, low_rests)
        facing = weight * pull(table, q + cols, low)
        faced[1, q] = facing + weight * pull(table, q + cols, high)
        begun[rim + cols + q] = facing + weight * pull(table, q + cols, high_rests)
    curved[...] = total
    copies[2].wait()
    slot = lax.broadcasted_iota(jnp.int32, rows.shape, 0)
    rows[...] = jnp.where(slot < count[0], sight[...], 0.0)
    copies[3].wait()
    squares = jnp.zeros(norm.shape, jnp.float32)
    for c in range(cols):
        mres = masked(residual[c])
        squares = squares + jnp.sum(mres * mres, axis=0)
    norm[...] = squares
    copies[4].wait()
    copies[5].wait()


def forward_kernel(
    crossing, rows, across, within, from_across, from_within, faced, norm, curved, jac,
    weighted, sums, window,
):
    slots, crossings = crossing.shape
    rim, species = across.shape[:2]
    span = rim * species
    odd = parity()
    places = (1 + odd, across), (2 - odd, within), (3 * odd, from_across), (3 - 3 * odd, from_within)
    for place, part in places:
        window[pl.ds(place * span, span)] = part[...].reshape(span, *part.shape[2:])
    total = curved[...]
    for q in range(rim):
        for side, part in (odd, from_across), (1 - odd, from_within):
            total = total + 2.0 * jnp.sum(faced[side, q] * part[q].astype(jnp.float32), axis=0)
    for i in range(slots):
        picked = jnp.concatenate([window[crossing[i, j]] for j in range(crossings)], axis=1)
        tiles = jnp.concatenate([jac[i, j] for j in range(crossings)], axis=1)
        integrals = lax.dot_general(
            tiles, picked, (((1,), (1,)), ((), ())), preferred_element_type=jnp.float32
        )
        integrals = jnp.transpose(integrals)
        product = (rows[pl.ds(i, 1), :] * integrals).astype(jnp.bfloat16)
        weighted[i] = product
        total = total + product.astype(jnp.float32) * integrals
    half = sums.shape[0]
    parts = [jnp.sum(x, axis=1, keepdims=True) for x in (norm[...], total)]
    parts = [part[h * half : (h + 1) * half] for h in range(2) for part in parts]
    lane = lax.broadcasted_iota(jnp.int32, sums.shape, 1)
    block = jnp.zeros(sums.shape, jnp.float32)
    for k, part in enumerate(parts):
        block = jnp.where(lane == k, part, block)
    sums[...] = block


def backward_kernel(
    crossing, classes, smooth, weighted, jac, begun, from_across, from_within,
    image, across, within, sums, near,
):
    slots, crossings = crossing.shape
    cols, species, probes, tile = image.shape
    rim = across.shape[0]
    span = rim * species
    odd = parity()
    near[odd] = from_across[...].astype(jnp.float32)
    near[1 - odd] = from_within[...].astype(jnp.float32)
    table = coupling(classes, cols, range(-rim, cols))
    weight = smooth[...][:, None, :]
    beside = {q - rim: near[0, q] for q in range(rim)} | {q + cols: near[1, q] for q in range(rim)}
    for c in range(cols):
        place = pl.ds(span + c * species, species)
        sums[place] = begun[rim + c] + weight * pull(table, c, beside)
    sums[pl.ds(0, span)] = begun[pl.ds(0, rim)].reshape(span, probes, tile)
    sums[pl.ds(3 * span, span)] = begun[pl.ds(rim + cols, rim)].reshape(span, probes, tile)
    for i in range(slots):
        tiles = jnp.concatenate([jac[i, j] for j in range(crossings)], axis=1)
        terms = jnp.dot(weighted[i], tiles, preferred_element_type=jnp.float32)
        for j in range(crossings):
            sums[crossing[i, j]] += terms[:, j * tile : (j + 1) * tile]
    for part, place in (across, 3 * odd), (within, 3 - 3 * odd):
        part[...] = sums[pl.ds(place * span, span)].astype(part.dtype).reshape(part.shape)
    image[...] = sums[pl.ds(span, 2 * span)].reshape(image.shape)


def final_kernel(
    solution, residual, direction, image, from_across, from_within, sums,
    solution_next, residual_next, step_length,
):
    whole = jnp.sum(sums[...], axis=0)
    norm = jnp.concatenate([whole[:, 0:1], whole[:, 2:3]], axis=0)
    curvature = jnp.concatenate([whole[:, 1:2], whole[:, 3:4]], axis=0)
    step = norm / (curvature + EPSILON)
    rim = from_across.shape[0]
    wide = jnp.broadcast_to(step, direction.shape[2:])
    step_length[...] = jnp.transpose(wide)[0:1]
    wide = wide[None]
    odd = parity()
    for q in range(rim):
        for c, part in (odd * rim + q, from_across), ((1 - odd) * rim + q, from_within):
            total = masked(image[c] + part[q].astype(jnp.float32))
            solution_next[c] = masked(solution[c] + wide * direction[c])
            residual_next[c] = masked(residual[c]) - wide * total


def swapped(across, within):
    count = lax.axis_size("orbit")
    assert count % 2 == 0
    outer = [(i, (i + 2 * (i % 2) - 1) % count) for i in range(count)]
    inner = [(i, i ^ 1) for i in range(count)]
    return lax.ppermute(across, "orbit", outer), lax.ppermute(within, "orbit", inner)


def local(
    solution, residual, direction, jacobian, crossing, tile_count, sightline_weight,
    length_class, smooth_weight,
):
    cols, species, probes, width = direction.shape
    assert REACH <= cols
    rim = cols // 2
    slots = crossing.shape[0]
    f32, bf16 = jnp.float32, jnp.bfloat16
    shape = jax.ShapeDtypeStruct
    column = (species, probes, width)
    elements = direction.size
    dot_flops = 2 * jacobian.size * probes
    near = shape((rim,) + column, bf16)
    whole = shape(direction.shape, f32)
    small = shape((probes, width), f32)

    across, within = call(
        rounding_kernel, (near, near), [VMEM()], 2 * elements, 6 * elements
    )(direction)
    from_across, from_within = swapped(across, within)

    begun, faced, norm, curved, rows, jac, crossing, length_class = call(
        inner_kernel,
        (
            shape((2 * cols,) + column, f32), shape((2, rim) + column, f32), small, small,
            shape(sightline_weight.shape, f32), shape(jacobian.shape, bf16),
            pltpu.SMEM(crossing.shape, jnp.int32), pltpu.SMEM(length_class.shape, jnp.int32),
        ),
        [VMEM(), SMEM()] + [HBM()] * 6,
        60 * elements,
        4 * jacobian.size,
        [
            pltpu.VMEM(direction.shape, f32),
            pltpu.VMEM(smooth_weight.shape, f32),
            pltpu.VMEM(sightline_weight.shape, f32),
            pltpu.SemaphoreType.DMA((6,)),
        ],
        [VMEM()] * 6 + [SMEM()] * 2,
    )(
        direction, tile_count,
        *map(in_hbm, (
            residual, length_class, smooth_weight, sightline_weight, crossing, jacobian,
        )),
    )

    devices = lax.axis_size("orbit")
    peers = devices // 2
    weighted, sums = call(
        forward_kernel,
        (shape((slots, probes, width), bf16), shape((probes // 2, width), f32)),
        [SMEM()] + [VMEM()] * 9,
        dot_flops,
        2 * jacobian.size,
        [pltpu.VMEM((2 * cols * species, probes, width), bf16)],
    )(crossing, rows, across, within, from_across, from_within, faced, norm, curved, jac)
    assert devices % 4 == 0
    twin = lax.ppermute(sums, "orbit", [(i, i ^ 2) for i in range(devices)])

    image, across, within = call(
        backward_kernel,
        (whole, near, near),
        [SMEM()] * 2 + [VMEM()] * 6,
        dot_flops,
        2 * jacobian.size,
        [
            pltpu.VMEM((2 * cols * species, probes, width), f32),
            pltpu.VMEM((2, rim) + column, f32),
        ],
    )(crossing, length_class, smooth_weight, weighted, jac, begun, from_across, from_within)
    within, twin = lax.optimization_barrier((within, twin))
    from_across, from_within = swapped(across, within)
    alike = [[i for i in range(devices) if i & 2 == side] for side in (0, 2)]
    sums = jnp.broadcast_to((sums + twin)[None], (peers,) + sums.shape)
    sums = lax.all_to_all(sums, "orbit", 0, 0, axis_index_groups=alike)

    solution_next, residual_next, step_length = call(
        final_kernel,
        (whole, whole, shape((1, probes), f32)),
        [VMEM()] * 7,
        8 * elements,
        28 * elements,
    )(solution, residual, direction, image, from_across, from_within, sums)
    return solution_next, residual_next, step_length.reshape(probes)


def solution(mesh):
    wide = P(("grp", "orbit"), None, None, None)
    placed = (
        wide, wide, wide, wide,
        P(("grp", "orbit"), None),
        P(("grp", "orbit")),
        P(("grp", "orbit"), None),
        P("grp"),
        P(),
    )
    return jax.shard_map(
        local, mesh=mesh, in_specs=placed, out_specs=(wide, wide, P("grp")), check_vma=False
    )
```

```python
import functools

import jax
import jax.numpy as jnp
from jax import lax
from jax.experimental import pallas as pl
from jax.experimental.pallas import tpu as pltpu
from jax.sharding import PartitionSpec as P

LEVELS = 120
CLASSES = 4
REACH = 8
EPSILON = 1e-06
VMEM_LIMIT = 24 * 1024 * 1024

SMEM = functools.partial(pl.BlockSpec, memory_space=pltpu.SMEM)
VMEM = functools.partial(pl.BlockSpec, memory_space=pltpu.VMEM)
HBM = functools.partial(pl.BlockSpec, memory_space=pltpu.HBM)


def in_hbm(array):
    return pltpu.with_memory_space_constraint(array, pltpu.HBM)


def live_lanes(shape):
    return lax.broadcasted_iota(jnp.int32, shape, len(shape) - 1) < LEVELS


def masked(values):
    return jnp.where(live_lanes(values.shape), values, 0.0)


def call(kernel, out_shape, in_specs, flops, moved, scratch=(), out_specs=None):
    return pl.pallas_call(
        kernel,
        out_shape=out_shape,
        in_specs=in_specs,
        out_specs=tuple(out_specs or [VMEM()] * len(out_shape)),
        scratch_shapes=list(scratch),
        compiler_params=pltpu.CompilerParams(vmem_limit_bytes=VMEM_LIMIT),
        cost_estimate=pl.CostEstimate(flops=flops, bytes_accessed=moved, transcendentals=0),
    )


def parity():
    return lax.rem(lax.axis_index("orbit"), 2)


def rounding_kernel(direction, across, within):
    rim = across.shape[0]
    odd = parity()
    for c in range(rim):
        across[c] = masked(direction[odd * rim + c]).astype(jnp.bfloat16)
        within[c] = masked(direction[(1 - odd) * rim + c]).astype(jnp.bfloat16)


def coupling(classes, cols, columns):
    total = classes.shape[0]
    first = lax.axis_index("orbit") * cols
    table = {}
    for c in columns:
        length = (classes[lax.rem(first + c + total, total)] + 1) * REACH // CLASSES
        for k in range(1, REACH + 1):
            table[c, k] = jnp.where(k <= length, jnp.float32(1.0 / (k * k)), jnp.float32(0.0))
    return table


def pull(table, to, values):
    result = None
    for c, value in values.items():
        if c != to and abs(c - to) <= REACH:
            term = table[min(c, to), abs(c - to)] * value
            result = term if result is None else result + term
    return 0.0 if result is None else -result


def inner_kernel(
    direction, count, residual_hbm, classes_hbm, smooth_hbm, sight_hbm, crossing_hbm, jac_hbm,
    begun, faced, norm, curved, rows, jac, crossing, classes, residual, smooth, sight, sems,
):
    pairs = (
        (classes_hbm, classes), (smooth_hbm, smooth), (sight_hbm, sight),
        (residual_hbm, residual), (crossing_hbm, crossing), (jac_hbm, jac),
    )
    copies = [pltpu.make_async_copy(*pair, sems.at[i]) for i, pair in enumerate(pairs)]
    for copy in copies:
        copy.start()
    copies[0].wait()
    copies[1].wait()
    cols = direction.shape[0]
    rim = cols // 2
    table = coupling(classes, cols, range(-REACH, cols))
    weight = smooth[...][:, None, :]
    total = jnp.zeros(norm.shape, jnp.float32)
    values = {c: masked(direction[c]) for c in range(cols)}
    rests = {c: v - v.astype(jnp.bfloat16).astype(jnp.float32) for c, v in values.items()}
    for c in range(cols):
        centre = jnp.float32(1.0)
        for k in range(1, REACH + 1):
            centre = centre + (table[c, k] + table[c - k, k])
        result = weight * (centre * values[c] + pull(table, c, values))
        begun[rim + c] = result
        total = total + jnp.sum(values[c] * result, axis=0)
    low = {c: values[c] for c in range(rim)}
    high = {c: values[c] for c in range(rim, cols)}
    low_rests = {c: rests[c] for c in range(rim)}
    high_rests = {c: rests[c] for c in range(rim, cols)}
    for q in range(rim):
        facing = weight * pull(table, q - rim, high)
        faced[0, q] = facing
        begun[q] = facing + weight * pull(table, q - rim, low_rests)
        facing = weight * pull(table, q + cols, low)
        faced[1, q] = facing + weight * pull(table, q + cols, high)
        begun[rim + cols + q] = facing + weight * pull(table, q + cols, high_rests)
    curved[...] = total
    copies[2].wait()
    slot = lax.broadcasted_iota(jnp.int32, rows.shape, 0)
    rows[...] = jnp.where(slot < count[0], sight[...], 0.0)
    copies[3].wait()
    squares = jnp.zeros(norm.shape, jnp.float32)
    for c in range(cols):
        mres = masked(residual[c])
        squares = squares + jnp.sum(mres * mres, axis=0)
    norm[...] = squares
    copies[4].wait()
    copies[5].wait()


def forward_kernel(
    crossing, rows, across, within, from_across, from_within, faced, norm, curved, jac,
    weighted, sums, window,
):
    slots, crossings = crossing.shape
    rim, species = across.shape[:2]
    span = rim * species
    odd = parity()
    places = (1 + odd, across), (2 - odd, within), (3 * odd, from_across), (3 - 3 * odd, from_within)
    for place, part in places:
        window[pl.ds(place * span, span)] = part[...].reshape(span, *part.shape[2:])
    total = curved[...]
    for q in range(rim):
        for side, part in (odd, from_across), (1 - odd, from_within):
            total = total + 2.0 * jnp.sum(faced[side, q] * part[q].astype(jnp.float32), axis=0)
    for i in range(slots):
        picked = jnp.concatenate([window[crossing[i, j]] for j in range(crossings)], axis=1)
        tiles = jnp.concatenate([jac[i, j] for j in range(crossings)], axis=1)
        integrals = lax.dot_general(
            tiles, picked, (((1,), (1,)), ((), ())), preferred_element_type=jnp.float32
        )
        integrals = jnp.transpose(integrals)
        product = (rows[pl.ds(i, 1), :] * integrals).astype(jnp.bfloat16)
        weighted[i] = product
        total = total + product.astype(jnp.float32) * integrals
    half = sums.shape[0]
    parts = [jnp.sum(x, axis=1, keepdims=True) for x in (norm[...], total)]
    parts = [part[h * half : (h + 1) * half] for h in range(2) for part in parts]
    lane = lax.broadcasted_iota(jnp.int32, sums.shape, 1)
    block = jnp.zeros(sums.shape, jnp.float32)
    for k, part in enumerate(parts):
        block = jnp.where(lane == k, part, block)
    sums[...] = block


def backward_kernel(
    crossing, classes, smooth, weighted, jac, begun, from_across, from_within,
    image, across, within, sums, near,
):
    slots, crossings = crossing.shape
    cols, species, probes, tile = image.shape
    rim = across.shape[0]
    span = rim * species
    odd = parity()
    near[odd] = from_across[...].astype(jnp.float32)
    near[1 - odd] = from_within[...].astype(jnp.float32)
    table = coupling(classes, cols, range(-rim, cols))
    weight = smooth[...][:, None, :]
    beside = {q - rim: near[0, q] for q in range(rim)} | {q + cols: near[1, q] for q in range(rim)}
    for c in range(cols):
        place = pl.ds(span + c * species, species)
        sums[place] = begun[rim + c] + weight * pull(table, c, beside)
    sums[pl.ds(0, span)] = begun[pl.ds(0, rim)].reshape(span, probes, tile)
    sums[pl.ds(3 * span, span)] = begun[pl.ds(rim + cols, rim)].reshape(span, probes, tile)
    for i in range(slots):
        tiles = jnp.concatenate([jac[i, j] for j in range(crossings)], axis=1)
        terms = jnp.dot(weighted[i], tiles, preferred_element_type=jnp.float32)
        for j in range(crossings):
            sums[crossing[i, j]] += terms[:, j * tile : (j + 1) * tile]
    for part, place in (across, 3 * odd), (within, 3 - 3 * odd):
        part[...] = sums[pl.ds(place * span, span)].astype(part.dtype).reshape(part.shape)
    image[...] = sums[pl.ds(span, 2 * span)].reshape(image.shape)


def final_kernel(
    solution, residual, direction, image, from_across, from_within, *rest
):
    *held, solution_next, residual_next, step_length = rest
    whole = tree_sum([part[...] for part in held])
    norm = jnp.concatenate([whole[:, 0:1], whole[:, 2:3]], axis=0)
    curvature = jnp.concatenate([whole[:, 1:2], whole[:, 3:4]], axis=0)
    step = norm / (curvature + EPSILON)
    rim = from_across.shape[0]
    wide = jnp.broadcast_to(step, direction.shape[2:])
    step_length[...] = jnp.transpose(wide)[0:1]
    wide = wide[None]
    odd = parity()
    for q in range(rim):
        for c, part in (odd * rim + q, from_across), ((1 - odd) * rim + q, from_within):
            total = masked(image[c] + part[q].astype(jnp.float32))
            solution_next[c] = masked(solution[c] + wide * direction[c])
            residual_next[c] = masked(residual[c]) - wide * total


def swapped(across, within):
    count = lax.axis_size("orbit")
    assert count % 2 == 0
    outer = [(i, (i + 2 * (i % 2) - 1) % count) for i in range(count)]
    inner = [(i, i ^ 1) for i in range(count)]
    return lax.ppermute(across, "orbit", outer), lax.ppermute(within, "orbit", inner)


def sum_steps(devices):
    assert devices & (devices - 1) == 0
    bits = [1 << b for b in range(devices.bit_length() - 1)]
    return [bits[k : k + 2] for k in range(0, len(bits), 2)]


def partners(array, bits):
    devices = range(lax.axis_size("orbit"))
    masks = [sum(bit for k, bit in enumerate(bits) if m >> k & 1) for m in range(1, 1 << len(bits))]
    found = {
        mask: lax.ppermute(array, "orbit", [(i, i ^ mask) for i in devices]) for mask in masks[::-1]
    }
    return [found[mask] for mask in masks]


def tree_sum(parts):
    while len(parts) > 1:
        parts = [parts[k] + parts[k + 1] for k in range(0, len(parts), 2)]
    return parts[0]


def local(
    solution, residual, direction, jacobian, crossing, tile_count, sightline_weight,
    length_class, smooth_weight,
):
    cols, species, probes, width = direction.shape
    assert REACH <= cols
    rim = cols // 2
    slots = crossing.shape[0]
    f32, bf16 = jnp.float32, jnp.bfloat16
    shape = jax.ShapeDtypeStruct
    column = (species, probes, width)
    elements = direction.size
    dot_flops = 2 * jacobian.size * probes
    near = shape((rim,) + column, bf16)
    whole = shape(direction.shape, f32)
    small = shape((probes, width), f32)

    across, within = call(
        rounding_kernel, (near, near), [VMEM()], 2 * elements, 6 * elements
    )(direction)
    from_across, from_within = swapped(across, within)

    begun, faced, norm, curved, rows, jac, crossing, length_class = call(
        inner_kernel,
        (
            shape((2 * cols,) + column, f32), shape((2, rim) + column, f32), small, small,
            shape(sightline_weight.shape, f32), shape(jacobian.shape, bf16),
            pltpu.SMEM(crossing.shape, jnp.int32), pltpu.SMEM(length_class.shape, jnp.int32),
        ),
        [VMEM(), SMEM()] + [HBM()] * 6,
        60 * elements,
        4 * jacobian.size,
        [
            pltpu.VMEM(direction.shape, f32),
            pltpu.VMEM(smooth_weight.shape, f32),
            pltpu.VMEM(sightline_weight.shape, f32),
            pltpu.SemaphoreType.DMA((6,)),
        ],
        [VMEM()] * 6 + [SMEM()] * 2,
    )(
        direction, tile_count,
        *map(in_hbm, (
            residual, length_class, smooth_weight, sightline_weight, crossing, jacobian,
        )),
    )

    devices = lax.axis_size("orbit")
    peers = devices // 2
    weighted, sums = call(
        forward_kernel,
        (shape((slots, probes, width), bf16), shape((probes // 2, width), f32)),
        [SMEM()] + [VMEM()] * 9,
        dot_flops,
        2 * jacobian.size,
        [pltpu.VMEM((2 * cols * species, probes, width), bf16)],
    )(crossing, rows, across, within, from_across, from_within, faced, norm, curved, jac)
    steps = sum_steps(devices)
    held = [sums] + partners(sums, steps[0])

    image, across, within = call(
        backward_kernel,
        (whole, near, near),
        [SMEM()] * 2 + [VMEM()] * 6,
        dot_flops,
        2 * jacobian.size,
        [
            pltpu.VMEM((2 * cols * species, probes, width), f32),
            pltpu.VMEM((2, rim) + column, f32),
        ],
    )(crossing, length_class, smooth_weight, weighted, jac, begun, from_across, from_within)
    within, *held = lax.optimization_barrier((within, *held))
    from_across, from_within = swapped(across, within)
    for step in steps[1:]:
        sums = tree_sum(held)
        held = [sums] + partners(sums, step)

    solution_next, residual_next, step_length = call(
        final_kernel,
        (whole, whole, shape((1, probes), f32)),
        [VMEM()] * (6 + len(held)),
        8 * elements,
        28 * elements,
    )(solution, residual, direction, image, from_across, from_within, *held)
    return solution_next, residual_next, step_length.reshape(probes)


def solution(mesh):
    wide = P(("grp", "orbit"), None, None, None)
    placed = (
        wide, wide, wide, wide,
        P(("grp", "orbit"), None),
        P(("grp", "orbit")),
        P(("grp", "orbit"), None),
        P("grp"),
        P(),
    )
    return jax.shard_map(
        local, mesh=mesh, in_specs=placed, out_specs=(wide, wide, P("grp")), check_vma=False
    )
```

```python
import functools

import jax
import jax.numpy as jnp
from jax import lax
from jax.experimental import pallas as pl
from jax.experimental.pallas import tpu as pltpu
from jax.sharding import PartitionSpec as P

LEVELS = 120
CLASSES = 4
REACH = 8
EPSILON = 1e-06
VMEM_LIMIT = 24 * 1024 * 1024

SMEM = functools.partial(pl.BlockSpec, memory_space=pltpu.SMEM)
VMEM = functools.partial(pl.BlockSpec, memory_space=pltpu.VMEM)
HBM = functools.partial(pl.BlockSpec, memory_space=pltpu.HBM)


def in_hbm(array):
    return pltpu.with_memory_space_constraint(array, pltpu.HBM)


def live_lanes(shape):
    return lax.broadcasted_iota(jnp.int32, shape, len(shape) - 1) < LEVELS


def masked(values):
    return jnp.where(live_lanes(values.shape), values, 0.0)


def call(kernel, out_shape, in_specs, flops, moved, scratch=(), out_specs=None):
    return pl.pallas_call(
        kernel,
        out_shape=out_shape,
        in_specs=in_specs,
        out_specs=tuple(out_specs or [VMEM()] * len(out_shape)),
        scratch_shapes=list(scratch),
        compiler_params=pltpu.CompilerParams(vmem_limit_bytes=VMEM_LIMIT),
        cost_estimate=pl.CostEstimate(flops=flops, bytes_accessed=moved, transcendentals=0),
    )


def parity():
    return lax.rem(lax.axis_index("orbit"), 2)


def rounding_kernel(direction_hbm, direction, across, within, sems):
    rim = across.shape[0]
    odd = parity()
    halves = ((odd, across), (1 - odd, within))
    copies = []
    for k, (place, _) in enumerate(halves):
        half = pl.ds(place * rim, rim)
        copies.append(
            pltpu.make_async_copy(direction_hbm.at[half], direction.at[half], sems.at[k])
        )
        copies[-1].start()
    for copy, (place, half) in zip(copies, halves):
        copy.wait()
        for c in range(rim):
            half[c] = masked(direction[place * rim + c]).astype(jnp.bfloat16)


def coupling(classes, cols, columns):
    total = classes.shape[0]
    first = lax.axis_index("orbit") * cols
    table = {}
    for c in columns:
        length = (classes[lax.rem(first + c + total, total)] + 1) * REACH // CLASSES
        for k in range(1, REACH + 1):
            table[c, k] = jnp.where(k <= length, jnp.float32(1.0 / (k * k)), jnp.float32(0.0))
    return table


def pull(table, to, values):
    result = None
    for c, value in values.items():
        if c != to and abs(c - to) <= REACH:
            term = table[min(c, to), abs(c - to)] * value
            result = term if result is None else result + term
    return 0.0 if result is None else -result


def inner_kernel(
    direction, count, residual_hbm, classes_hbm, smooth_hbm, sight_hbm, crossing_hbm, jac_hbm,
    begun, faced, norm, curved, rows, jac, crossing, classes, residual, smooth, sight, sems,
):
    pairs = (
        (classes_hbm, classes), (smooth_hbm, smooth), (sight_hbm, sight),
        (residual_hbm, residual), (crossing_hbm, crossing), (jac_hbm, jac),
    )
    copies = [pltpu.make_async_copy(*pair, sems.at[i]) for i, pair in enumerate(pairs)]
    for copy in copies:
        copy.start()
    copies[0].wait()
    copies[1].wait()
    cols = direction.shape[0]
    rim = cols // 2
    table = coupling(classes, cols, range(-REACH, cols))
    weight = smooth[...][:, None, :]
    total = jnp.zeros(norm.shape, jnp.float32)
    values = {c: masked(direction[c]) for c in range(cols)}
    rests = {c: v - v.astype(jnp.bfloat16).astype(jnp.float32) for c, v in values.items()}
    for c in range(cols):
        centre = jnp.float32(1.0)
        for k in range(1, REACH + 1):
            centre = centre + (table[c, k] + table[c - k, k])
        result = weight * (centre * values[c] + pull(table, c, values))
        begun[rim + c] = result
        total = total + jnp.sum(values[c] * result, axis=0)
    low = {c: values[c] for c in range(rim)}
    high = {c: values[c] for c in range(rim, cols)}
    low_rests = {c: rests[c] for c in range(rim)}
    high_rests = {c: rests[c] for c in range(rim, cols)}
    for q in range(rim):
        facing = weight * pull(table, q - rim, high)
        faced[0, q] = facing
        begun[q] = facing + weight * pull(table, q - rim, low_rests)
        facing = weight * pull(table, q + cols, low)
        faced[1, q] = facing + weight * pull(table, q + cols, high)
        begun[rim + cols + q] = facing + weight * pull(table, q + cols, high_rests)
    curved[...] = total
    copies[2].wait()
    slot = lax.broadcasted_iota(jnp.int32, rows.shape, 0)
    rows[...] = jnp.where(slot < count[0], sight[...], 0.0)
    copies[3].wait()
    squares = jnp.zeros(norm.shape, jnp.float32)
    for c in range(cols):
        mres = masked(residual[c])
        squares = squares + jnp.sum(mres * mres, axis=0)
    norm[...] = squares
    copies[4].wait()
    copies[5].wait()


def forward_kernel(
    crossing, rows, across, within, from_across, from_within, faced, norm, curved, jac,
    weighted, sums, window,
):
    slots, crossings = crossing.shape
    rim, species = across.shape[:2]
    span = rim * species
    odd = parity()
    places = (1 + odd, across), (2 - odd, within), (3 * odd, from_across), (3 - 3 * odd, from_within)
    for place, part in places:
        window[pl.ds(place * span, span)] = part[...].reshape(span, *part.shape[2:])
    total = curved[...]
    for q in range(rim):
        for side, part in (odd, from_across), (1 - odd, from_within):
            total = total + 2.0 * jnp.sum(faced[side, q] * part[q].astype(jnp.float32), axis=0)
    for i in range(slots):
        picked = jnp.concatenate([window[crossing[i, j]] for j in range(crossings)], axis=1)
        tiles = jnp.concatenate([jac[i, j] for j in range(crossings)], axis=1)
        integrals = lax.dot_general(
            picked, tiles, (((1,), (1,)), ((), ())), preferred_element_type=jnp.float32
        )
        product = (rows[pl.ds(i, 1), :] * integrals).astype(jnp.bfloat16)
        weighted[i] = product
        total = total + product.astype(jnp.float32) * integrals
    half = sums.shape[0]
    parts = [jnp.sum(x, axis=1, keepdims=True) for x in (norm[...], total)]
    parts = [part[h * half : (h + 1) * half] for h in range(2) for part in parts]
    lane = lax.broadcasted_iota(jnp.int32, sums.shape, 1)
    block = jnp.zeros(sums.shape, jnp.float32)
    for k, part in enumerate(parts):
        block = jnp.where(lane == k, part, block)
    sums[...] = block


def backward_kernel(
    crossing, classes, smooth, weighted, jac, begun, from_across, from_within,
    image, across, within, sums, near,
):
    slots, crossings = crossing.shape
    cols, species, probes, tile = image.shape
    rim = across.shape[0]
    span = rim * species
    odd = parity()
    near[odd] = from_across[...].astype(jnp.float32)
    near[1 - odd] = from_within[...].astype(jnp.float32)
    table = coupling(classes, cols, range(-rim, cols))
    weight = smooth[...][:, None, :]
    beside = {q - rim: near[0, q] for q in range(rim)} | {q + cols: near[1, q] for q in range(rim)}
    for c in range(cols):
        place = pl.ds(span + c * species, species)
        sums[place] = begun[rim + c] + weight * pull(table, c, beside)
    sums[pl.ds(0, span)] = begun[pl.ds(0, rim)].reshape(span, probes, tile)
    sums[pl.ds(3 * span, span)] = begun[pl.ds(rim + cols, rim)].reshape(span, probes, tile)
    for i in range(slots):
        tiles = jnp.concatenate([jac[i, j] for j in range(crossings)], axis=1)
        terms = jnp.dot(weighted[i], tiles, preferred_element_type=jnp.float32)
        for j in range(crossings):
            sums[crossing[i, j]] += terms[:, j * tile : (j + 1) * tile]
    for part, place in (across, 3 * odd), (within, 3 - 3 * odd):
        part[...] = sums[pl.ds(place * span, span)].astype(part.dtype).reshape(part.shape)
    image[...] = sums[pl.ds(span, 2 * span)].reshape(image.shape)


def final_kernel(
    solution, residual, direction, image, from_across, from_within, sums,
    solution_next, residual_next, step_length,
):
    whole = jnp.sum(sums[...], axis=0)
    norm = jnp.concatenate([whole[:, 0:1], whole[:, 2:3]], axis=0)
    curvature = jnp.concatenate([whole[:, 1:2], whole[:, 3:4]], axis=0)
    step = norm / (curvature + EPSILON)
    rim = from_across.shape[0]
    wide = jnp.broadcast_to(step, direction.shape[2:])
    step_length[...] = jnp.transpose(wide)[0:1]
    wide = wide[None]
    odd = parity()
    for q in range(rim):
        for c, part in (odd * rim + q, from_across), ((1 - odd) * rim + q, from_within):
            total = masked(image[c] + part[q].astype(jnp.float32))
            solution_next[c] = masked(solution[c] + wide * direction[c])
            residual_next[c] = masked(residual[c]) - wide * total


def swapped(across, within):
    count = lax.axis_size("orbit")
    assert count % 2 == 0
    outer = [(i, (i + 2 * (i % 2) - 1) % count) for i in range(count)]
    inner = [(i, i ^ 1) for i in range(count)]
    return lax.ppermute(across, "orbit", outer), lax.ppermute(within, "orbit", inner)


def local(
    solution, residual, direction, jacobian, crossing, tile_count, sightline_weight,
    length_class, smooth_weight,
):
    cols, species, probes, width = direction.shape
    assert REACH <= cols
    rim = cols // 2
    slots = crossing.shape[0]
    f32, bf16 = jnp.float32, jnp.bfloat16
    shape = jax.ShapeDtypeStruct
    column = (species, probes, width)
    elements = direction.size
    dot_flops = 2 * jacobian.size * probes
    near = shape((rim,) + column, bf16)
    whole = shape(direction.shape, f32)
    small = shape((probes, width), f32)

    held, across, within = call(
        rounding_kernel,
        (whole, near, near),
        [HBM()],
        2 * elements,
        10 * elements,
        [pltpu.SemaphoreType.DMA((2,))],
    )(in_hbm(direction))
    from_across, from_within = swapped(across, within)

    begun, faced, norm, curved, rows, jac, crossing, length_class = call(
        inner_kernel,
        (
            shape((2 * cols,) + column, f32), shape((2, rim) + column, f32), small, small,
            shape(sightline_weight.shape, f32), shape(jacobian.shape, bf16),
            pltpu.SMEM(crossing.shape, jnp.int32), pltpu.SMEM(length_class.shape, jnp.int32),
        ),
        [VMEM(), SMEM()] + [HBM()] * 6,
        60 * elements,
        4 * jacobian.size,
        [
            pltpu.VMEM(direction.shape, f32),
            pltpu.VMEM(smooth_weight.shape, f32),
            pltpu.VMEM(sightline_weight.shape, f32),
            pltpu.SemaphoreType.DMA((6,)),
        ],
        [VMEM()] * 6 + [SMEM()] * 2,
    )(
        held, tile_count,
        *map(in_hbm, (
            residual, length_class, smooth_weight, sightline_weight, crossing, jacobian,
        )),
    )

    devices = lax.axis_size("orbit")
    peers = devices // 2
    weighted, sums = call(
        forward_kernel,
        (shape((slots, probes, width), bf16), shape((probes // 2, width), f32)),
        [SMEM()] + [VMEM()] * 9,
        dot_flops,
        2 * jacobian.size,
        [pltpu.VMEM((2 * cols * species, probes, width), bf16)],
    )(crossing, rows, across, within, from_across, from_within, faced, norm, curved, jac)
    assert devices % 4 == 0
    twin = lax.ppermute(sums, "orbit", [(i, i ^ 2) for i in range(devices)])

    image, across, within = call(
        backward_kernel,
        (whole, near, near),
        [SMEM()] * 2 + [VMEM()] * 6,
        dot_flops,
        2 * jacobian.size,
        [
            pltpu.VMEM((2 * cols * species, probes, width), f32),
            pltpu.VMEM((2, rim) + column, f32),
        ],
    )(crossing, length_class, smooth_weight, weighted, jac, begun, from_across, from_within)
    within, twin = lax.optimization_barrier((within, twin))
    from_across, from_within = swapped(across, within)
    alike = [[i for i in range(devices) if i & 2 == side] for side in (0, 2)]
    sums = jnp.broadcast_to((sums + twin)[None], (peers,) + sums.shape)
    sums = lax.all_to_all(sums, "orbit", 0, 0, axis_index_groups=alike)

    solution_next, residual_next, step_length = call(
        final_kernel,
        (whole, whole, shape((1, probes), f32)),
        [VMEM()] * 7,
        8 * elements,
        28 * elements,
    )(solution, residual, direction, image, from_across, from_within, sums)
    return solution_next, residual_next, step_length.reshape(probes)


def solution(mesh):
    wide = P(("grp", "orbit"), None, None, None)
    placed = (
        wide, wide, wide, wide,
        P(("grp", "orbit"), None),
        P(("grp", "orbit")),
        P(("grp", "orbit"), None),
        P("grp"),
        P(),
    )
    return jax.shard_map(
        local, mesh=mesh, in_specs=placed, out_specs=(wide, wide, P("grp")), check_vma=False
    )
```

```python
import functools

import jax
import jax.numpy as jnp
from jax import lax
from jax.experimental import pallas as pl
from jax.experimental.pallas import tpu as pltpu
from jax.sharding import PartitionSpec as P

LEVELS = 120
CLASSES = 4
REACH = 8
EPSILON = 1e-06
GROUP = 2
VMEM_LIMIT = 24 * 1024 * 1024

SMEM = functools.partial(pl.BlockSpec, memory_space=pltpu.SMEM)
VMEM = functools.partial(pl.BlockSpec, memory_space=pltpu.VMEM)
HBM = functools.partial(pl.BlockSpec, memory_space=pltpu.HBM)


def in_hbm(array):
    return pltpu.with_memory_space_constraint(array, pltpu.HBM)


def live_lanes(shape):
    return lax.broadcasted_iota(jnp.int32, shape, len(shape) - 1) < LEVELS


def masked(values):
    return jnp.where(live_lanes(values.shape), values, 0.0)


def call(kernel, out_shape, in_specs, flops, moved, scratch=(), out_specs=None):
    return pl.pallas_call(
        kernel,
        out_shape=out_shape,
        in_specs=in_specs,
        out_specs=tuple(out_specs or [VMEM()] * len(out_shape)),
        scratch_shapes=list(scratch),
        compiler_params=pltpu.CompilerParams(vmem_limit_bytes=VMEM_LIMIT),
        cost_estimate=pl.CostEstimate(flops=flops, bytes_accessed=moved, transcendentals=0),
    )


def parity():
    return lax.rem(lax.axis_index("orbit"), 2)


def rounding_kernel(direction_hbm, direction, across, within, sems):
    rim = across.shape[0]
    odd = parity()
    halves = ((odd, across), (1 - odd, within))
    copies = []
    for k, (place, _) in enumerate(halves):
        half = pl.ds(place * rim, rim)
        copies.append(
            pltpu.make_async_copy(direction_hbm.at[half], direction.at[half], sems.at[k])
        )
        copies[-1].start()
    for copy, (place, half) in zip(copies, halves):
        copy.wait()
        for c in range(rim):
            half[c] = masked(direction[place * rim + c]).astype(jnp.bfloat16)


def coupling(classes, cols, columns):
    total = classes.shape[0]
    first = lax.axis_index("orbit") * cols
    table = {}
    for c in columns:
        length = (classes[lax.rem(first + c + total, total)] + 1) * REACH // CLASSES
        for k in range(1, REACH + 1):
            table[c, k] = jnp.where(k <= length, jnp.float32(1.0 / (k * k)), jnp.float32(0.0))
    return table


def pull(table, to, values):
    result = None
    for c, value in values.items():
        if c != to and abs(c - to) <= REACH:
            term = table[min(c, to), abs(c - to)] * value
            result = term if result is None else result + term
    return 0.0 if result is None else -result


def slot_groups(slots):
    return [range(i, min(i + GROUP, slots)) for i in range(0, slots, GROUP)]


def if_live(count, group, work):
    if group[0] == 0:
        work()
    else:
        pl.when(group[0] < count)(work)


def inner_kernel(
    direction, count, residual_hbm, classes_hbm, smooth_hbm, sight_hbm, crossing_hbm, jac_hbm,
    begun, faced, norm, curved, rows, jac, crossing, classes, live, residual, smooth, sight, sems,
):
    pairs = (
        (classes_hbm, classes), (smooth_hbm, smooth), (sight_hbm, sight),
        (residual_hbm, residual), (crossing_hbm, crossing),
    )
    copies = [pltpu.make_async_copy(*pair, sems.at[i]) for i, pair in enumerate(pairs)]
    for copy in copies:
        copy.start()

    def load(group):
        part = pl.ds(group[0], len(group))
        return pltpu.make_async_copy(
            jac_hbm.at[part], jac.at[part], sems.at[len(pairs) + group[0] // GROUP]
        )

    for group in slot_groups(jac.shape[0]):
        if_live(count[0], group, lambda: load(group).start())
    live[0] = count[0]
    copies[0].wait()
    copies[1].wait()
    cols = direction.shape[0]
    rim = cols // 2
    table = coupling(classes, cols, range(-REACH, cols))
    weight = smooth[...][:, None, :]
    total = jnp.zeros(norm.shape, jnp.float32)
    values = {c: masked(direction[c]) for c in range(cols)}
    rests = {c: v - v.astype(jnp.bfloat16).astype(jnp.float32) for c, v in values.items()}
    for c in range(cols):
        centre = jnp.float32(1.0)
        for k in range(1, REACH + 1):
            centre = centre + (table[c, k] + table[c - k, k])
        result = weight * (centre * values[c] + pull(table, c, values))
        begun[rim + c] = result
        total = total + jnp.sum(values[c] * result, axis=0)
    low = {c: values[c] for c in range(rim)}
    high = {c: values[c] for c in range(rim, cols)}
    low_rests = {c: rests[c] for c in range(rim)}
    high_rests = {c: rests[c] for c in range(rim, cols)}
    for q in range(rim):
        facing = weight * pull(table, q - rim, high)
        faced[0, q] = facing
        begun[q] = facing + weight * pull(table, q - rim, low_rests)
        facing = weight * pull(table, q + cols, low)
        faced[1, q] = facing + weight * pull(table, q + cols, high)
        begun[rim + cols + q] = facing + weight * pull(table, q + cols, high_rests)
    curved[...] = total
    copies[2].wait()
    slot = lax.broadcasted_iota(jnp.int32, rows.shape, 0)
    rows[...] = jnp.where(slot < count[0], sight[...], 0.0)
    copies[3].wait()
    squares = jnp.zeros(norm.shape, jnp.float32)
    for c in range(cols):
        mres = masked(residual[c])
        squares = squares + jnp.sum(mres * mres, axis=0)
    norm[...] = squares
    copies[4].wait()
    for group in slot_groups(jac.shape[0]):
        if_live(count[0], group, lambda: load(group).wait())


def forward_kernel(
    crossing, live, rows, across, within, from_across, from_within, faced, norm, curved, jac,
    weighted, sums, window, total,
):
    slots, crossings = crossing.shape
    rim, species = across.shape[:2]
    span = rim * species
    odd = parity()
    places = (1 + odd, across), (2 - odd, within), (3 * odd, from_across), (3 - 3 * odd, from_within)
    for place, part in places:
        window[pl.ds(place * span, span)] = part[...].reshape(span, *part.shape[2:])
    edges = curved[...]
    for q in range(rim):
        for side, part in (odd, from_across), (1 - odd, from_within):
            edges = edges + 2.0 * jnp.sum(faced[side, q] * part[q].astype(jnp.float32), axis=0)
    total[...] = edges

    def project(group):
        added = jnp.zeros(total.shape, jnp.float32)
        for i in group:
            picked = jnp.concatenate([window[crossing[i, j]] for j in range(crossings)], axis=1)
            tiles = jnp.concatenate([jac[i, j] for j in range(crossings)], axis=1)
            integrals = lax.dot_general(
                picked, tiles, (((1,), (1,)), ((), ())), preferred_element_type=jnp.float32
            )
            product = (rows[pl.ds(i, 1), :] * integrals).astype(jnp.bfloat16)
            weighted[i] = product
            added = added + product.astype(jnp.float32) * integrals
        total[...] += added

    for group in slot_groups(slots):
        if_live(live[0], group, lambda: project(group))
    half = sums.shape[0]
    parts = [jnp.sum(x, axis=1, keepdims=True) for x in (norm[...], total[...])]
    parts = [part[h * half : (h + 1) * half] for h in range(2) for part in parts]
    lane = lax.broadcasted_iota(jnp.int32, sums.shape, 1)
    block = jnp.zeros(sums.shape, jnp.float32)
    for k, part in enumerate(parts):
        block = jnp.where(lane == k, part, block)
    sums[...] = block


def backward_kernel(
    crossing, classes, live, smooth, weighted, jac, begun, from_across, from_within,
    image, across, within, sums, near,
):
    slots, crossings = crossing.shape
    cols, species, probes, tile = image.shape
    rim = across.shape[0]
    span = rim * species
    odd = parity()
    near[odd] = from_across[...].astype(jnp.float32)
    near[1 - odd] = from_within[...].astype(jnp.float32)
    table = coupling(classes, cols, range(-rim, cols))
    weight = smooth[...][:, None, :]
    beside = {q - rim: near[0, q] for q in range(rim)} | {q + cols: near[1, q] for q in range(rim)}
    for c in range(cols):
        place = pl.ds(span + c * species, species)
        sums[place] = begun[rim + c] + weight * pull(table, c, beside)
    sums[pl.ds(0, span)] = begun[pl.ds(0, rim)].reshape(span, probes, tile)
    sums[pl.ds(3 * span, span)] = begun[pl.ds(rim + cols, rim)].reshape(span, probes, tile)

    def project(group):
        for i in group:
            tiles = jnp.concatenate([jac[i, j] for j in range(crossings)], axis=1)
            terms = jnp.dot(weighted[i], tiles, preferred_element_type=jnp.float32)
            for j in range(crossings):
                sums[crossing[i, j]] += terms[:, j * tile : (j + 1) * tile]

    for group in slot_groups(slots):
        if_live(live[0], group, lambda: project(group))
    for part, place in (across, 3 * odd), (within, 3 - 3 * odd):
        part[...] = sums[pl.ds(place * span, span)].astype(part.dtype).reshape(part.shape)
    image[...] = sums[pl.ds(span, 2 * span)].reshape(image.shape)


def final_kernel(
    solution, residual, direction, image, from_across, from_within, sums,
    solution_next, residual_next, step_length,
):
    whole = jnp.sum(sums[...], axis=0)
    norm = jnp.concatenate([whole[:, 0:1], whole[:, 2:3]], axis=0)
    curvature = jnp.concatenate([whole[:, 1:2], whole[:, 3:4]], axis=0)
    step = norm / (curvature + EPSILON)
    rim = from_across.shape[0]
    wide = jnp.broadcast_to(step, direction.shape[2:])
    step_length[...] = jnp.transpose(wide)[0:1]
    wide = wide[None]
    odd = parity()
    for q in range(rim):
        for c, part in (odd * rim + q, from_across), ((1 - odd) * rim + q, from_within):
            total = masked(image[c] + part[q].astype(jnp.float32))
            solution_next[c] = masked(solution[c] + wide * direction[c])
            residual_next[c] = masked(residual[c]) - wide * total


def swapped(across, within):
    count = lax.axis_size("orbit")
    assert count % 2 == 0
    outer = [(i, (i + 2 * (i % 2) - 1) % count) for i in range(count)]
    inner = [(i, i ^ 1) for i in range(count)]
    return lax.ppermute(across, "orbit", outer), lax.ppermute(within, "orbit", inner)


def local(
    solution, residual, direction, jacobian, crossing, tile_count, sightline_weight,
    length_class, smooth_weight,
):
    cols, species, probes, width = direction.shape
    assert REACH <= cols
    rim = cols // 2
    slots = crossing.shape[0]
    f32, bf16 = jnp.float32, jnp.bfloat16
    shape = jax.ShapeDtypeStruct
    column = (species, probes, width)
    elements = direction.size
    dot_flops = 2 * jacobian.size * probes
    near = shape((rim,) + column, bf16)
    whole = shape(direction.shape, f32)
    small = shape((probes, width), f32)

    held, across, within = call(
        rounding_kernel,
        (whole, near, near),
        [HBM()],
        2 * elements,
        10 * elements,
        [pltpu.SemaphoreType.DMA((2,))],
    )(in_hbm(direction))
    from_across, from_within = swapped(across, within)

    begun, faced, norm, curved, rows, jac, crossing, length_class, live = call(
        inner_kernel,
        (
            shape((2 * cols,) + column, f32), shape((2, rim) + column, f32), small, small,
            shape(sightline_weight.shape, f32), shape(jacobian.shape, bf16),
            pltpu.SMEM(crossing.shape, jnp.int32), pltpu.SMEM(length_class.shape, jnp.int32),
            pltpu.SMEM((8,), jnp.int32),
        ),
        [VMEM(), SMEM()] + [HBM()] * 6,
        60 * elements,
        4 * jacobian.size,
        [
            pltpu.VMEM(direction.shape, f32),
            pltpu.VMEM(smooth_weight.shape, f32),
            pltpu.VMEM(sightline_weight.shape, f32),
            pltpu.SemaphoreType.DMA((5 + len(slot_groups(slots)),)),
        ],
        [VMEM()] * 6 + [SMEM()] * 3,
    )(
        held, tile_count,
        *map(in_hbm, (
            residual, length_class, smooth_weight, sightline_weight, crossing, jacobian,
        )),
    )

    devices = lax.axis_size("orbit")
    peers = devices // 2
    weighted, sums = call(
        forward_kernel,
        (shape((slots, probes, width), bf16), shape((probes // 2, width), f32)),
        [SMEM()] * 2 + [VMEM()] * 9,
        dot_flops,
        2 * jacobian.size,
        [pltpu.VMEM((2 * cols * species, probes, width), bf16), pltpu.VMEM((probes, width), f32)],
    )(crossing, live, rows, across, within, from_across, from_within, faced, norm, curved, jac)
    assert devices % 4 == 0
    twin = lax.ppermute(sums, "orbit", [(i, i ^ 2) for i in range(devices)])

    image, across, within = call(
        backward_kernel,
        (whole, near, near),
        [SMEM()] * 3 + [VMEM()] * 6,
        dot_flops,
        2 * jacobian.size,
        [
            pltpu.VMEM((2 * cols * species, probes, width), f32),
            pltpu.VMEM((2, rim) + column, f32),
        ],
    )(crossing, length_class, live, smooth_weight, weighted, jac, begun, from_across, from_within)
    within, twin = lax.optimization_barrier((within, twin))
    from_across, from_within = swapped(across, within)
    alike = [[i for i in range(devices) if i & 2 == side] for side in (0, 2)]
    sums = jnp.broadcast_to((sums + twin)[None], (peers,) + sums.shape)
    sums = lax.all_to_all(sums, "orbit", 0, 0, axis_index_groups=alike)

    solution_next, residual_next, step_length = call(
        final_kernel,
        (whole, whole, shape((1, probes), f32)),
        [VMEM()] * 7,
        8 * elements,
        28 * elements,
    )(solution, residual, direction, image, from_across, from_within, sums)
    return solution_next, residual_next, step_length.reshape(probes)


def solution(mesh):
    wide = P(("grp", "orbit"), None, None, None)
    placed = (
        wide, wide, wide, wide,
        P(("grp", "orbit"), None),
        P(("grp", "orbit")),
        P(("grp", "orbit"), None),
        P("grp"),
        P(),
    )
    return jax.shard_map(
        local, mesh=mesh, in_specs=placed, out_specs=(wide, wide, P("grp")), check_vma=False
    )
```

```python
import functools

import jax
import jax.numpy as jnp
from jax import lax
from jax.experimental import pallas as pl
from jax.experimental.pallas import tpu as pltpu
from jax.sharding import PartitionSpec as P

LEVELS = 120
CLASSES = 4
REACH = 8
EPSILON = 1e-06
GROUP = 2
VMEM_LIMIT = 24 * 1024 * 1024

SMEM = functools.partial(pl.BlockSpec, memory_space=pltpu.SMEM)
VMEM = functools.partial(pl.BlockSpec, memory_space=pltpu.VMEM)
HBM = functools.partial(pl.BlockSpec, memory_space=pltpu.HBM)


def in_hbm(array):
    return pltpu.with_memory_space_constraint(array, pltpu.HBM)


def live_lanes(shape):
    return lax.broadcasted_iota(jnp.int32, shape, len(shape) - 1) < LEVELS


def masked(values):
    return jnp.where(live_lanes(values.shape), values, 0.0)


def call(kernel, out_shape, in_specs, flops, moved, scratch=(), out_specs=None):
    return pl.pallas_call(
        kernel,
        out_shape=out_shape,
        in_specs=in_specs,
        out_specs=tuple(out_specs or [VMEM()] * len(out_shape)),
        scratch_shapes=list(scratch),
        compiler_params=pltpu.CompilerParams(vmem_limit_bytes=VMEM_LIMIT),
        cost_estimate=pl.CostEstimate(flops=flops, bytes_accessed=moved, transcendentals=0),
    )


def parity():
    return lax.rem(lax.axis_index("orbit"), 2)


def rounding_kernel(direction_hbm, direction, across, within, sems):
    rim = across.shape[0]
    odd = parity()
    halves = ((odd, across), (1 - odd, within))
    copies = []
    for k, (place, _) in enumerate(halves):
        half = pl.ds(place * rim, rim)
        copies.append(
            pltpu.make_async_copy(direction_hbm.at[half], direction.at[half], sems.at[k])
        )
        copies[-1].start()
    for copy, (place, half) in zip(copies, halves):
        copy.wait()
        for c in range(rim):
            half[c] = masked(direction[place * rim + c]).astype(jnp.bfloat16)


def coupling(classes, cols, columns):
    total = classes.shape[0]
    first = lax.axis_index("orbit") * cols
    table = {}
    for c in columns:
        length = (classes[lax.rem(first + c + total, total)] + 1) * REACH // CLASSES
        for k in range(1, REACH + 1):
            table[c, k] = jnp.where(k <= length, jnp.float32(1.0 / (k * k)), jnp.float32(0.0))
    return table


def pull(table, to, values):
    result = None
    for c, value in values.items():
        if c != to and abs(c - to) <= REACH:
            term = table[min(c, to), abs(c - to)] * value
            result = term if result is None else result + term
    return 0.0 if result is None else -result


def slot_groups(slots):
    return [range(i, min(i + GROUP, slots)) for i in range(0, slots, GROUP)]


def if_live(count, group, work):
    if group[0] == 0:
        work()
    else:
        pl.when(group[0] < count)(work)


def inner_kernel(
    direction, count, residual_hbm, classes_hbm, smooth_hbm, sight_hbm, crossing_hbm, jac_hbm,
    begun, faced, norm, curved, rows, jac, crossing, classes, live, residual, smooth, sight, sems,
):
    pairs = (
        (classes_hbm, classes), (smooth_hbm, smooth), (sight_hbm, sight),
        (residual_hbm, residual), (crossing_hbm, crossing),
    )
    copies = [pltpu.make_async_copy(*pair, sems.at[i]) for i, pair in enumerate(pairs)]
    for copy in copies:
        copy.start()

    def load(group):
        part = pl.ds(group[0], len(group))
        return pltpu.make_async_copy(
            jac_hbm.at[part], jac.at[part], sems.at[len(pairs) + group[0] // GROUP]
        )

    for group in slot_groups(jac.shape[0]):
        if_live(count[0], group, lambda: load(group).start())
    live[0] = count[0]
    copies[0].wait()
    copies[1].wait()
    cols = direction.shape[0]
    rim = cols // 2
    table = coupling(classes, cols, range(-REACH, cols))
    weight = smooth[...][:, None, :]
    total = jnp.zeros(norm.shape, jnp.float32)
    values = {c: masked(direction[c]) for c in range(cols)}
    rests = {c: v - v.astype(jnp.bfloat16).astype(jnp.float32) for c, v in values.items()}
    for c in range(cols):
        centre = jnp.float32(1.0)
        for k in range(1, REACH + 1):
            centre = centre + (table[c, k] + table[c - k, k])
        result = weight * (centre * values[c] + pull(table, c, values))
        begun[rim + c] = result
        total = total + jnp.sum(values[c] * result, axis=0)
    low = {c: values[c] for c in range(rim)}
    high = {c: values[c] for c in range(rim, cols)}
    low_rests = {c: rests[c] for c in range(rim)}
    high_rests = {c: rests[c] for c in range(rim, cols)}
    for q in range(rim):
        facing = weight * pull(table, q - rim, high)
        faced[0, q] = facing
        begun[q] = facing + weight * pull(table, q - rim, low_rests)
        facing = weight * pull(table, q + cols, low)
        faced[1, q] = facing + weight * pull(table, q + cols, high)
        begun[rim + cols + q] = facing + weight * pull(table, q + cols, high_rests)
    curved[...] = total
    copies[2].wait()
    slot = lax.broadcasted_iota(jnp.int32, rows.shape, 0)
    rows[...] = jnp.where(slot < count[0], sight[...], 0.0)
    copies[3].wait()
    squares = jnp.zeros(norm.shape, jnp.float32)
    for c in range(cols):
        mres = masked(residual[c])
        squares = squares + jnp.sum(mres * mres, axis=0)
    norm[...] = squares
    copies[4].wait()
    for group in slot_groups(jac.shape[0]):
        if_live(count[0], group, lambda: load(group).wait())


def forward_kernel(
    crossing, live, rows, across, within, from_across, from_within, faced, norm, curved, jac,
    weighted, sums, window, total,
):
    slots, crossings = crossing.shape
    rim, species = across.shape[:2]
    span = rim * species
    odd = parity()
    places = (1 + odd, across), (2 - odd, within), (3 * odd, from_across), (3 - 3 * odd, from_within)
    for place, part in places:
        window[pl.ds(place * span, span)] = part[...].reshape(span, *part.shape[2:])
    edges = curved[...]
    for q in range(rim):
        for side, part in (odd, from_across), (1 - odd, from_within):
            edges = edges + 2.0 * jnp.sum(faced[side, q] * part[q].astype(jnp.float32), axis=0)
    total[...] = edges

    def project(group):
        added = jnp.zeros(total.shape, jnp.float32)
        for i in group:
            picked = jnp.concatenate([window[crossing[i, j]] for j in range(crossings)], axis=1)
            tiles = jnp.concatenate([jac[i, j] for j in range(crossings)], axis=1)
            integrals = lax.dot_general(
                picked, tiles, (((1,), (1,)), ((), ())), preferred_element_type=jnp.float32
            )
            product = (rows[pl.ds(i, 1), :] * integrals).astype(jnp.bfloat16)
            weighted[i] = product
            added = added + product.astype(jnp.float32) * integrals
        total[...] += added

    for group in slot_groups(slots):
        if_live(live[0], group, lambda: project(group))
    half = sums.shape[0]
    parts = [jnp.sum(x, axis=1, keepdims=True) for x in (norm[...], total[...])]
    parts = [part[h * half : (h + 1) * half] for h in range(2) for part in parts]
    lane = lax.broadcasted_iota(jnp.int32, sums.shape, 1)
    block = jnp.zeros(sums.shape, jnp.float32)
    for k, part in enumerate(parts):
        block = jnp.where(lane == k, part, block)
    sums[...] = block


def backward_kernel(
    crossing, classes, live, smooth, weighted, jac, begun, from_across, from_within,
    image, across, within, sums, near,
):
    slots, crossings = crossing.shape
    cols, species, probes, tile = image.shape
    rim = across.shape[0]
    span = rim * species
    odd = parity()
    near[odd] = from_across[...].astype(jnp.float32)
    near[1 - odd] = from_within[...].astype(jnp.float32)
    table = coupling(classes, cols, range(-rim, cols))
    weight = smooth[...][:, None, :]
    beside = {q - rim: near[0, q] for q in range(rim)} | {q + cols: near[1, q] for q in range(rim)}
    for c in range(cols):
        place = pl.ds(span + c * species, species)
        sums[place] = begun[rim + c] + weight * pull(table, c, beside)
    sums[pl.ds(0, span)] = begun[pl.ds(0, rim)].reshape(span, probes, tile)
    sums[pl.ds(3 * span, span)] = begun[pl.ds(rim + cols, rim)].reshape(span, probes, tile)

    def project(group):
        for i in group:
            tiles = jnp.concatenate([jac[i, j] for j in range(crossings)], axis=1)
            terms = jnp.dot(weighted[i], tiles, preferred_element_type=jnp.float32)
            for j in range(crossings):
                sums[crossing[i, j]] += terms[:, j * tile : (j + 1) * tile]

    for group in slot_groups(slots):
        if_live(live[0], group, lambda: project(group))
    for part, place in (across, 3 * odd), (within, 3 - 3 * odd):
        part[...] = sums[pl.ds(place * span, span)].astype(part.dtype).reshape(part.shape)
    image[...] = sums[pl.ds(span, 2 * span)].reshape(image.shape)


def final_kernel(
    solution, residual, direction, image, from_across, from_within, *rest
):
    *held, solution_next, residual_next, step_length = rest
    whole = tree_sum([part[...] for part in held])
    norm = jnp.concatenate([whole[:, 0:1], whole[:, 2:3]], axis=0)
    curvature = jnp.concatenate([whole[:, 1:2], whole[:, 3:4]], axis=0)
    step = norm / (curvature + EPSILON)
    rim = from_across.shape[0]
    wide = jnp.broadcast_to(step, direction.shape[2:])
    step_length[...] = jnp.transpose(wide)[0:1]
    wide = wide[None]
    odd = parity()
    for q in range(rim):
        for c, part in (odd * rim + q, from_across), ((1 - odd) * rim + q, from_within):
            total = masked(image[c] + part[q].astype(jnp.float32))
            solution_next[c] = masked(solution[c] + wide * direction[c])
            residual_next[c] = masked(residual[c]) - wide * total


def swapped_across(half):
    count = lax.axis_size("orbit")
    assert count % 2 == 0
    return lax.ppermute(half, "orbit", [(i, (i + 2 * (i % 2) - 1) % count) for i in range(count)])


def swapped_within(half):
    return lax.ppermute(half, "orbit", [(i, i ^ 1) for i in range(lax.axis_size("orbit"))])


def sum_steps(devices):
    assert devices >= 4 and devices & (devices - 1) == 0
    bits = [1 << b for b in range(1, devices.bit_length() - 1)]
    return [bits[:1]] + [bits[k : k + 2] for k in range(1, len(bits), 2)] + [[1]]


def partners(array, bits):
    devices = range(lax.axis_size("orbit"))
    masks = [sum(bit for k, bit in enumerate(bits) if m >> k & 1) for m in range(1, 1 << len(bits))]
    found = {
        mask: lax.ppermute(array, "orbit", [(i, i ^ mask) for i in devices]) for mask in masks[::-1]
    }
    return [found[mask] for mask in masks]


def tree_sum(parts):
    while len(parts) > 1:
        parts = [parts[k] + parts[k + 1] for k in range(0, len(parts), 2)]
    return parts[0]


def local(
    solution, residual, direction, jacobian, crossing, tile_count, sightline_weight,
    length_class, smooth_weight,
):
    cols, species, probes, width = direction.shape
    assert REACH <= cols
    rim = cols // 2
    slots = crossing.shape[0]
    f32, bf16 = jnp.float32, jnp.bfloat16
    shape = jax.ShapeDtypeStruct
    column = (species, probes, width)
    elements = direction.size
    dot_flops = 2 * jacobian.size * probes
    near = shape((rim,) + column, bf16)
    whole = shape(direction.shape, f32)
    small = shape((probes, width), f32)

    held, across, within = call(
        rounding_kernel,
        (whole, near, near),
        [HBM()],
        2 * elements,
        10 * elements,
        [pltpu.SemaphoreType.DMA((2,))],
    )(in_hbm(direction))
    from_across, from_within = swapped_across(across), swapped_within(within)

    begun, faced, norm, curved, rows, jac, crossing, length_class, live = call(
        inner_kernel,
        (
            shape((2 * cols,) + column, f32), shape((2, rim) + column, f32), small, small,
            shape(sightline_weight.shape, f32), shape(jacobian.shape, bf16),
            pltpu.SMEM(crossing.shape, jnp.int32), pltpu.SMEM(length_class.shape, jnp.int32),
            pltpu.SMEM((8,), jnp.int32),
        ),
        [VMEM(), SMEM()] + [HBM()] * 6,
        60 * elements,
        4 * jacobian.size,
        [
            pltpu.VMEM(direction.shape, f32),
            pltpu.VMEM(smooth_weight.shape, f32),
            pltpu.VMEM(sightline_weight.shape, f32),
            pltpu.SemaphoreType.DMA((5 + len(slot_groups(slots)),)),
        ],
        [VMEM()] * 6 + [SMEM()] * 3,
    )(
        held, tile_count,
        *map(in_hbm, (
            residual, length_class, smooth_weight, sightline_weight, crossing, jacobian,
        )),
    )

    devices = lax.axis_size("orbit")
    peers = devices // 2
    weighted, sums = call(
        forward_kernel,
        (shape((slots, probes, width), bf16), shape((probes // 2, width), f32)),
        [SMEM()] * 2 + [VMEM()] * 9,
        dot_flops,
        2 * jacobian.size,
        [pltpu.VMEM((2 * cols * species, probes, width), bf16), pltpu.VMEM((probes, width), f32)],
    )(crossing, live, rows, across, within, from_across, from_within, faced, norm, curved, jac)
    near_step, *far_steps = sum_steps(devices)
    held = [sums] + partners(sums, near_step)

    image, across, within = call(
        backward_kernel,
        (whole, near, near),
        [SMEM()] * 3 + [VMEM()] * 6,
        dot_flops,
        2 * jacobian.size,
        [
            pltpu.VMEM((2 * cols * species, probes, width), f32),
            pltpu.VMEM((2, rim) + column, f32),
        ],
    )(crossing, length_class, live, smooth_weight, weighted, jac, begun, from_across, from_within)
    from_across = swapped_across(across)
    within, *held = lax.optimization_barrier((within, *held))
    for step in far_steps[:-1]:
        sums = tree_sum(held)
        held = [sums] + partners(sums, step)
    within, *held = lax.optimization_barrier((within, *held))
    sums = tree_sum(held)
    held = [sums] + partners(sums, far_steps[-1])
    from_within = swapped_within(within)

    solution_next, residual_next, step_length = call(
        final_kernel,
        (whole, whole, shape((1, probes), f32)),
        [VMEM()] * (6 + len(held)),
        8 * elements,
        28 * elements,
    )(solution, residual, direction, image, from_across, from_within, *held)
    return solution_next, residual_next, step_length.reshape(probes)


def solution(mesh):
    wide = P(("grp", "orbit"), None, None, None)
    placed = (
        wide, wide, wide, wide,
        P(("grp", "orbit"), None),
        P(("grp", "orbit")),
        P(("grp", "orbit"), None),
        P("grp"),
        P(),
    )
    return jax.shard_map(
        local, mesh=mesh, in_specs=placed, out_specs=(wide, wide, P("grp")), check_vma=False
    )
```

```python
import functools

import jax
import jax.numpy as jnp
from jax import lax
from jax.experimental import pallas as pl
from jax.experimental.pallas import tpu as pltpu
from jax.sharding import PartitionSpec as P

LEVELS = 120
CLASSES = 4
REACH = 8
EPSILON = 1e-06
GROUP = 2
VMEM_LIMIT = 24 * 1024 * 1024

SMEM = functools.partial(pl.BlockSpec, memory_space=pltpu.SMEM)
VMEM = functools.partial(pl.BlockSpec, memory_space=pltpu.VMEM)
HBM = functools.partial(pl.BlockSpec, memory_space=pltpu.HBM)


def in_hbm(array):
    return pltpu.with_memory_space_constraint(array, pltpu.HBM)


def live_lanes(shape):
    return lax.broadcasted_iota(jnp.int32, shape, len(shape) - 1) < LEVELS


def masked(values):
    return jnp.where(live_lanes(values.shape), values, 0.0)


def call(kernel, out_shape, in_specs, flops, moved, scratch=(), out_specs=None):
    return pl.pallas_call(
        kernel,
        out_shape=out_shape,
        in_specs=in_specs,
        out_specs=tuple(out_specs or [VMEM()] * len(out_shape)),
        scratch_shapes=list(scratch),
        compiler_params=pltpu.CompilerParams(vmem_limit_bytes=VMEM_LIMIT),
        cost_estimate=pl.CostEstimate(flops=flops, bytes_accessed=moved, transcendentals=0),
    )


def parity():
    return lax.rem(lax.axis_index("orbit"), 2)


def rounding_kernel(direction_hbm, direction, across, within, sems):
    rim = across.shape[0]
    odd = parity()
    halves = ((odd, across), (1 - odd, within))
    copies = []
    for k, (place, _) in enumerate(halves):
        half = pl.ds(place * rim, rim)
        copies.append(
            pltpu.make_async_copy(direction_hbm.at[half], direction.at[half], sems.at[k])
        )
        copies[-1].start()
    for copy, (place, half) in zip(copies, halves):
        copy.wait()
        for c in range(rim):
            half[c] = masked(direction[place * rim + c]).astype(jnp.bfloat16)


def coupling(classes, cols, columns):
    total = classes.shape[0]
    first = lax.axis_index("orbit") * cols
    table = {}
    for c in columns:
        length = (classes[lax.rem(first + c + total, total)] + 1) * REACH // CLASSES
        for k in range(1, REACH + 1):
            table[c, k] = jnp.where(k <= length, jnp.float32(1.0 / (k * k)), jnp.float32(0.0))
    return table


def pull(table, to, values):
    result = None
    for c, value in values.items():
        if c != to and abs(c - to) <= REACH:
            term = table[min(c, to), abs(c - to)] * value
            result = term if result is None else result + term
    return 0.0 if result is None else -result


def slot_groups(slots):
    return [range(i, min(i + GROUP, slots)) for i in range(0, slots, GROUP)]


def if_live(count, group, work):
    if group[0] == 0:
        work()
    else:
        pl.when(group[0] < count)(work)


def inner_kernel(
    direction, count, residual_hbm, classes_hbm, smooth_hbm, sight_hbm, crossing_hbm, jac_hbm,
    begun, faced, norm, curved, rows, jac, crossing, classes, live, residual, smooth, sight, sems,
):
    pairs = (
        (classes_hbm, classes), (smooth_hbm, smooth), (sight_hbm, sight),
        (residual_hbm, residual), (crossing_hbm, crossing),
    )
    copies = [pltpu.make_async_copy(*pair, sems.at[i]) for i, pair in enumerate(pairs)]
    for copy in copies:
        copy.start()

    def load(group):
        part = pl.ds(group[0], len(group))
        return pltpu.make_async_copy(
            jac_hbm.at[part], jac.at[part], sems.at[len(pairs) + group[0] // GROUP]
        )

    for group in slot_groups(jac.shape[0]):
        if_live(count[0], group, lambda: load(group).start())
    live[0] = count[0]
    copies[0].wait()
    copies[1].wait()
    cols = direction.shape[0]
    rim = cols // 2
    table = coupling(classes, cols, range(-REACH, cols))
    weight = smooth[...][:, None, :]
    total = jnp.zeros(norm.shape, jnp.float32)
    values = {c: masked(direction[c]) for c in range(cols)}
    rests = {c: v - v.astype(jnp.bfloat16).astype(jnp.float32) for c, v in values.items()}
    for c in range(cols):
        centre = jnp.float32(1.0)
        for k in range(1, REACH + 1):
            centre = centre + (table[c, k] + table[c - k, k])
        result = weight * (centre * values[c] + pull(table, c, values))
        begun[rim + c] = result
        total = total + jnp.sum(values[c] * result, axis=0)
    low = {c: values[c] for c in range(rim)}
    high = {c: values[c] for c in range(rim, cols)}
    low_rests = {c: rests[c] for c in range(rim)}
    high_rests = {c: rests[c] for c in range(rim, cols)}
    for q in range(rim):
        facing = weight * pull(table, q - rim, high)
        faced[0, q] = facing
        begun[q] = facing + weight * pull(table, q - rim, low_rests)
        facing = weight * pull(table, q + cols, low)
        faced[1, q] = facing + weight * pull(table, q + cols, high)
        begun[rim + cols + q] = facing + weight * pull(table, q + cols, high_rests)
    curved[...] = total
    copies[2].wait()
    slot = lax.broadcasted_iota(jnp.int32, rows.shape, 0)
    rows[...] = jnp.where(slot < count[0], sight[...], 0.0)
    copies[3].wait()
    squares = jnp.zeros(norm.shape, jnp.float32)
    for c in range(cols):
        mres = masked(residual[c])
        squares = squares + jnp.sum(mres * mres, axis=0)
    norm[...] = squares
    copies[4].wait()
    for group in slot_groups(jac.shape[0]):
        if_live(count[0], group, lambda: load(group).wait())


def forward_kernel(
    crossing, live, rows, across, within, from_across, from_within, faced, norm, curved, jac,
    weighted, sums, window, total,
):
    slots, crossings = crossing.shape
    rim, species = across.shape[:2]
    span = rim * species
    odd = parity()
    places = (1 + odd, across), (2 - odd, within), (3 * odd, from_across), (3 - 3 * odd, from_within)
    for place, part in places:
        window[pl.ds(place * span, span)] = part[...].reshape(span, *part.shape[2:])
    edges = curved[...]
    for q in range(rim):
        for side, part in (odd, from_across), (1 - odd, from_within):
            edges = edges + 2.0 * jnp.sum(faced[side, q] * part[q].astype(jnp.float32), axis=0)
    total[...] = edges

    def project(group):
        added = jnp.zeros(total.shape, jnp.float32)
        for i in group:
            picked = jnp.concatenate([window[crossing[i, j]] for j in range(crossings)], axis=1)
            tiles = jnp.concatenate([jac[i, j] for j in range(crossings)], axis=1)
            integrals = lax.dot_general(
                picked, tiles, (((1,), (1,)), ((), ())), preferred_element_type=jnp.float32
            )
            product = (rows[pl.ds(i, 1), :] * integrals).astype(jnp.bfloat16)
            weighted[i] = product
            added = added + product.astype(jnp.float32) * integrals
        total[...] += added

    for group in slot_groups(slots):
        if_live(live[0], group, lambda: project(group))
    half = sums.shape[0]
    parts = [jnp.sum(x, axis=1, keepdims=True) for x in (norm[...], total[...])]
    parts = [part[h * half : (h + 1) * half] for h in range(2) for part in parts]
    lane = lax.broadcasted_iota(jnp.int32, sums.shape, 1)
    block = jnp.zeros(sums.shape, jnp.float32)
    for k, part in enumerate(parts):
        block = jnp.where(lane == k, part, block)
    sums[...] = block


def backward_kernel(
    crossing, classes, live, smooth, weighted, jac, begun, from_across, from_within,
    image, across, within, sums, near,
):
    slots, crossings = crossing.shape
    cols, species, probes, tile = image.shape
    rim = across.shape[0]
    span = rim * species
    odd = parity()
    near[odd] = from_across[...].astype(jnp.float32)
    near[1 - odd] = from_within[...].astype(jnp.float32)
    table = coupling(classes, cols, range(-rim, cols))
    weight = smooth[...][:, None, :]
    beside = {q - rim: near[0, q] for q in range(rim)} | {q + cols: near[1, q] for q in range(rim)}
    for c in range(cols):
        place = pl.ds(span + c * species, species)
        sums[place] = begun[rim + c] + weight * pull(table, c, beside)
    sums[pl.ds(0, span)] = begun[pl.ds(0, rim)].reshape(span, probes, tile)
    sums[pl.ds(3 * span, span)] = begun[pl.ds(rim + cols, rim)].reshape(span, probes, tile)

    def project(group):
        for i in group:
            tiles = jnp.concatenate([jac[i, j] for j in range(crossings)], axis=1)
            terms = jnp.dot(weighted[i], tiles, preferred_element_type=jnp.float32)
            for j in range(crossings):
                sums[crossing[i, j]] += terms[:, j * tile : (j + 1) * tile]

    for group in slot_groups(slots):
        if_live(live[0], group, lambda: project(group))
    for part, place in (across, 3 * odd), (within, 3 - 3 * odd):
        part[...] = sums[pl.ds(place * span, span)].astype(part.dtype).reshape(part.shape)
    image[...] = sums[pl.ds(span, 2 * span)].reshape(image.shape)


def final_kernel(
    solution, residual, direction, image, from_across, from_within, *rest
):
    *held, solution_next, residual_next, step_length = rest
    whole = tree_sum([part[...] for part in held])
    norm = jnp.concatenate([whole[:, 0:1], whole[:, 2:3]], axis=0)
    curvature = jnp.concatenate([whole[:, 1:2], whole[:, 3:4]], axis=0)
    step = norm / (curvature + EPSILON)
    rim = from_across.shape[0]
    wide = jnp.broadcast_to(step, direction.shape[2:])
    step_length[...] = jnp.transpose(wide)[0:1]
    wide = wide[None]
    odd = parity()
    for q in range(rim):
        for c, part in (odd * rim + q, from_across), ((1 - odd) * rim + q, from_within):
            total = masked(image[c] + part[q].astype(jnp.float32))
            solution_next[c] = masked(solution[c] + wide * direction[c])
            residual_next[c] = masked(residual[c]) - wide * total


def swapped_across(half):
    count = lax.axis_size("orbit")
    assert count % 2 == 0
    return lax.ppermute(half, "orbit", [(i, (i + 2 * (i % 2) - 1) % count) for i in range(count)])


def swapped_within(half):
    return lax.ppermute(half, "orbit", [(i, i ^ 1) for i in range(lax.axis_size("orbit"))])


def sum_steps(devices):
    assert devices >= 4 and devices & (devices - 1) == 0
    return [[1 << b] for b in range(1, devices.bit_length() - 1)] + [[1]]


def partners(array, bits):
    devices = range(lax.axis_size("orbit"))
    masks = [sum(bit for k, bit in enumerate(bits) if m >> k & 1) for m in range(1, 1 << len(bits))]
    found = {
        mask: lax.ppermute(array, "orbit", [(i, i ^ mask) for i in devices]) for mask in masks[::-1]
    }
    return [found[mask] for mask in masks]


def tree_sum(parts):
    while len(parts) > 1:
        parts = [parts[k] + parts[k + 1] for k in range(0, len(parts), 2)]
    return parts[0]


def local(
    solution, residual, direction, jacobian, crossing, tile_count, sightline_weight,
    length_class, smooth_weight,
):
    cols, species, probes, width = direction.shape
    assert REACH <= cols
    rim = cols // 2
    slots = crossing.shape[0]
    f32, bf16 = jnp.float32, jnp.bfloat16
    shape = jax.ShapeDtypeStruct
    column = (species, probes, width)
    elements = direction.size
    dot_flops = 2 * jacobian.size * probes
    near = shape((rim,) + column, bf16)
    whole = shape(direction.shape, f32)
    small = shape((probes, width), f32)

    held, across, within = call(
        rounding_kernel,
        (whole, near, near),
        [HBM()],
        2 * elements,
        10 * elements,
        [pltpu.SemaphoreType.DMA((2,))],
    )(in_hbm(direction))
    from_across, from_within = swapped_across(across), swapped_within(within)

    begun, faced, norm, curved, rows, jac, crossing, length_class, live = call(
        inner_kernel,
        (
            shape((2 * cols,) + column, f32), shape((2, rim) + column, f32), small, small,
            shape(sightline_weight.shape, f32), shape(jacobian.shape, bf16),
            pltpu.SMEM(crossing.shape, jnp.int32), pltpu.SMEM(length_class.shape, jnp.int32),
            pltpu.SMEM((8,), jnp.int32),
        ),
        [VMEM(), SMEM()] + [HBM()] * 6,
        60 * elements,
        4 * jacobian.size,
        [
            pltpu.VMEM(direction.shape, f32),
            pltpu.VMEM(smooth_weight.shape, f32),
            pltpu.VMEM(sightline_weight.shape, f32),
            pltpu.SemaphoreType.DMA((5 + len(slot_groups(slots)),)),
        ],
        [VMEM()] * 6 + [SMEM()] * 3,
    )(
        held, tile_count,
        *map(in_hbm, (
            residual, length_class, smooth_weight, sightline_weight, crossing, jacobian,
        )),
    )

    devices = lax.axis_size("orbit")
    peers = devices // 2
    weighted, sums = call(
        forward_kernel,
        (shape((slots, probes, width), bf16), shape((probes // 2, width), f32)),
        [SMEM()] * 2 + [VMEM()] * 9,
        dot_flops,
        2 * jacobian.size,
        [pltpu.VMEM((2 * cols * species, probes, width), bf16), pltpu.VMEM((probes, width), f32)],
    )(crossing, live, rows, across, within, from_across, from_within, faced, norm, curved, jac)
    near_step, *far_steps = sum_steps(devices)
    held = [sums] + partners(sums, near_step)

    image, across, within = call(
        backward_kernel,
        (whole, near, near),
        [SMEM()] * 3 + [VMEM()] * 6,
        dot_flops,
        2 * jacobian.size,
        [
            pltpu.VMEM((2 * cols * species, probes, width), f32),
            pltpu.VMEM((2, rim) + column, f32),
        ],
    )(crossing, length_class, live, smooth_weight, weighted, jac, begun, from_across, from_within)
    from_across = swapped_across(across)
    within, *held = lax.optimization_barrier((within, *held))
    sums = tree_sum(held)
    held = [sums] + partners(sums, far_steps[0])
    within, *held = lax.optimization_barrier((within, *held))
    from_within = swapped_within(within)
    for step in far_steps[1:]:
        sums = tree_sum(held)
        held = [sums] + partners(sums, step)

    solution_next, residual_next, step_length = call(
        final_kernel,
        (whole, whole, shape((1, probes), f32)),
        [VMEM()] * (6 + len(held)),
        8 * elements,
        28 * elements,
    )(solution, residual, direction, image, from_across, from_within, *held)
    return solution_next, residual_next, step_length.reshape(probes)


def solution(mesh):
    wide = P(("grp", "orbit"), None, None, None)
    placed = (
        wide, wide, wide, wide,
        P(("grp", "orbit"), None),
        P(("grp", "orbit")),
        P(("grp", "orbit"), None),
        P("grp"),
        P(),
    )
    return jax.shard_map(
        local, mesh=mesh, in_specs=placed, out_specs=(wide, wide, P("grp")), check_vma=False
    )
```

```python
import functools

import jax
import jax.numpy as jnp
from jax import lax
from jax.experimental import pallas as pl
from jax.experimental.pallas import tpu as pltpu
from jax.sharding import PartitionSpec as P

LEVELS = 120
CLASSES = 4
REACH = 8
EPSILON = 1e-06
GROUP = 2
VMEM_LIMIT = 24 * 1024 * 1024

SMEM = functools.partial(pl.BlockSpec, memory_space=pltpu.SMEM)
VMEM = functools.partial(pl.BlockSpec, memory_space=pltpu.VMEM)
HBM = functools.partial(pl.BlockSpec, memory_space=pltpu.HBM)


def in_hbm(array):
    return pltpu.with_memory_space_constraint(array, pltpu.HBM)


def live_lanes(shape):
    return lax.broadcasted_iota(jnp.int32, shape, len(shape) - 1) < LEVELS


def masked(values):
    return jnp.where(live_lanes(values.shape), values, 0.0)


def call(kernel, out_shape, in_specs, flops, moved, scratch=(), out_specs=None):
    return pl.pallas_call(
        kernel,
        out_shape=out_shape,
        in_specs=in_specs,
        out_specs=tuple(out_specs or [VMEM()] * len(out_shape)),
        scratch_shapes=list(scratch),
        compiler_params=pltpu.CompilerParams(vmem_limit_bytes=VMEM_LIMIT),
        cost_estimate=pl.CostEstimate(flops=flops, bytes_accessed=moved, transcendentals=0),
    )


def parity():
    return lax.rem(lax.axis_index("orbit"), 2)


def rounding_kernel(direction_hbm, direction, across, within, sems):
    rim = across.shape[0]
    odd = parity()
    halves = ((odd, across), (1 - odd, within))
    copies = []
    for k, (place, _) in enumerate(halves):
        half = pl.ds(place * rim, rim)
        copies.append(
            pltpu.make_async_copy(direction_hbm.at[half], direction.at[half], sems.at[k])
        )
        copies[-1].start()
    for copy, (place, half) in zip(copies, halves):
        copy.wait()
        for c in range(rim):
            half[c] = masked(direction[place * rim + c]).astype(jnp.bfloat16)


def coupling(classes, cols, columns):
    total = classes.shape[0]
    first = lax.axis_index("orbit") * cols
    table = {}
    for c in columns:
        length = (classes[lax.rem(first + c + total, total)] + 1) * REACH // CLASSES
        for k in range(1, REACH + 1):
            table[c, k] = jnp.where(k <= length, jnp.float32(1.0 / (k * k)), jnp.float32(0.0))
    return table


def pull(table, to, values):
    result = None
    for c, value in values.items():
        if c != to and abs(c - to) <= REACH:
            term = table[min(c, to), abs(c - to)] * value
            result = term if result is None else result + term
    return 0.0 if result is None else -result


def slot_groups(slots):
    return [range(i, min(i + GROUP, slots)) for i in range(0, slots, GROUP)]


def if_live(count, group, work):
    if group[0] == 0:
        work()
    else:
        pl.when(group[0] < count)(work)


def inner_kernel(
    direction, count, residual_hbm, classes_hbm, smooth_hbm, sight_hbm, crossing_hbm, jac_hbm,
    begun, faced, norm, curved, rows, jac, crossing, classes, live, residual, smooth, sight, sems,
):
    pairs = (
        (classes_hbm, classes), (smooth_hbm, smooth), (sight_hbm, sight),
        (residual_hbm, residual), (crossing_hbm, crossing),
    )
    copies = [pltpu.make_async_copy(*pair, sems.at[i]) for i, pair in enumerate(pairs)]
    for copy in copies:
        copy.start()

    def load(group):
        part = pl.ds(group[0], len(group))
        return pltpu.make_async_copy(
            jac_hbm.at[part], jac.at[part], sems.at[len(pairs) + group[0] // GROUP]
        )

    for group in slot_groups(jac.shape[0]):
        if_live(count[0], group, lambda: load(group).start())
    live[0] = count[0]
    copies[0].wait()
    copies[1].wait()
    cols = direction.shape[0]
    rim = cols // 2
    table = coupling(classes, cols, range(-REACH, cols))
    weight = smooth[...][:, None, :]
    total = jnp.zeros(norm.shape, jnp.float32)
    values = {c: masked(direction[c]) for c in range(cols)}
    rests = {c: v - v.astype(jnp.bfloat16).astype(jnp.float32) for c, v in values.items()}
    for c in range(cols):
        centre = jnp.float32(1.0)
        for k in range(1, REACH + 1):
            centre = centre + (table[c, k] + table[c - k, k])
        result = weight * (centre * values[c] + pull(table, c, values))
        begun[rim + c] = result
        total = total + jnp.sum(values[c] * result, axis=0)
    low = {c: values[c] for c in range(rim)}
    high = {c: values[c] for c in range(rim, cols)}
    low_rests = {c: rests[c] for c in range(rim)}
    high_rests = {c: rests[c] for c in range(rim, cols)}
    for q in range(rim):
        facing = weight * pull(table, q - rim, high)
        faced[0, q] = facing
        begun[q] = facing + weight * pull(table, q - rim, low_rests)
        facing = weight * pull(table, q + cols, low)
        faced[1, q] = facing + weight * pull(table, q + cols, high)
        begun[rim + cols + q] = facing + weight * pull(table, q + cols, high_rests)
    curved[...] = total
    copies[2].wait()
    slot = lax.broadcasted_iota(jnp.int32, rows.shape, 0)
    rows[...] = jnp.where(slot < count[0], sight[...], 0.0)
    copies[3].wait()
    squares = jnp.zeros(norm.shape, jnp.float32)
    for c in range(cols):
        mres = masked(residual[c])
        squares = squares + jnp.sum(mres * mres, axis=0)
    norm[...] = squares
    copies[4].wait()
    for group in slot_groups(jac.shape[0]):
        if_live(count[0], group, lambda: load(group).wait())


def forward_kernel(
    crossing, live, rows, across, within, from_across, from_within, faced, norm, curved, jac,
    weighted, sums, window, total,
):
    slots, crossings = crossing.shape
    rim, species = across.shape[:2]
    span = rim * species
    odd = parity()
    places = (1 + odd, across), (2 - odd, within), (3 * odd, from_across), (3 - 3 * odd, from_within)
    for place, part in places:
        window[pl.ds(place * span, span)] = part[...].reshape(span, *part.shape[2:])
    edges = curved[...]
    for q in range(rim):
        for side, part in (odd, from_across), (1 - odd, from_within):
            edges = edges + 2.0 * jnp.sum(faced[side, q] * part[q].astype(jnp.float32), axis=0)
    total[...] = edges

    def project(group):
        added = jnp.zeros(total.shape, jnp.float32)
        for i in group:
            picked = jnp.concatenate([window[crossing[i, j]] for j in range(crossings)], axis=1)
            tiles = jnp.concatenate([jac[i, j] for j in range(crossings)], axis=1)
            integrals = lax.dot_general(
                picked, tiles, (((1,), (1,)), ((), ())), preferred_element_type=jnp.float32
            )
            product = (rows[pl.ds(i, 1), :] * integrals).astype(jnp.bfloat16)
            weighted[i] = product
            added = added + product.astype(jnp.float32) * integrals
        total[...] += added

    for group in slot_groups(slots):
        if_live(live[0], group, lambda: project(group))
    half = sums.shape[0]
    parts = [jnp.sum(x, axis=1, keepdims=True) for x in (norm[...], total[...])]
    parts = [part[h * half : (h + 1) * half] for h in range(2) for part in parts]
    lane = lax.broadcasted_iota(jnp.int32, sums.shape, 1)
    block = jnp.zeros(sums.shape, jnp.float32)
    for k, part in enumerate(parts):
        block = jnp.where(lane == k, part, block)
    sums[...] = block


def backward_kernel(
    crossing, classes, live, smooth, weighted, jac, begun, from_across, from_within,
    image, across, within, sums, near,
):
    slots, crossings = crossing.shape
    cols, species, probes, tile = image.shape
    rim = across.shape[0]
    span = rim * species
    odd = parity()
    near[odd] = from_across[...].astype(jnp.float32)
    near[1 - odd] = from_within[...].astype(jnp.float32)
    table = coupling(classes, cols, range(-rim, cols))
    weight = smooth[...][:, None, :]
    beside = {q - rim: near[0, q] for q in range(rim)} | {q + cols: near[1, q] for q in range(rim)}
    for c in range(cols):
        place = pl.ds(span + c * species, species)
        sums[place] = begun[rim + c] + weight * pull(table, c, beside)
    sums[pl.ds(0, span)] = begun[pl.ds(0, rim)].reshape(span, probes, tile)
    sums[pl.ds(3 * span, span)] = begun[pl.ds(rim + cols, rim)].reshape(span, probes, tile)

    def project(group):
        for i in group:
            tiles = jnp.concatenate([jac[i, j] for j in range(crossings)], axis=1)
            terms = jnp.dot(weighted[i], tiles, preferred_element_type=jnp.float32)
            for j in range(crossings):
                sums[crossing[i, j]] += terms[:, j * tile : (j + 1) * tile]

    for group in slot_groups(slots):
        if_live(live[0], group, lambda: project(group))
    for part, place in (across, 3 * odd), (within, 3 - 3 * odd):
        part[...] = sums[pl.ds(place * span, span)].astype(part.dtype).reshape(part.shape)
    image[...] = sums[pl.ds(span, 2 * span)].reshape(image.shape)


def final_kernel(
    solution, residual, direction, image, from_across, from_within, *rest
):
    *held, solution_next, residual_next, step_length = rest
    whole = tree_sum([part[...] for part in held])
    norm = jnp.concatenate([whole[:, 0:1], whole[:, 2:3]], axis=0)
    curvature = jnp.concatenate([whole[:, 1:2], whole[:, 3:4]], axis=0)
    step = norm / (curvature + EPSILON)
    rim = from_across.shape[0]
    wide = jnp.broadcast_to(step, direction.shape[2:])
    step_length[...] = jnp.transpose(wide)[0:1]
    wide = wide[None]
    odd = parity()
    for q in range(rim):
        for c, part in (odd * rim + q, from_across), ((1 - odd) * rim + q, from_within):
            total = masked(image[c] + part[q].astype(jnp.float32))
            solution_next[c] = masked(solution[c] + wide * direction[c])
            residual_next[c] = masked(residual[c]) - wide * total


def swapped_across(half):
    count = lax.axis_size("orbit")
    assert count % 2 == 0
    return lax.ppermute(half, "orbit", [(i, (i + 2 * (i % 2) - 1) % count) for i in range(count)])


def swapped_within(half):
    return lax.ppermute(half, "orbit", [(i, i ^ 1) for i in range(lax.axis_size("orbit"))])


def sum_steps(devices):
    assert devices >= 8 and devices & (devices - 1) == 0
    return [[1 << b] for b in range(1, devices.bit_length() - 2)] + [[1, devices // 2]]


def partners(array, bits):
    devices = range(lax.axis_size("orbit"))
    masks = [sum(bit for k, bit in enumerate(bits) if m >> k & 1) for m in range(1, 1 << len(bits))]
    found = {
        mask: lax.ppermute(array, "orbit", [(i, i ^ mask) for i in devices]) for mask in masks[::-1]
    }
    return [found[mask] for mask in masks]


def tree_sum(parts):
    while len(parts) > 1:
        parts = [parts[k] + parts[k + 1] for k in range(0, len(parts), 2)]
    return parts[0]


def local(
    solution, residual, direction, jacobian, crossing, tile_count, sightline_weight,
    length_class, smooth_weight,
):
    cols, species, probes, width = direction.shape
    assert REACH <= cols
    rim = cols // 2
    slots = crossing.shape[0]
    f32, bf16 = jnp.float32, jnp.bfloat16
    shape = jax.ShapeDtypeStruct
    column = (species, probes, width)
    elements = direction.size
    dot_flops = 2 * jacobian.size * probes
    near = shape((rim,) + column, bf16)
    whole = shape(direction.shape, f32)
    small = shape((probes, width), f32)

    held, across, within = call(
        rounding_kernel,
        (whole, near, near),
        [HBM()],
        2 * elements,
        10 * elements,
        [pltpu.SemaphoreType.DMA((2,))],
    )(in_hbm(direction))
    from_across, from_within = swapped_across(across), swapped_within(within)

    begun, faced, norm, curved, rows, jac, crossing, length_class, live = call(
        inner_kernel,
        (
            shape((2 * cols,) + column, f32), shape((2, rim) + column, f32), small, small,
            shape(sightline_weight.shape, f32), shape(jacobian.shape, bf16),
            pltpu.SMEM(crossing.shape, jnp.int32), pltpu.SMEM(length_class.shape, jnp.int32),
            pltpu.SMEM((8,), jnp.int32),
        ),
        [VMEM(), SMEM()] + [HBM()] * 6,
        60 * elements,
        4 * jacobian.size,
        [
            pltpu.VMEM(direction.shape, f32),
            pltpu.VMEM(smooth_weight.shape, f32),
            pltpu.VMEM(sightline_weight.shape, f32),
            pltpu.SemaphoreType.DMA((5 + len(slot_groups(slots)),)),
        ],
        [VMEM()] * 6 + [SMEM()] * 3,
    )(
        held, tile_count,
        *map(in_hbm, (
            residual, length_class, smooth_weight, sightline_weight, crossing, jacobian,
        )),
    )

    devices = lax.axis_size("orbit")
    peers = devices // 2
    weighted, sums = call(
        forward_kernel,
        (shape((slots, probes, width), bf16), shape((probes // 2, width), f32)),
        [SMEM()] * 2 + [VMEM()] * 9,
        dot_flops,
        2 * jacobian.size,
        [pltpu.VMEM((2 * cols * species, probes, width), bf16), pltpu.VMEM((probes, width), f32)],
    )(crossing, live, rows, across, within, from_across, from_within, faced, norm, curved, jac)
    near_step, *far_steps = sum_steps(devices)
    held = [sums] + partners(sums, near_step)

    image, across, within = call(
        backward_kernel,
        (whole, near, near),
        [SMEM()] * 3 + [VMEM()] * 6,
        dot_flops,
        2 * jacobian.size,
        [
            pltpu.VMEM((2 * cols * species, probes, width), f32),
            pltpu.VMEM((2, rim) + column, f32),
        ],
    )(crossing, length_class, live, smooth_weight, weighted, jac, begun, from_across, from_within)
    from_across = swapped_across(across)
    within, *held = lax.optimization_barrier((within, *held))
    sums = tree_sum(held)
    held = [sums] + partners(sums, far_steps[0])
    within, *held = lax.optimization_barrier((within, *held))
    from_within = swapped_within(within)
    for step in far_steps[1:]:
        sums = tree_sum(held)
        held = [sums] + partners(sums, step)

    solution_next, residual_next, step_length = call(
        final_kernel,
        (whole, whole, shape((1, probes), f32)),
        [VMEM()] * (6 + len(held)),
        8 * elements,
        28 * elements,
    )(solution, residual, direction, image, from_across, from_within, *held)
    return solution_next, residual_next, step_length.reshape(probes)


def solution(mesh):
    wide = P(("grp", "orbit"), None, None, None)
    placed = (
        wide, wide, wide, wide,
        P(("grp", "orbit"), None),
        P(("grp", "orbit")),
        P(("grp", "orbit"), None),
        P("grp"),
        P(),
    )
    return jax.shard_map(
        local, mesh=mesh, in_specs=placed, out_specs=(wide, wide, P("grp")), check_vma=False
    )
```

```python
import functools

import jax
import jax.numpy as jnp
from jax import lax
from jax.experimental import pallas as pl
from jax.experimental.pallas import tpu as pltpu
from jax.sharding import PartitionSpec as P

LEVELS = 120
CLASSES = 4
REACH = 8
EPSILON = 1e-06
GROUP = 2
VMEM_LIMIT = 24 * 1024 * 1024

SMEM = functools.partial(pl.BlockSpec, memory_space=pltpu.SMEM)
VMEM = functools.partial(pl.BlockSpec, memory_space=pltpu.VMEM)
HBM = functools.partial(pl.BlockSpec, memory_space=pltpu.HBM)


def in_hbm(array):
    return pltpu.with_memory_space_constraint(array, pltpu.HBM)


def live_lanes(shape):
    return lax.broadcasted_iota(jnp.int32, shape, len(shape) - 1) < LEVELS


def masked(values):
    return jnp.where(live_lanes(values.shape), values, 0.0)


def call(kernel, out_shape, in_specs, flops, moved, scratch=(), out_specs=None):
    return pl.pallas_call(
        kernel,
        out_shape=out_shape,
        in_specs=in_specs,
        out_specs=tuple(out_specs or [VMEM()] * len(out_shape)),
        scratch_shapes=list(scratch),
        compiler_params=pltpu.CompilerParams(vmem_limit_bytes=VMEM_LIMIT),
        cost_estimate=pl.CostEstimate(flops=flops, bytes_accessed=moved, transcendentals=0),
    )


def parity():
    return lax.rem(lax.axis_index("orbit"), 2)


def rounding_kernel(direction_hbm, direction, across, within, sems):
    rim = across.shape[0]
    odd = parity()
    halves = ((odd, across), (1 - odd, within))
    copies = []
    for k, (place, _) in enumerate(halves):
        half = pl.ds(place * rim, rim)
        copies.append(
            pltpu.make_async_copy(direction_hbm.at[half], direction.at[half], sems.at[k])
        )
        copies[-1].start()
    for copy, (place, half) in zip(copies, halves):
        copy.wait()
        for c in range(rim):
            half[c] = masked(direction[place * rim + c]).astype(jnp.bfloat16)


def coupling(classes, cols, columns):
    total = classes.shape[0]
    first = lax.axis_index("orbit") * cols
    table = {}
    for c in columns:
        length = (classes[lax.rem(first + c + total, total)] + 1) * REACH // CLASSES
        for k in range(1, REACH + 1):
            table[c, k] = jnp.where(k <= length, jnp.float32(1.0 / (k * k)), jnp.float32(0.0))
    return table


def pull(table, to, values):
    result = None
    for c, value in values.items():
        if c != to and abs(c - to) <= REACH:
            term = table[min(c, to), abs(c - to)] * value
            result = term if result is None else result + term
    return 0.0 if result is None else -result


def slot_groups(slots):
    return [range(i, min(i + GROUP, slots)) for i in range(0, slots, GROUP)]


def if_live(count, group, work):
    if group[0] == 0:
        work()
    else:
        pl.when(group[0] < count)(work)


def inner_kernel(
    direction, count, residual_hbm, classes_hbm, smooth_hbm, sight_hbm, crossing_hbm, jac_hbm,
    begun, faced, norm, curved, rows, jac, crossing, classes, live, residual, smooth, sight, sems,
):
    pairs = (
        (classes_hbm, classes), (smooth_hbm, smooth), (sight_hbm, sight),
        (residual_hbm, residual), (crossing_hbm, crossing),
    )
    copies = [pltpu.make_async_copy(*pair, sems.at[i]) for i, pair in enumerate(pairs)]
    for copy in copies:
        copy.start()

    def load(group):
        part = pl.ds(group[0], len(group))
        return pltpu.make_async_copy(
            jac_hbm.at[part], jac.at[part], sems.at[len(pairs) + group[0] // GROUP]
        )

    for group in slot_groups(jac.shape[0]):
        if_live(count[0], group, lambda: load(group).start())
    live[0] = count[0]
    copies[0].wait()
    copies[1].wait()
    cols = direction.shape[0]
    rim = cols // 2
    table = coupling(classes, cols, range(-REACH, cols))
    weight = smooth[...][:, None, :]
    total = jnp.zeros(norm.shape, jnp.float32)
    values = {c: masked(direction[c]) for c in range(cols)}
    rests = {c: v - v.astype(jnp.bfloat16).astype(jnp.float32) for c, v in values.items()}
    for c in range(cols):
        centre = jnp.float32(1.0)
        for k in range(1, REACH + 1):
            centre = centre + (table[c, k] + table[c - k, k])
        result = weight * (centre * values[c] + pull(table, c, values))
        begun[rim + c] = result
        total = total + jnp.sum(values[c] * result, axis=0)
    low = {c: values[c] for c in range(rim)}
    high = {c: values[c] for c in range(rim, cols)}
    low_rests = {c: rests[c] for c in range(rim)}
    high_rests = {c: rests[c] for c in range(rim, cols)}
    for q in range(rim):
        facing = weight * pull(table, q - rim, high)
        faced[0, q] = facing
        begun[q] = facing + weight * pull(table, q - rim, low_rests)
        facing = weight * pull(table, q + cols, low)
        faced[1, q] = facing + weight * pull(table, q + cols, high)
        begun[rim + cols + q] = facing + weight * pull(table, q + cols, high_rests)
    curved[...] = total
    copies[2].wait()
    slot = lax.broadcasted_iota(jnp.int32, rows.shape, 0)
    rows[...] = jnp.where(slot < count[0], sight[...], 0.0)
    copies[3].wait()
    squares = jnp.zeros(norm.shape, jnp.float32)
    for c in range(cols):
        mres = masked(residual[c])
        squares = squares + jnp.sum(mres * mres, axis=0)
    norm[...] = squares
    copies[4].wait()
    for group in slot_groups(jac.shape[0]):
        if_live(count[0], group, lambda: load(group).wait())


def forward_kernel(
    crossing, live, rows, across, within, from_across, from_within, faced, norm, curved, jac,
    weighted, sums, window, total,
):
    slots, crossings = crossing.shape
    rim, species = across.shape[:2]
    span = rim * species
    odd = parity()
    places = (1 + odd, across), (2 - odd, within), (3 * odd, from_across), (3 - 3 * odd, from_within)
    for place, part in places:
        window[pl.ds(place * span, span)] = part[...].reshape(span, *part.shape[2:])
    edges = curved[...]
    for q in range(rim):
        for side, part in (odd, from_across), (1 - odd, from_within):
            edges = edges + 2.0 * jnp.sum(faced[side, q] * part[q].astype(jnp.float32), axis=0)
    total[...] = edges

    def project(group):
        added = jnp.zeros(total.shape, jnp.float32)
        for i in group:
            picked = jnp.concatenate([window[crossing[i, j]] for j in range(crossings)], axis=1)
            tiles = jnp.concatenate([jac[i, j] for j in range(crossings)], axis=1)
            integrals = lax.dot_general(
                picked, tiles, (((1,), (1,)), ((), ())), preferred_element_type=jnp.float32
            )
            product = (rows[pl.ds(i, 1), :] * integrals).astype(jnp.bfloat16)
            weighted[i] = product
            added = added + product.astype(jnp.float32) * integrals
        total[...] += added

    for group in slot_groups(slots):
        if_live(live[0], group, lambda: project(group))
    half = sums.shape[0]
    parts = [jnp.sum(x, axis=1, keepdims=True) for x in (norm[...], total[...])]
    parts = [part[h * half : (h + 1) * half] for h in range(2) for part in parts]
    lane = lax.broadcasted_iota(jnp.int32, sums.shape, 1)
    block = jnp.zeros(sums.shape, jnp.float32)
    for k, part in enumerate(parts):
        block = jnp.where(lane == k, part, block)
    sums[...] = block


def backward_kernel(
    crossing, classes, live, smooth, weighted, jac, begun, from_across, from_within,
    image, across, within, sums, near,
):
    slots, crossings = crossing.shape
    cols, species, probes, tile = image.shape
    rim = across.shape[0]
    span = rim * species
    odd = parity()
    near[odd] = from_across[...].astype(jnp.float32)
    near[1 - odd] = from_within[...].astype(jnp.float32)
    table = coupling(classes, cols, range(-rim, cols))
    weight = smooth[...][:, None, :]
    beside = {q - rim: near[0, q] for q in range(rim)} | {q + cols: near[1, q] for q in range(rim)}
    for c in range(cols):
        place = pl.ds(span + c * species, species)
        sums[place] = begun[rim + c] + weight * pull(table, c, beside)
    sums[pl.ds(0, span)] = begun[pl.ds(0, rim)].reshape(span, probes, tile)
    sums[pl.ds(3 * span, span)] = begun[pl.ds(rim + cols, rim)].reshape(span, probes, tile)

    def project(group):
        for i in group:
            tiles = jnp.concatenate([jac[i, j] for j in range(crossings)], axis=1)
            terms = jnp.dot(weighted[i], tiles, preferred_element_type=jnp.float32)
            for j in range(crossings):
                sums[crossing[i, j]] += terms[:, j * tile : (j + 1) * tile]

    for group in slot_groups(slots):
        if_live(live[0], group, lambda: project(group))
    for part, place in (across, 3 * odd), (within, 3 - 3 * odd):
        part[...] = sums[pl.ds(place * span, span)].astype(part.dtype).reshape(part.shape)
    image[...] = sums[pl.ds(span, 2 * span)].reshape(image.shape)


def final_kernel(
    solution, residual, direction, image, from_across, from_within, *rest
):
    *held, solution_next, residual_next, step_length = rest
    whole = tree_sum([part[...] for part in held])
    norm = jnp.concatenate([whole[:, 0:1], whole[:, 2:3]], axis=0)
    curvature = jnp.concatenate([whole[:, 1:2], whole[:, 3:4]], axis=0)
    step = norm / (curvature + EPSILON)
    rim = from_across.shape[0]
    wide = jnp.broadcast_to(step, direction.shape[2:])
    step_length[...] = jnp.transpose(wide)[0:1]
    wide = wide[None]
    odd = parity()
    for q in range(rim):
        for c, part in (odd * rim + q, from_across), ((1 - odd) * rim + q, from_within):
            total = masked(image[c] + part[q].astype(jnp.float32))
            solution_next[c] = masked(solution[c] + wide * direction[c])
            residual_next[c] = masked(residual[c]) - wide * total


def swapped_across(half):
    count = lax.axis_size("orbit")
    assert count % 2 == 0
    return lax.ppermute(half, "orbit", [(i, (i + 2 * (i % 2) - 1) % count) for i in range(count)])


def swapped_within(half):
    return lax.ppermute(half, "orbit", [(i, i ^ 1) for i in range(lax.axis_size("orbit"))])


def sum_steps(devices):
    assert devices >= 8 and devices & (devices - 1) == 0
    return [[1 << b] for b in range(1, devices.bit_length() - 2)] + [[1, devices // 2]]


def partners(array, bits):
    devices = range(lax.axis_size("orbit"))
    masks = [sum(bit for k, bit in enumerate(bits) if m >> k & 1) for m in range(1, 1 << len(bits))]
    found = {
        mask: lax.ppermute(array, "orbit", [(i, i ^ mask) for i in devices]) for mask in masks[::-1]
    }
    return [found[mask] for mask in masks[::-1]]


def tree_sum(parts):
    while len(parts) > 1:
        parts = [parts[k] + parts[k + 1] for k in range(0, len(parts), 2)]
    return parts[0]


def local(
    solution, residual, direction, jacobian, crossing, tile_count, sightline_weight,
    length_class, smooth_weight,
):
    cols, species, probes, width = direction.shape
    assert REACH <= cols
    rim = cols // 2
    slots = crossing.shape[0]
    f32, bf16 = jnp.float32, jnp.bfloat16
    shape = jax.ShapeDtypeStruct
    column = (species, probes, width)
    elements = direction.size
    dot_flops = 2 * jacobian.size * probes
    near = shape((rim,) + column, bf16)
    whole = shape(direction.shape, f32)
    small = shape((probes, width), f32)

    held, across, within = call(
        rounding_kernel,
        (whole, near, near),
        [HBM()],
        2 * elements,
        10 * elements,
        [pltpu.SemaphoreType.DMA((2,))],
    )(in_hbm(direction))
    from_across, from_within = swapped_across(across), swapped_within(within)

    begun, faced, norm, curved, rows, jac, crossing, length_class, live = call(
        inner_kernel,
        (
            shape((2 * cols,) + column, f32), shape((2, rim) + column, f32), small, small,
            shape(sightline_weight.shape, f32), shape(jacobian.shape, bf16),
            pltpu.SMEM(crossing.shape, jnp.int32), pltpu.SMEM(length_class.shape, jnp.int32),
            pltpu.SMEM((8,), jnp.int32),
        ),
        [VMEM(), SMEM()] + [HBM()] * 6,
        60 * elements,
        4 * jacobian.size,
        [
            pltpu.VMEM(direction.shape, f32),
            pltpu.VMEM(smooth_weight.shape, f32),
            pltpu.VMEM(sightline_weight.shape, f32),
            pltpu.SemaphoreType.DMA((5 + len(slot_groups(slots)),)),
        ],
        [VMEM()] * 6 + [SMEM()] * 3,
    )(
        held, tile_count,
        *map(in_hbm, (
            residual, length_class, smooth_weight, sightline_weight, crossing, jacobian,
        )),
    )

    devices = lax.axis_size("orbit")
    peers = devices // 2
    weighted, sums = call(
        forward_kernel,
        (shape((slots, probes, width), bf16), shape((probes // 2, width), f32)),
        [SMEM()] * 2 + [VMEM()] * 9,
        dot_flops,
        2 * jacobian.size,
        [pltpu.VMEM((2 * cols * species, probes, width), bf16), pltpu.VMEM((probes, width), f32)],
    )(crossing, live, rows, across, within, from_across, from_within, faced, norm, curved, jac)
    near_step, *far_steps = sum_steps(devices)
    held = [sums] + partners(sums, near_step)

    image, across, within = call(
        backward_kernel,
        (whole, near, near),
        [SMEM()] * 3 + [VMEM()] * 6,
        dot_flops,
        2 * jacobian.size,
        [
            pltpu.VMEM((2 * cols * species, probes, width), f32),
            pltpu.VMEM((2, rim) + column, f32),
        ],
    )(crossing, length_class, live, smooth_weight, weighted, jac, begun, from_across, from_within)
    from_across = swapped_across(across)
    within, *held = lax.optimization_barrier((within, *held))
    sums = tree_sum(held)
    held = [sums] + partners(sums, far_steps[0])
    within, *held = lax.optimization_barrier((within, *held))
    from_within = swapped_within(within)
    for step in far_steps[1:]:
        sums = tree_sum(held)
        held = [sums] + partners(sums, step)

    solution_next, residual_next, step_length = call(
        final_kernel,
        (whole, whole, shape((1, probes), f32)),
        [VMEM()] * (6 + len(held)),
        8 * elements,
        28 * elements,
    )(solution, residual, direction, image, from_across, from_within, *held)
    return solution_next, residual_next, step_length.reshape(probes)


def solution(mesh):
    wide = P(("grp", "orbit"), None, None, None)
    placed = (
        wide, wide, wide, wide,
        P(("grp", "orbit"), None),
        P(("grp", "orbit")),
        P(("grp", "orbit"), None),
        P("grp"),
        P(),
    )
    return jax.shard_map(
        local, mesh=mesh, in_specs=placed, out_specs=(wide, wide, P("grp")), check_vma=False
    )
```

```python
import functools

import jax
import jax.numpy as jnp
from jax import lax
from jax.experimental import pallas as pl
from jax.experimental.pallas import tpu as pltpu
from jax.sharding import PartitionSpec as P

LEVELS = 120
CLASSES = 4
REACH = 8
EPSILON = 1e-06
GROUP = 2
VMEM_LIMIT = 24 * 1024 * 1024

SMEM = functools.partial(pl.BlockSpec, memory_space=pltpu.SMEM)
VMEM = functools.partial(pl.BlockSpec, memory_space=pltpu.VMEM)
HBM = functools.partial(pl.BlockSpec, memory_space=pltpu.HBM)


def in_hbm(array):
    return pltpu.with_memory_space_constraint(array, pltpu.HBM)


def live_lanes(shape):
    return lax.broadcasted_iota(jnp.int32, shape, len(shape) - 1) < LEVELS


def masked(values):
    return jnp.where(live_lanes(values.shape), values, 0.0)


def call(kernel, out_shape, in_specs, flops, moved, scratch=(), out_specs=None):
    return pl.pallas_call(
        kernel,
        out_shape=out_shape,
        in_specs=in_specs,
        out_specs=tuple(out_specs or [VMEM()] * len(out_shape)),
        scratch_shapes=list(scratch),
        compiler_params=pltpu.CompilerParams(vmem_limit_bytes=VMEM_LIMIT),
        cost_estimate=pl.CostEstimate(flops=flops, bytes_accessed=moved, transcendentals=0),
    )


def parity():
    return lax.rem(lax.axis_index("orbit"), 2)


def rounding_kernel(leaves, direction_hbm, direction, half, sem):
    rim = half.shape[0]
    place = pl.ds((parity() if leaves else 1 - parity()) * rim, rim)
    copy = pltpu.make_async_copy(direction_hbm.at[place], direction, sem)
    copy.start()
    copy.wait()
    half[...] = masked(direction[...]).astype(jnp.bfloat16)


def coupling(classes, cols, columns):
    total = classes.shape[0]
    first = lax.axis_index("orbit") * cols
    table = {}
    for c in columns:
        length = (classes[lax.rem(first + c + total, total)] + 1) * REACH // CLASSES
        for k in range(1, REACH + 1):
            table[c, k] = jnp.where(k <= length, jnp.float32(1.0 / (k * k)), jnp.float32(0.0))
    return table


def pull(table, to, values):
    result = None
    for c, value in values.items():
        if c != to and abs(c - to) <= REACH:
            term = table[min(c, to), abs(c - to)] * value
            result = term if result is None else result + term
    return 0.0 if result is None else -result


def slot_groups(slots):
    return [range(i, min(i + GROUP, slots)) for i in range(0, slots, GROUP)]


def if_live(count, group, work):
    if group[0] == 0:
        work()
    else:
        pl.when(group[0] < count)(work)


def inner_kernel(
    leaving, staying, count, residual_hbm, classes_hbm, smooth_hbm, sight_hbm, crossing_hbm, jac_hbm,
    begun, faced, norm, curved, rows, jac, crossing, classes, live,
    direction, residual, smooth, sight, sems,
):
    pairs = (
        (classes_hbm, classes), (smooth_hbm, smooth), (sight_hbm, sight),
        (residual_hbm, residual), (crossing_hbm, crossing),
    )
    copies = [pltpu.make_async_copy(*pair, sems.at[i]) for i, pair in enumerate(pairs)]
    for copy in copies:
        copy.start()

    def load(group):
        part = pl.ds(group[0], len(group))
        return pltpu.make_async_copy(
            jac_hbm.at[part], jac.at[part], sems.at[len(pairs) + group[0] // GROUP]
        )

    for group in slot_groups(jac.shape[0]):
        if_live(count[0], group, lambda: load(group).start())
    live[0] = count[0]
    copies[0].wait()
    copies[1].wait()
    rim = leaving.shape[0]
    cols = 2 * rim
    odd = parity()
    direction[pl.ds(odd * rim, rim)] = leaving[...]
    direction[pl.ds((1 - odd) * rim, rim)] = staying[...]
    table = coupling(classes, cols, range(-REACH, cols))
    weight = smooth[...][:, None, :]
    total = jnp.zeros(norm.shape, jnp.float32)
    values = {c: masked(direction[c]) for c in range(cols)}
    rests = {c: v - v.astype(jnp.bfloat16).astype(jnp.float32) for c, v in values.items()}
    for c in range(cols):
        centre = jnp.float32(1.0)
        for k in range(1, REACH + 1):
            centre = centre + (table[c, k] + table[c - k, k])
        result = weight * (centre * values[c] + pull(table, c, values))
        begun[rim + c] = result
        total = total + jnp.sum(values[c] * result, axis=0)
    low = {c: values[c] for c in range(rim)}
    high = {c: values[c] for c in range(rim, cols)}
    low_rests = {c: rests[c] for c in range(rim)}
    high_rests = {c: rests[c] for c in range(rim, cols)}
    for q in range(rim):
        facing = weight * pull(table, q - rim, high)
        faced[0, q] = facing
        begun[q] = facing + weight * pull(table, q - rim, low_rests)
        facing = weight * pull(table, q + cols, low)
        faced[1, q] = facing + weight * pull(table, q + cols, high)
        begun[rim + cols + q] = facing + weight * pull(table, q + cols, high_rests)
    curved[...] = total
    copies[2].wait()
    slot = lax.broadcasted_iota(jnp.int32, rows.shape, 0)
    rows[...] = jnp.where(slot < count[0], sight[...], 0.0)
    copies[3].wait()
    squares = jnp.zeros(norm.shape, jnp.float32)
    for c in range(cols):
        mres = masked(residual[c])
        squares = squares + jnp.sum(mres * mres, axis=0)
    norm[...] = squares
    copies[4].wait()
    for group in slot_groups(jac.shape[0]):
        if_live(count[0], group, lambda: load(group).wait())


def forward_kernel(
    crossing, live, rows, across, within, from_across, from_within, faced, norm, curved, jac,
    weighted, sums, window, total,
):
    slots, crossings = crossing.shape
    rim, species = across.shape[:2]
    span = rim * species
    odd = parity()
    places = (1 + odd, across), (2 - odd, within), (3 * odd, from_across), (3 - 3 * odd, from_within)
    for place, part in places:
        window[pl.ds(place * span, span)] = part[...].reshape(span, *part.shape[2:])
    edges = curved[...]
    for q in range(rim):
        for side, part in (odd, from_across), (1 - odd, from_within):
            edges = edges + 2.0 * jnp.sum(faced[side, q] * part[q].astype(jnp.float32), axis=0)
    total[...] = edges

    def project(group):
        added = jnp.zeros(total.shape, jnp.float32)
        for i in group:
            picked = jnp.concatenate([window[crossing[i, j]] for j in range(crossings)], axis=1)
            tiles = jnp.concatenate([jac[i, j] for j in range(crossings)], axis=1)
            integrals = lax.dot_general(
                picked, tiles, (((1,), (1,)), ((), ())), preferred_element_type=jnp.float32
            )
            product = (rows[pl.ds(i, 1), :] * integrals).astype(jnp.bfloat16)
            weighted[i] = product
            added = added + product.astype(jnp.float32) * integrals
        total[...] += added

    for group in slot_groups(slots):
        if_live(live[0], group, lambda: project(group))
    half = sums.shape[0]
    parts = [jnp.sum(x, axis=1, keepdims=True) for x in (norm[...], total[...])]
    parts = [part[h * half : (h + 1) * half] for h in range(2) for part in parts]
    lane = lax.broadcasted_iota(jnp.int32, sums.shape, 1)
    block = jnp.zeros(sums.shape, jnp.float32)
    for k, part in enumerate(parts):
        block = jnp.where(lane == k, part, block)
    sums[...] = block


def backward_kernel(
    crossing, classes, live, smooth, weighted, jac, begun, from_across, from_within,
    image, across, within, sums, near,
):
    slots, crossings = crossing.shape
    cols, species, probes, tile = image.shape
    rim = across.shape[0]
    span = rim * species
    odd = parity()
    near[odd] = from_across[...].astype(jnp.float32)
    near[1 - odd] = from_within[...].astype(jnp.float32)
    table = coupling(classes, cols, range(-rim, cols))
    weight = smooth[...][:, None, :]
    beside = {q - rim: near[0, q] for q in range(rim)} | {q + cols: near[1, q] for q in range(rim)}
    for c in range(cols):
        place = pl.ds(span + c * species, species)
        sums[place] = begun[rim + c] + weight * pull(table, c, beside)
    sums[pl.ds(0, span)] = begun[pl.ds(0, rim)].reshape(span, probes, tile)
    sums[pl.ds(3 * span, span)] = begun[pl.ds(rim + cols, rim)].reshape(span, probes, tile)

    def project(group):
        for i in group:
            tiles = jnp.concatenate([jac[i, j] for j in range(crossings)], axis=1)
            terms = jnp.dot(weighted[i], tiles, preferred_element_type=jnp.float32)
            for j in range(crossings):
                sums[crossing[i, j]] += terms[:, j * tile : (j + 1) * tile]

    for group in slot_groups(slots):
        if_live(live[0], group, lambda: project(group))
    for part, place in (across, 3 * odd), (within, 3 - 3 * odd):
        part[...] = sums[pl.ds(place * span, span)].astype(part.dtype).reshape(part.shape)
    image[...] = sums[pl.ds(span, 2 * span)].reshape(image.shape)


def final_kernel(
    solution, residual, direction, image, from_across, from_within, *rest
):
    *held, solution_next, residual_next, step_length = rest
    whole = tree_sum([part[...] for part in held])
    norm = jnp.concatenate([whole[:, 0:1], whole[:, 2:3]], axis=0)
    curvature = jnp.concatenate([whole[:, 1:2], whole[:, 3:4]], axis=0)
    step = norm / (curvature + EPSILON)
    rim = from_across.shape[0]
    wide = jnp.broadcast_to(step, direction.shape[2:])
    step_length[...] = jnp.transpose(wide)[0:1]
    wide = wide[None]
    odd = parity()
    for q in range(rim):
        for c, part in (odd * rim + q, from_across), ((1 - odd) * rim + q, from_within):
            total = masked(image[c] + part[q].astype(jnp.float32))
            solution_next[c] = masked(solution[c] + wide * direction[c])
            residual_next[c] = masked(residual[c]) - wide * total


def swapped_across(half):
    count = lax.axis_size("orbit")
    assert count % 2 == 0
    return lax.ppermute(half, "orbit", [(i, (i + 2 * (i % 2) - 1) % count) for i in range(count)])


def swapped_within(half):
    return lax.ppermute(half, "orbit", [(i, i ^ 1) for i in range(lax.axis_size("orbit"))])


def sum_steps(devices):
    assert devices >= 8 and devices & (devices - 1) == 0
    return [[1 << b] for b in range(1, devices.bit_length() - 2)] + [[1, devices // 2]]


def partners(array, bits):
    devices = range(lax.axis_size("orbit"))
    masks = [sum(bit for k, bit in enumerate(bits) if m >> k & 1) for m in range(1, 1 << len(bits))]
    found = {
        mask: lax.ppermute(array, "orbit", [(i, i ^ mask) for i in devices]) for mask in masks[::-1]
    }
    return [found[mask] for mask in masks[::-1]]


def tree_sum(parts):
    while len(parts) > 1:
        parts = [parts[k] + parts[k + 1] for k in range(0, len(parts), 2)]
    return parts[0]


def local(
    solution, residual, direction, jacobian, crossing, tile_count, sightline_weight,
    length_class, smooth_weight,
):
    cols, species, probes, width = direction.shape
    assert REACH <= cols
    rim = cols // 2
    slots = crossing.shape[0]
    f32, bf16 = jnp.float32, jnp.bfloat16
    shape = jax.ShapeDtypeStruct
    column = (species, probes, width)
    elements = direction.size
    dot_flops = 2 * jacobian.size * probes
    near = shape((rim,) + column, bf16)
    whole = shape(direction.shape, f32)
    small = shape((probes, width), f32)

    halves = [
        call(
            functools.partial(rounding_kernel, leaves),
            (shape(near.shape, f32), near),
            [HBM()],
            elements,
            5 * elements,
            [pltpu.SemaphoreType.DMA],
        )(in_hbm(direction))
        for leaves in (True, False)
    ]
    (leaving, across), (staying, within) = halves
    from_across, from_within = swapped_across(across), swapped_within(within)

    begun, faced, norm, curved, rows, jac, crossing, length_class, live = call(
        inner_kernel,
        (
            shape((2 * cols,) + column, f32), shape((2, rim) + column, f32), small, small,
            shape(sightline_weight.shape, f32), shape(jacobian.shape, bf16),
            pltpu.SMEM(crossing.shape, jnp.int32), pltpu.SMEM(length_class.shape, jnp.int32),
            pltpu.SMEM((8,), jnp.int32),
        ),
        [VMEM(), VMEM(), SMEM()] + [HBM()] * 6,
        60 * elements,
        4 * jacobian.size,
        [
            pltpu.VMEM(direction.shape, f32),
            pltpu.VMEM(direction.shape, f32),
            pltpu.VMEM(smooth_weight.shape, f32),
            pltpu.VMEM(sightline_weight.shape, f32),
            pltpu.SemaphoreType.DMA((5 + len(slot_groups(slots)),)),
        ],
        [VMEM()] * 6 + [SMEM()] * 3,
    )(
        leaving, staying, tile_count,
        *map(in_hbm, (
            residual, length_class, smooth_weight, sightline_weight, crossing, jacobian,
        )),
    )

    devices = lax.axis_size("orbit")
    peers = devices // 2
    weighted, sums = call(
        forward_kernel,
        (shape((slots, probes, width), bf16), shape((probes // 2, width), f32)),
        [SMEM()] * 2 + [VMEM()] * 9,
        dot_flops,
        2 * jacobian.size,
        [pltpu.VMEM((2 * cols * species, probes, width), bf16), pltpu.VMEM((probes, width), f32)],
    )(crossing, live, rows, across, within, from_across, from_within, faced, norm, curved, jac)
    near_step, *far_steps = sum_steps(devices)
    held = [sums] + partners(sums, near_step)

    image, across, within = call(
        backward_kernel,
        (whole, near, near),
        [SMEM()] * 3 + [VMEM()] * 6,
        dot_flops,
        2 * jacobian.size,
        [
            pltpu.VMEM((2 * cols * species, probes, width), f32),
            pltpu.VMEM((2, rim) + column, f32),
        ],
    )(crossing, length_class, live, smooth_weight, weighted, jac, begun, from_across, from_within)
    from_across = swapped_across(across)
    within, *held = lax.optimization_barrier((within, *held))
    sums = tree_sum(held)
    held = [sums] + partners(sums, far_steps[0])
    from_within = swapped_within(within)
    for step in far_steps[1:]:
        sums = tree_sum(held)
        held = [sums] + partners(sums, step)

    solution_next, residual_next, step_length = call(
        final_kernel,
        (whole, whole, shape((1, probes), f32)),
        [VMEM()] * (6 + len(held)),
        8 * elements,
        28 * elements,
    )(solution, residual, direction, image, from_across, from_within, *held)
    return solution_next, residual_next, step_length.reshape(probes)


def solution(mesh):
    wide = P(("grp", "orbit"), None, None, None)
    placed = (
        wide, wide, wide, wide,
        P(("grp", "orbit"), None),
        P(("grp", "orbit")),
        P(("grp", "orbit"), None),
        P("grp"),
        P(),
    )
    return jax.shard_map(
        local, mesh=mesh, in_specs=placed, out_specs=(wide, wide, P("grp")), check_vma=False
    )
```

```python
import functools

import jax
import jax.numpy as jnp
from jax import lax
from jax.experimental import pallas as pl
from jax.experimental.pallas import tpu as pltpu
from jax.sharding import PartitionSpec as P

LEVELS = 120
CLASSES = 4
REACH = 8
EPSILON = 1e-06
GROUP = 2
VMEM_LIMIT = 24 * 1024 * 1024

SMEM = functools.partial(pl.BlockSpec, memory_space=pltpu.SMEM)
VMEM = functools.partial(pl.BlockSpec, memory_space=pltpu.VMEM)
HBM = functools.partial(pl.BlockSpec, memory_space=pltpu.HBM)


def in_hbm(array):
    return pltpu.with_memory_space_constraint(array, pltpu.HBM)


def live_lanes(shape):
    return lax.broadcasted_iota(jnp.int32, shape, len(shape) - 1) < LEVELS


def masked(values):
    return jnp.where(live_lanes(values.shape), values, 0.0)


def call(kernel, out_shape, in_specs, flops, moved, scratch=(), out_specs=None):
    return pl.pallas_call(
        kernel,
        out_shape=out_shape,
        in_specs=in_specs,
        out_specs=tuple(out_specs or [VMEM()] * len(out_shape)),
        scratch_shapes=list(scratch),
        compiler_params=pltpu.CompilerParams(vmem_limit_bytes=VMEM_LIMIT),
        cost_estimate=pl.CostEstimate(flops=flops, bytes_accessed=moved, transcendentals=0),
    )


def parity():
    return lax.rem(lax.axis_index("orbit"), 2)


def rounding_kernel(direction_hbm, direction, across, within, sems):
    rim = across.shape[0]
    odd = parity()
    halves = ((odd, across), (1 - odd, within))
    copies = []
    for k, (place, _) in enumerate(halves):
        half = pl.ds(place * rim, rim)
        copies.append(
            pltpu.make_async_copy(direction_hbm.at[half], direction.at[half], sems.at[k])
        )
        copies[-1].start()
    for copy, (place, half) in zip(copies, halves):
        copy.wait()
        for c in range(rim):
            half[c] = masked(direction[place * rim + c]).astype(jnp.bfloat16)


def coupling(classes, cols, columns):
    total = classes.shape[0]
    first = lax.axis_index("orbit") * cols
    table = {}
    for c in columns:
        length = (classes[lax.rem(first + c + total, total)] + 1) * REACH // CLASSES
        for k in range(1, REACH + 1):
            table[c, k] = jnp.where(k <= length, jnp.float32(1.0 / (k * k)), jnp.float32(0.0))
    return table


def pull(table, to, values):
    result = None
    for c, value in values.items():
        if c != to and abs(c - to) <= REACH:
            term = table[min(c, to), abs(c - to)] * value
            result = term if result is None else result + term
    return 0.0 if result is None else -result


def slot_groups(slots):
    return [range(i, min(i + GROUP, slots)) for i in range(0, slots, GROUP)]


def early_slots(slots):
    return slot_groups(slots)[-1][0] if slots > GROUP else slots


def slot_tiles(jac, late, i):
    part, row = (jac, i) if i < jac.shape[0] else (late, i - jac.shape[0])
    return jnp.concatenate([part[row, j] for j in range(part.shape[1])], axis=1)


def if_live(count, group, work):
    if group[0] == 0:
        work()
    else:
        pl.when(group[0] < count)(work)


def inner_kernel(
    direction, count, residual_hbm, classes_hbm, smooth_hbm, sight_hbm, crossing_hbm, jac_hbm,
    begun, faced, norm, curved, rows, jac, crossing, classes, live, residual, smooth, sight, sems,
):
    pairs = (
        (classes_hbm, classes), (smooth_hbm, smooth), (sight_hbm, sight),
        (residual_hbm, residual), (crossing_hbm, crossing),
    )
    copies = [pltpu.make_async_copy(*pair, sems.at[i]) for i, pair in enumerate(pairs)]
    for copy in copies:
        copy.start()

    def load(group):
        part = pl.ds(group[0], len(group))
        return pltpu.make_async_copy(
            jac_hbm.at[part], jac.at[part], sems.at[len(pairs) + group[0] // GROUP]
        )

    early = slot_groups(jac.shape[0])
    for group in early:
        if_live(count[0], group, lambda: load(group).start())
    live[0] = count[0]
    copies[0].wait()
    copies[1].wait()
    cols = direction.shape[0]
    rim = cols // 2
    table = coupling(classes, cols, range(-REACH, cols))
    weight = smooth[...][:, None, :]
    total = jnp.zeros(norm.shape, jnp.float32)
    values = {c: masked(direction[c]) for c in range(cols)}
    rests = {c: v - v.astype(jnp.bfloat16).astype(jnp.float32) for c, v in values.items()}
    for c in range(cols):
        centre = jnp.float32(1.0)
        for k in range(1, REACH + 1):
            centre = centre + (table[c, k] + table[c - k, k])
        result = weight * (centre * values[c] + pull(table, c, values))
        begun[rim + c] = result
        total = total + jnp.sum(values[c] * result, axis=0)
    low = {c: values[c] for c in range(rim)}
    high = {c: values[c] for c in range(rim, cols)}
    low_rests = {c: rests[c] for c in range(rim)}
    high_rests = {c: rests[c] for c in range(rim, cols)}
    for q in range(rim):
        facing = weight * pull(table, q - rim, high)
        faced[0, q] = facing
        begun[q] = facing + weight * pull(table, q - rim, low_rests)
        facing = weight * pull(table, q + cols, low)
        faced[1, q] = facing + weight * pull(table, q + cols, high)
        begun[rim + cols + q] = facing + weight * pull(table, q + cols, high_rests)
    curved[...] = total
    copies[2].wait()
    slot = lax.broadcasted_iota(jnp.int32, rows.shape, 0)
    rows[...] = jnp.where(slot < count[0], sight[...], 0.0)
    copies[3].wait()
    squares = jnp.zeros(norm.shape, jnp.float32)
    for c in range(cols):
        mres = masked(residual[c])
        squares = squares + jnp.sum(mres * mres, axis=0)
    norm[...] = squares
    copies[4].wait()
    for group in early:
        if_live(count[0], group, lambda: load(group).wait())


def forward_kernel(
    crossing, live, rows, across, within, from_across, from_within, faced, norm, curved, jac, jac_hbm,
    weighted, sums, late, window, total, sem,
):
    slots, crossings = crossing.shape
    last = slot_groups(slots)[-1]
    load = pltpu.make_async_copy(jac_hbm.at[pl.ds(last[0], len(last))], late, sem)
    if_live(live[0], last, load.start)
    rim, species = across.shape[:2]
    span = rim * species
    odd = parity()
    places = (1 + odd, across), (2 - odd, within), (3 * odd, from_across), (3 - 3 * odd, from_within)
    for place, part in places:
        window[pl.ds(place * span, span)] = part[...].reshape(span, *part.shape[2:])
    edges = curved[...]
    for q in range(rim):
        for side, part in (odd, from_across), (1 - odd, from_within):
            edges = edges + 2.0 * jnp.sum(faced[side, q] * part[q].astype(jnp.float32), axis=0)
    total[...] = edges

    def project(group):
        if group == last:
            load.wait()
        added = jnp.zeros(total.shape, jnp.float32)
        for i in group:
            picked = jnp.concatenate([window[crossing[i, j]] for j in range(crossings)], axis=1)
            tiles = slot_tiles(jac, late, i)
            integrals = lax.dot_general(
                picked, tiles, (((1,), (1,)), ((), ())), preferred_element_type=jnp.float32
            )
            product = (rows[pl.ds(i, 1), :] * integrals).astype(jnp.bfloat16)
            weighted[i] = product
            added = added + product.astype(jnp.float32) * integrals
        total[...] += added

    for group in slot_groups(slots):
        if_live(live[0], group, lambda: project(group))
    half = sums.shape[0]
    parts = [jnp.sum(x, axis=1, keepdims=True) for x in (norm[...], total[...])]
    parts = [part[h * half : (h + 1) * half] for h in range(2) for part in parts]
    lane = lax.broadcasted_iota(jnp.int32, sums.shape, 1)
    block = jnp.zeros(sums.shape, jnp.float32)
    for k, part in enumerate(parts):
        block = jnp.where(lane == k, part, block)
    sums[...] = block


def backward_kernel(
    crossing, classes, live, smooth, weighted, jac, late, begun, from_across, from_within,
    image, across, within, sums, near,
):
    slots, crossings = crossing.shape
    cols, species, probes, tile = image.shape
    rim = across.shape[0]
    span = rim * species
    odd = parity()
    near[odd] = from_across[...].astype(jnp.float32)
    near[1 - odd] = from_within[...].astype(jnp.float32)
    table = coupling(classes, cols, range(-rim, cols))
    weight = smooth[...][:, None, :]
    beside = {q - rim: near[0, q] for q in range(rim)} | {q + cols: near[1, q] for q in range(rim)}
    for c in range(cols):
        place = pl.ds(span + c * species, species)
        sums[place] = begun[rim + c] + weight * pull(table, c, beside)
    sums[pl.ds(0, span)] = begun[pl.ds(0, rim)].reshape(span, probes, tile)
    sums[pl.ds(3 * span, span)] = begun[pl.ds(rim + cols, rim)].reshape(span, probes, tile)

    def project(group):
        for i in group:
            tiles = slot_tiles(jac, late, i)
            terms = jnp.dot(weighted[i], tiles, preferred_element_type=jnp.float32)
            for j in range(crossings):
                sums[crossing[i, j]] += terms[:, j * tile : (j + 1) * tile]

    for group in slot_groups(slots):
        if_live(live[0], group, lambda: project(group))
    for part, place in (across, 3 * odd), (within, 3 - 3 * odd):
        part[...] = sums[pl.ds(place * span, span)].astype(part.dtype).reshape(part.shape)
    image[...] = sums[pl.ds(span, 2 * span)].reshape(image.shape)


def final_kernel(
    solution, residual, direction, image, from_across, from_within, *rest
):
    *held, solution_out, residual_out, step_length, solution_next, residual_next, sems = rest
    whole = tree_sum([part[...] for part in held])
    norm = jnp.concatenate([whole[:, 0:1], whole[:, 2:3]], axis=0)
    curvature = jnp.concatenate([whole[:, 1:2], whole[:, 3:4]], axis=0)
    step = norm / (curvature + EPSILON)
    rim = from_across.shape[0]
    wide = jnp.broadcast_to(step, direction.shape[2:])
    step_length[...] = jnp.transpose(wide)[0:1]
    wide = wide[None]
    odd = parity()
    copies = [
        pltpu.make_async_copy(solution_next, solution_out, sems.at[0]),
        pltpu.make_async_copy(residual_next, residual_out, sems.at[1]),
    ]
    for c in range(2 * rim):
        solution_next[c] = masked(solution[c] + wide * direction[c])
    copies[0].start()
    for q in range(rim):
        for c, part in (odd * rim + q, from_across), ((1 - odd) * rim + q, from_within):
            total = masked(image[c] + part[q].astype(jnp.float32))
            residual_next[c] = masked(residual[c]) - wide * total
    copies[1].start()
    for copy in copies:
        copy.wait()


def swapped_across(half):
    count = lax.axis_size("orbit")
    assert count % 2 == 0
    return lax.ppermute(half, "orbit", [(i, (i + 2 * (i % 2) - 1) % count) for i in range(count)])


def swapped_within(half):
    return lax.ppermute(half, "orbit", [(i, i ^ 1) for i in range(lax.axis_size("orbit"))])


def sum_steps(devices):
    assert devices >= 8 and devices & (devices - 1) == 0
    return [[1 << b] for b in range(1, devices.bit_length() - 2)] + [[1, devices // 2]]


def partners(array, bits):
    devices = range(lax.axis_size("orbit"))
    masks = [sum(bit for k, bit in enumerate(bits) if m >> k & 1) for m in range(1, 1 << len(bits))]
    found = {
        mask: lax.ppermute(array, "orbit", [(i, i ^ mask) for i in devices]) for mask in masks[::-1]
    }
    return [found[mask] for mask in masks]


def tree_sum(parts):
    while len(parts) > 1:
        parts = [parts[k] + parts[k + 1] for k in range(0, len(parts), 2)]
    return parts[0]


def local(
    solution, residual, direction, jacobian, crossing, tile_count, sightline_weight,
    length_class, smooth_weight,
):
    cols, species, probes, width = direction.shape
    assert REACH <= cols
    rim = cols // 2
    slots = crossing.shape[0]
    early = early_slots(slots)
    f32, bf16 = jnp.float32, jnp.bfloat16
    shape = jax.ShapeDtypeStruct
    column = (species, probes, width)
    elements = direction.size
    dot_flops = 2 * jacobian.size * probes
    near = shape((rim,) + column, bf16)
    whole = shape(direction.shape, f32)
    small = shape((probes, width), f32)

    held, across, within = call(
        rounding_kernel,
        (whole, near, near),
        [HBM()],
        2 * elements,
        10 * elements,
        [pltpu.SemaphoreType.DMA((2,))],
    )(in_hbm(direction))
    from_across, from_within = swapped_across(across), swapped_within(within)

    begun, faced, norm, curved, rows, jac, crossing, length_class, live = call(
        inner_kernel,
        (
            shape((2 * cols,) + column, f32), shape((2, rim) + column, f32), small, small,
            shape(sightline_weight.shape, f32), shape((early,) + jacobian.shape[1:], bf16),
            pltpu.SMEM(crossing.shape, jnp.int32), pltpu.SMEM(length_class.shape, jnp.int32),
            pltpu.SMEM((8,), jnp.int32),
        ),
        [VMEM(), SMEM()] + [HBM()] * 6,
        60 * elements,
        4 * jacobian.size,
        [
            pltpu.VMEM(direction.shape, f32),
            pltpu.VMEM(smooth_weight.shape, f32),
            pltpu.VMEM(sightline_weight.shape, f32),
            pltpu.SemaphoreType.DMA((5 + len(slot_groups(early)),)),
        ],
        [VMEM()] * 6 + [SMEM()] * 3,
    )(
        held, tile_count,
        *map(in_hbm, (
            residual, length_class, smooth_weight, sightline_weight, crossing, jacobian,
        )),
    )

    devices = lax.axis_size("orbit")
    peers = devices // 2
    weighted, sums, late = call(
        forward_kernel,
        (
            shape((slots, probes, width), bf16), shape((probes // 2, width), f32),
            shape((slots - early,) + jacobian.shape[1:], bf16),
        ),
        [SMEM()] * 2 + [VMEM()] * 9 + [HBM()],
        dot_flops,
        2 * jacobian.size,
        [
            pltpu.VMEM((2 * cols * species, probes, width), bf16),
            pltpu.VMEM((probes, width), f32),
            pltpu.SemaphoreType.DMA,
        ],
    )(
        crossing, live, rows, across, within, from_across, from_within, faced, norm, curved, jac,
        in_hbm(jacobian),
    )
    near_step, *far_steps = sum_steps(devices)
    held = [sums] + partners(sums, near_step)

    image, across, within = call(
        backward_kernel,
        (whole, near, near),
        [SMEM()] * 3 + [VMEM()] * 7,
        dot_flops,
        2 * jacobian.size,
        [
            pltpu.VMEM((2 * cols * species, probes, width), f32),
            pltpu.VMEM((2, rim) + column, f32),
        ],
    )(crossing, length_class, live, smooth_weight, weighted, jac, late, begun, from_across, from_within)
    from_across = swapped_across(across)
    within, *held = lax.optimization_barrier((within, *held))
    sums = tree_sum(held)
    held = [sums] + partners(sums, far_steps[0])
    within, *held = lax.optimization_barrier((within, *held))
    from_within = swapped_within(within)
    for step in far_steps[1:]:
        sums = tree_sum(held)
        held = [sums] + partners(sums, step)

    solution_next, residual_next, step_length = call(
        final_kernel,
        (whole, whole, shape((1, probes), f32)),
        [VMEM()] * (6 + len(held)),
        8 * elements,
        28 * elements,
        [pltpu.VMEM(direction.shape, f32)] * 2 + [pltpu.SemaphoreType.DMA((2,))],
        [HBM()] * 2 + [VMEM()],
    )(solution, residual, direction, image, from_across, from_within, *held)
    return solution_next, residual_next, step_length.reshape(probes)


def solution(mesh):
    wide = P(("grp", "orbit"), None, None, None)
    placed = (
        wide, wide, wide, wide,
        P(("grp", "orbit"), None),
        P(("grp", "orbit")),
        P(("grp", "orbit"), None),
        P("grp"),
        P(),
    )
    return jax.shard_map(
        local, mesh=mesh, in_specs=placed, out_specs=(wide, wide, P("grp")), check_vma=False
    )
```

```python
import functools

import jax
import jax.numpy as jnp
from jax import lax
from jax.experimental import pallas as pl
from jax.experimental.pallas import tpu as pltpu
from jax.sharding import PartitionSpec as P

LEVELS = 120
CLASSES = 4
REACH = 8
EPSILON = 1e-06
GROUP = 2
VMEM_LIMIT = 24 * 1024 * 1024

SMEM = functools.partial(pl.BlockSpec, memory_space=pltpu.SMEM)
VMEM = functools.partial(pl.BlockSpec, memory_space=pltpu.VMEM)
HBM = functools.partial(pl.BlockSpec, memory_space=pltpu.HBM)


def in_hbm(array):
    return pltpu.with_memory_space_constraint(array, pltpu.HBM)


def live_lanes(shape):
    return lax.broadcasted_iota(jnp.int32, shape, len(shape) - 1) < LEVELS


def masked(values):
    return jnp.where(live_lanes(values.shape), values, 0.0)


def call(kernel, out_shape, in_specs, flops, moved, scratch=(), out_specs=None):
    return pl.pallas_call(
        kernel,
        out_shape=out_shape,
        in_specs=in_specs,
        out_specs=tuple(out_specs or [VMEM()] * len(out_shape)),
        scratch_shapes=list(scratch),
        compiler_params=pltpu.CompilerParams(vmem_limit_bytes=VMEM_LIMIT),
        cost_estimate=pl.CostEstimate(flops=flops, bytes_accessed=moved, transcendentals=0),
    )


def parity():
    return lax.rem(lax.axis_index("orbit"), 2)


def rounding_kernel(direction_hbm, direction, across, within, sems):
    rim = across.shape[0]
    odd = parity()
    halves = ((odd, across), (1 - odd, within))
    copies = []
    for k, (place, _) in enumerate(halves):
        half = pl.ds(place * rim, rim)
        copies.append(
            pltpu.make_async_copy(direction_hbm.at[half], direction.at[half], sems.at[k])
        )
        copies[-1].start()
    for copy, (place, half) in zip(copies, halves):
        copy.wait()
        for c in range(rim):
            half[c] = masked(direction[place * rim + c]).astype(jnp.bfloat16)


def coupling(classes, cols, columns):
    total = classes.shape[0]
    first = lax.axis_index("orbit") * cols
    table = {}
    for c in columns:
        length = (classes[lax.rem(first + c + total, total)] + 1) * REACH // CLASSES
        for k in range(1, REACH + 1):
            table[c, k] = jnp.where(k <= length, jnp.float32(1.0 / (k * k)), jnp.float32(0.0))
    return table


def pull(table, to, values):
    result = None
    for c, value in values.items():
        if c != to and abs(c - to) <= REACH:
            term = table[min(c, to), abs(c - to)] * value
            result = term if result is None else result + term
    return 0.0 if result is None else -result


def slot_groups(slots):
    return [range(i, min(i + GROUP, slots)) for i in range(0, slots, GROUP)]


def early_slots(slots):
    return slot_groups(slots)[-1][0] if slots > GROUP else slots


def slot_tiles(jac, late, i):
    part, row = (jac, i) if i < jac.shape[0] else (late, i - jac.shape[0])
    return jnp.concatenate([part[row, j] for j in range(part.shape[1])], axis=1)


def if_live(count, group, work):
    if group[0] == 0:
        work()
    else:
        pl.when(group[0] < count)(work)


def inner_kernel(
    direction, count, residual_hbm, classes_hbm, smooth_hbm, sight_hbm, crossing_hbm, jac_hbm,
    begun, faced, norm, curved, rows, jac, crossing, classes, live, residual, smooth, sight, sems,
):
    pairs = (
        (classes_hbm, classes), (smooth_hbm, smooth), (sight_hbm, sight),
        (residual_hbm, residual), (crossing_hbm, crossing),
    )
    copies = [pltpu.make_async_copy(*pair, sems.at[i]) for i, pair in enumerate(pairs)]
    for copy in copies:
        copy.start()

    def load(group):
        part = pl.ds(group[0], len(group))
        return pltpu.make_async_copy(
            jac_hbm.at[part], jac.at[part], sems.at[len(pairs) + group[0] // GROUP]
        )

    early = slot_groups(jac.shape[0])
    for group in early:
        if_live(count[0], group, lambda: load(group).start())
    live[0] = count[0]
    copies[0].wait()
    copies[1].wait()
    cols = direction.shape[0]
    rim = cols // 2
    table = coupling(classes, cols, range(-REACH, cols))
    weight = smooth[...][:, None, :]
    total = jnp.zeros(norm.shape, jnp.float32)
    values = {c: masked(direction[c]) for c in range(cols)}
    rests = {c: v - v.astype(jnp.bfloat16).astype(jnp.float32) for c, v in values.items()}
    for c in range(cols):
        centre = jnp.float32(1.0)
        for k in range(1, REACH + 1):
            centre = centre + (table[c, k] + table[c - k, k])
        result = weight * (centre * values[c] + pull(table, c, values))
        begun[rim + c] = result
        total = total + jnp.sum(values[c] * result, axis=0)
    low = {c: values[c] for c in range(rim)}
    high = {c: values[c] for c in range(rim, cols)}
    low_rests = {c: rests[c] for c in range(rim)}
    high_rests = {c: rests[c] for c in range(rim, cols)}
    for q in range(rim):
        facing = weight * pull(table, q - rim, high)
        faced[0, q] = facing
        begun[q] = facing + weight * pull(table, q - rim, low_rests)
        facing = weight * pull(table, q + cols, low)
        faced[1, q] = facing + weight * pull(table, q + cols, high)
        begun[rim + cols + q] = facing + weight * pull(table, q + cols, high_rests)
    curved[...] = total
    copies[2].wait()
    slot = lax.broadcasted_iota(jnp.int32, rows.shape, 0)
    rows[...] = jnp.where(slot < count[0], sight[...], 0.0)
    copies[3].wait()
    squares = jnp.zeros(norm.shape, jnp.float32)
    for c in range(cols):
        mres = masked(residual[c])
        squares = squares + jnp.sum(mres * mres, axis=0)
    norm[...] = squares
    copies[4].wait()
    for group in early:
        if_live(count[0], group, lambda: load(group).wait())


def forward_kernel(
    crossing, live, rows, across, within, from_across, from_within, faced, norm, curved, jac, jac_hbm,
    weighted, sums, late, window, total, sem,
):
    slots, crossings = crossing.shape
    last = slot_groups(slots)[-1]
    load = pltpu.make_async_copy(jac_hbm.at[pl.ds(last[0], len(last))], late, sem)
    if_live(live[0], last, load.start)
    rim, species = across.shape[:2]
    span = rim * species
    odd = parity()
    places = (1 + odd, across), (2 - odd, within), (3 * odd, from_across), (3 - 3 * odd, from_within)
    for place, part in places:
        window[pl.ds(place * span, span)] = part[...].reshape(span, *part.shape[2:])
    edges = curved[...]
    for q in range(rim):
        for side, part in (odd, from_across), (1 - odd, from_within):
            edges = edges + 2.0 * jnp.sum(faced[side, q] * part[q].astype(jnp.float32), axis=0)
    total[...] = edges

    def project(group):
        if group == last:
            load.wait()
        added = jnp.zeros(total.shape, jnp.float32)
        for i in group:
            picked = jnp.concatenate([window[crossing[i, j]] for j in range(crossings)], axis=1)
            tiles = slot_tiles(jac, late, i)
            integrals = lax.dot_general(
                picked, tiles, (((1,), (1,)), ((), ())), preferred_element_type=jnp.float32
            )
            product = (rows[pl.ds(i, 1), :] * integrals).astype(jnp.bfloat16)
            weighted[i] = product
            added = added + product.astype(jnp.float32) * integrals
        total[...] += added

    for group in slot_groups(slots):
        if_live(live[0], group, lambda: project(group))
    half = sums.shape[0]
    parts = [jnp.sum(x, axis=1, keepdims=True) for x in (norm[...], total[...])]
    parts = [part[h * half : (h + 1) * half] for h in range(2) for part in parts]
    lane = lax.broadcasted_iota(jnp.int32, sums.shape, 1)
    block = jnp.zeros(sums.shape, jnp.float32)
    for k, part in enumerate(parts):
        block = jnp.where(lane == k, part, block)
    sums[...] = block


def backward_kernel(
    crossing, classes, live, smooth, weighted, jac, late, begun, from_across, from_within,
    image, across, within, sums, near,
):
    slots, crossings = crossing.shape
    cols, species, probes, tile = image.shape
    rim = across.shape[0]
    span = rim * species
    odd = parity()
    near[odd] = from_across[...].astype(jnp.float32)
    near[1 - odd] = from_within[...].astype(jnp.float32)
    table = coupling(classes, cols, range(-rim, cols))
    weight = smooth[...][:, None, :]
    beside = {q - rim: near[0, q] for q in range(rim)} | {q + cols: near[1, q] for q in range(rim)}
    for c in range(cols):
        place = pl.ds(span + c * species, species)
        sums[place] = begun[rim + c] + weight * pull(table, c, beside)
    sums[pl.ds(0, span)] = begun[pl.ds(0, rim)].reshape(span, probes, tile)
    sums[pl.ds(3 * span, span)] = begun[pl.ds(rim + cols, rim)].reshape(span, probes, tile)

    def project(group):
        for i in group:
            tiles = slot_tiles(jac, late, i)
            terms = jnp.dot(weighted[i], tiles, preferred_element_type=jnp.float32)
            for j in range(crossings):
                sums[crossing[i, j]] += terms[:, j * tile : (j + 1) * tile]

    for group in slot_groups(slots):
        if_live(live[0], group, lambda: project(group))
    for part, place in (across, 3 * odd), (within, 3 - 3 * odd):
        part[...] = sums[pl.ds(place * span, span)].astype(part.dtype).reshape(part.shape)
    image[...] = sums[pl.ds(span, 2 * span)].reshape(image.shape)


def final_kernel(
    solution, residual, direction, image, from_across, from_within, *rest
):
    *held, solution_next, residual_next, step_length = rest
    whole = tree_sum([part[...] for part in held])
    norm = jnp.concatenate([whole[:, 0:1], whole[:, 2:3]], axis=0)
    curvature = jnp.concatenate([whole[:, 1:2], whole[:, 3:4]], axis=0)
    step = norm / (curvature + EPSILON)
    rim = from_across.shape[0]
    wide = jnp.broadcast_to(step, direction.shape[2:])
    step_length[...] = jnp.transpose(wide)[0:1]
    wide = wide[None]
    odd = parity()
    for q in range(rim):
        for c, part in (odd * rim + q, from_across), ((1 - odd) * rim + q, from_within):
            total = masked(image[c] + part[q].astype(jnp.float32))
            solution_next[c] = masked(solution[c] + wide * direction[c])
            residual_next[c] = masked(residual[c]) - wide * total


def swapped_across(half):
    count = lax.axis_size("orbit")
    assert count % 2 == 0
    return lax.ppermute(half, "orbit", [(i, (i + 2 * (i % 2) - 1) % count) for i in range(count)])


def swapped_within(half):
    return lax.ppermute(half, "orbit", [(i, i ^ 1) for i in range(lax.axis_size("orbit"))])


def sum_steps(devices):
    assert devices >= 4 and devices & (devices - 1) == 0
    return [[1 << b] for b in range(1, devices.bit_length() - 1)] + [[1]]


def partners(array, bits):
    devices = range(lax.axis_size("orbit"))
    masks = [sum(bit for k, bit in enumerate(bits) if m >> k & 1) for m in range(1, 1 << len(bits))]
    found = {
        mask: lax.ppermute(array, "orbit", [(i, i ^ mask) for i in devices]) for mask in masks[::-1]
    }
    return [found[mask] for mask in masks]


def tree_sum(parts):
    while len(parts) > 1:
        parts = [parts[k] + parts[k + 1] for k in range(0, len(parts), 2)]
    return parts[0]


def local(
    solution, residual, direction, jacobian, crossing, tile_count, sightline_weight,
    length_class, smooth_weight,
):
    cols, species, probes, width = direction.shape
    assert REACH <= cols
    rim = cols // 2
    slots = crossing.shape[0]
    early = early_slots(slots)
    f32, bf16 = jnp.float32, jnp.bfloat16
    shape = jax.ShapeDtypeStruct
    column = (species, probes, width)
    elements = direction.size
    dot_flops = 2 * jacobian.size * probes
    near = shape((rim,) + column, bf16)
    whole = shape(direction.shape, f32)
    small = shape((probes, width), f32)

    held, across, within = call(
        rounding_kernel,
        (whole, near, near),
        [HBM()],
        2 * elements,
        10 * elements,
        [pltpu.SemaphoreType.DMA((2,))],
    )(in_hbm(direction))
    from_across, from_within = swapped_across(across), swapped_within(within)

    begun, faced, norm, curved, rows, jac, crossing, length_class, live = call(
        inner_kernel,
        (
            shape((2 * cols,) + column, f32), shape((2, rim) + column, f32), small, small,
            shape(sightline_weight.shape, f32), shape((early,) + jacobian.shape[1:], bf16),
            pltpu.SMEM(crossing.shape, jnp.int32), pltpu.SMEM(length_class.shape, jnp.int32),
            pltpu.SMEM((8,), jnp.int32),
        ),
        [VMEM(), SMEM()] + [HBM()] * 6,
        60 * elements,
        4 * jacobian.size,
        [
            pltpu.VMEM(direction.shape, f32),
            pltpu.VMEM(smooth_weight.shape, f32),
            pltpu.VMEM(sightline_weight.shape, f32),
            pltpu.SemaphoreType.DMA((5 + len(slot_groups(early)),)),
        ],
        [VMEM()] * 6 + [SMEM()] * 3,
    )(
        held, tile_count,
        *map(in_hbm, (
            residual, length_class, smooth_weight, sightline_weight, crossing, jacobian,
        )),
    )

    devices = lax.axis_size("orbit")
    peers = devices // 2
    weighted, sums, late = call(
        forward_kernel,
        (
            shape((slots, probes, width), bf16), shape((probes // 2, width), f32),
            shape((slots - early,) + jacobian.shape[1:], bf16),
        ),
        [SMEM()] * 2 + [VMEM()] * 9 + [HBM()],
        dot_flops,
        2 * jacobian.size,
        [
            pltpu.VMEM((2 * cols * species, probes, width), bf16),
            pltpu.VMEM((probes, width), f32),
            pltpu.SemaphoreType.DMA,
        ],
    )(
        crossing, live, rows, across, within, from_across, from_within, faced, norm, curved, jac,
        in_hbm(jacobian),
    )
    near_step, *far_steps = sum_steps(devices)
    held = [sums] + partners(sums, near_step)

    image, across, within = call(
        backward_kernel,
        (whole, near, near),
        [SMEM()] * 3 + [VMEM()] * 7,
        dot_flops,
        2 * jacobian.size,
        [
            pltpu.VMEM((2 * cols * species, probes, width), f32),
            pltpu.VMEM((2, rim) + column, f32),
        ],
    )(crossing, length_class, live, smooth_weight, weighted, jac, late, begun, from_across, from_within)
    from_across = swapped_across(across)
    within, *held = lax.optimization_barrier((within, *held))
    sums = tree_sum(held)
    held = [sums] + partners(sums, far_steps[0])
    within, *held = lax.optimization_barrier((within, *held))
    from_within = swapped_within(within)
    for step in far_steps[1:]:
        sums = tree_sum(held)
        held = [sums] + partners(sums, step)

    solution_next, residual_next, step_length = call(
        final_kernel,
        (whole, whole, shape((1, probes), f32)),
        [VMEM()] * (6 + len(held)),
        8 * elements,
        28 * elements,
    )(solution, residual, direction, image, from_across, from_within, *held)
    return solution_next, residual_next, step_length.reshape(probes)


def solution(mesh):
    wide = P(("grp", "orbit"), None, None, None)
    placed = (
        wide, wide, wide, wide,
        P(("grp", "orbit"), None),
        P(("grp", "orbit")),
        P(("grp", "orbit"), None),
        P("grp"),
        P(),
    )
    return jax.shard_map(
        local, mesh=mesh, in_specs=placed, out_specs=(wide, wide, P("grp")), check_vma=False
    )
```

```python
import functools

import jax
import jax.numpy as jnp
from jax import lax
from jax.experimental import pallas as pl
from jax.experimental.pallas import tpu as pltpu
from jax.sharding import PartitionSpec as P

LEVELS = 120
CLASSES = 4
REACH = 8
EPSILON = 1e-06
GROUP = 2
VMEM_LIMIT = 24 * 1024 * 1024

SMEM = functools.partial(pl.BlockSpec, memory_space=pltpu.SMEM)
VMEM = functools.partial(pl.BlockSpec, memory_space=pltpu.VMEM)
HBM = functools.partial(pl.BlockSpec, memory_space=pltpu.HBM)


def in_hbm(array):
    return pltpu.with_memory_space_constraint(array, pltpu.HBM)


def live_lanes(shape):
    return lax.broadcasted_iota(jnp.int32, shape, len(shape) - 1) < LEVELS


def masked(values):
    return jnp.where(live_lanes(values.shape), values, 0.0)


def call(kernel, out_shape, in_specs, flops, moved, scratch=(), out_specs=None):
    return pl.pallas_call(
        kernel,
        out_shape=out_shape,
        in_specs=in_specs,
        out_specs=tuple(out_specs or [VMEM()] * len(out_shape)),
        scratch_shapes=list(scratch),
        compiler_params=pltpu.CompilerParams(vmem_limit_bytes=VMEM_LIMIT),
        cost_estimate=pl.CostEstimate(flops=flops, bytes_accessed=moved, transcendentals=0),
    )


def parity():
    return lax.rem(lax.axis_index("orbit"), 2)


def rounding_kernel(direction_hbm, direction, across, within, sems):
    rim = across.shape[0]
    odd = parity()
    halves = ((odd, across), (1 - odd, within))
    copies = []
    for k, (place, _) in enumerate(halves):
        half = pl.ds(place * rim, rim)
        copies.append(
            pltpu.make_async_copy(direction_hbm.at[half], direction.at[half], sems.at[k])
        )
        copies[-1].start()
    for copy, (place, half) in zip(copies, halves):
        copy.wait()
        for c in range(rim):
            half[c] = masked(direction[place * rim + c]).astype(jnp.bfloat16)


def coupling(classes, cols, columns):
    total = classes.shape[0]
    first = lax.axis_index("orbit") * cols
    table = {}
    for c in columns:
        length = (classes[lax.rem(first + c + total, total)] + 1) * REACH // CLASSES
        for k in range(1, REACH + 1):
            table[c, k] = jnp.where(k <= length, jnp.float32(1.0 / (k * k)), jnp.float32(0.0))
    return table


def pull(table, to, values):
    result = None
    for c, value in values.items():
        if c != to and abs(c - to) <= REACH:
            term = table[min(c, to), abs(c - to)] * value
            result = term if result is None else result + term
    return 0.0 if result is None else -result


def slot_groups(slots):
    return [range(i, min(i + GROUP, slots)) for i in range(0, slots, GROUP)]


def early_slots(slots):
    return slot_groups(slots)[-1][0] if slots > GROUP else slots


def slot_tiles(jac, late, i):
    part, row = (jac, i) if i < jac.shape[0] else (late, i - jac.shape[0])
    return jnp.concatenate([part[row, j] for j in range(part.shape[1])], axis=1)


def if_live(count, group, work):
    if group[0] == 0:
        work()
    else:
        pl.when(group[0] < count)(work)


def inner_kernel(
    direction, count, residual_hbm, classes_hbm, smooth_hbm, sight_hbm, crossing_hbm, jac_hbm,
    begun, faced, norm, curved, rows, jac, crossing, classes, live, residual, smooth, sight, sems,
):
    pairs = (
        (classes_hbm, classes), (smooth_hbm, smooth), (sight_hbm, sight),
        (residual_hbm, residual), (crossing_hbm, crossing),
    )
    copies = [pltpu.make_async_copy(*pair, sems.at[i]) for i, pair in enumerate(pairs)]
    for copy in copies:
        copy.start()

    def load(group):
        part = pl.ds(group[0], len(group))
        return pltpu.make_async_copy(
            jac_hbm.at[part], jac.at[part], sems.at[len(pairs) + group[0] // GROUP]
        )

    early = slot_groups(jac.shape[0])
    for group in early:
        if_live(count[0], group, lambda: load(group).start())
    live[0] = count[0]
    copies[0].wait()
    copies[1].wait()
    cols = direction.shape[0]
    rim = cols // 2
    table = coupling(classes, cols, range(-REACH, cols))
    weight = smooth[...][:, None, :]
    total = jnp.zeros(norm.shape, jnp.float32)
    values = {c: masked(direction[c]) for c in range(cols)}
    rests = {c: v - v.astype(jnp.bfloat16).astype(jnp.float32) for c, v in values.items()}
    for c in range(cols):
        centre = jnp.float32(1.0)
        for k in range(1, REACH + 1):
            centre = centre + (table[c, k] + table[c - k, k])
        result = weight * (centre * values[c] + pull(table, c, values))
        begun[rim + c] = result
        total = total + jnp.sum(values[c] * result, axis=0)
    low = {c: values[c] for c in range(rim)}
    high = {c: values[c] for c in range(rim, cols)}
    low_rests = {c: rests[c] for c in range(rim)}
    high_rests = {c: rests[c] for c in range(rim, cols)}
    for q in range(rim):
        facing = weight * pull(table, q - rim, high)
        faced[0, q] = facing
        begun[q] = facing + weight * pull(table, q - rim, low_rests)
        facing = weight * pull(table, q + cols, low)
        faced[1, q] = facing + weight * pull(table, q + cols, high)
        begun[rim + cols + q] = facing + weight * pull(table, q + cols, high_rests)
    curved[...] = total
    copies[2].wait()
    slot = lax.broadcasted_iota(jnp.int32, rows.shape, 0)
    rows[...] = jnp.where(slot < count[0], sight[...], 0.0)
    copies[3].wait()
    squares = jnp.zeros(norm.shape, jnp.float32)
    for c in range(cols):
        mres = masked(residual[c])
        squares = squares + jnp.sum(mres * mres, axis=0)
    norm[...] = squares
    copies[4].wait()
    for group in early:
        if_live(count[0], group, lambda: load(group).wait())


def forward_kernel(
    crossing, live, rows, across, within, from_across, from_within, faced, norm, curved, jac, jac_hbm,
    weighted, sums, late, window, total, sem,
):
    slots, crossings = crossing.shape
    last = slot_groups(slots)[-1]
    load = pltpu.make_async_copy(jac_hbm.at[pl.ds(last[0], len(last))], late, sem)
    if_live(live[0], last, load.start)
    rim, species = across.shape[:2]
    span = rim * species
    odd = parity()
    places = (1 + odd, across), (2 - odd, within), (3 * odd, from_across), (3 - 3 * odd, from_within)
    for place, part in places:
        window[pl.ds(place * span, span)] = part[...].reshape(span, *part.shape[2:])
    edges = curved[...]
    for q in range(rim):
        for side, part in (odd, from_across), (1 - odd, from_within):
            edges = edges + 2.0 * jnp.sum(faced[side, q] * part[q].astype(jnp.float32), axis=0)
    total[...] = edges

    def project(group):
        if group == last:
            load.wait()
        added = jnp.zeros(total.shape, jnp.float32)
        for i in group:
            picked = jnp.concatenate([window[crossing[i, j]] for j in range(crossings)], axis=1)
            tiles = slot_tiles(jac, late, i)
            integrals = lax.dot_general(
                picked, tiles, (((1,), (1,)), ((), ())), preferred_element_type=jnp.float32
            )
            product = (rows[pl.ds(i, 1), :] * integrals).astype(jnp.bfloat16)
            weighted[i] = product
            added = added + product.astype(jnp.float32) * integrals
        total[...] += added

    for group in slot_groups(slots):
        if_live(live[0], group, lambda: project(group))
    half = sums.shape[0]
    parts = [jnp.sum(x, axis=1, keepdims=True) for x in (norm[...], total[...])]
    parts = [part[h * half : (h + 1) * half] for h in range(2) for part in parts]
    lane = lax.broadcasted_iota(jnp.int32, sums.shape, 1)
    block = jnp.zeros(sums.shape, jnp.float32)
    for k, part in enumerate(parts):
        block = jnp.where(lane == k, part, block)
    sums[...] = block


def backward_kernel(
    crossing, classes, live, smooth, weighted, jac, late, begun, from_across, from_within,
    image, across, within, sums, near,
):
    slots, crossings = crossing.shape
    cols, species, probes, tile = image.shape
    rim = across.shape[0]
    span = rim * species
    odd = parity()
    near[odd] = from_across[...].astype(jnp.float32)
    near[1 - odd] = from_within[...].astype(jnp.float32)
    table = coupling(classes, cols, range(-rim, cols))
    weight = smooth[...][:, None, :]
    beside = {q - rim: near[0, q] for q in range(rim)} | {q + cols: near[1, q] for q in range(rim)}
    for c in range(cols):
        place = pl.ds(span + c * species, species)
        sums[place] = begun[rim + c] + weight * pull(table, c, beside)
    sums[pl.ds(0, span)] = begun[pl.ds(0, rim)].reshape(span, probes, tile)
    sums[pl.ds(3 * span, span)] = begun[pl.ds(rim + cols, rim)].reshape(span, probes, tile)

    def project(group):
        for i in group:
            tiles = slot_tiles(jac, late, i)
            terms = jnp.dot(weighted[i], tiles, preferred_element_type=jnp.float32)
            for j in range(crossings):
                sums[crossing[i, j]] += terms[:, j * tile : (j + 1) * tile]

    for group in slot_groups(slots):
        if_live(live[0], group, lambda: project(group))
    for part, place in (across, 3 * odd), (within, 3 - 3 * odd):
        part[...] = sums[pl.ds(place * span, span)].astype(part.dtype).reshape(part.shape)
    image[...] = sums[pl.ds(span, 2 * span)].reshape(image.shape)


def final_kernel(
    solution, residual, direction, image, from_across, from_within, held,
    solution_next, residual_next, step_length,
):
    whole = jnp.sum(held[...], axis=0)
    norm = jnp.concatenate([whole[:, 0:1], whole[:, 2:3]], axis=0)
    curvature = jnp.concatenate([whole[:, 1:2], whole[:, 3:4]], axis=0)
    step = norm / (curvature + EPSILON)
    rim = from_across.shape[0]
    wide = jnp.broadcast_to(step, direction.shape[2:])
    step_length[...] = jnp.transpose(wide)[0:1]
    wide = wide[None]
    odd = parity()
    for q in range(rim):
        for c, part in (odd * rim + q, from_across), ((1 - odd) * rim + q, from_within):
            total = masked(image[c] + part[q].astype(jnp.float32))
            solution_next[c] = masked(solution[c] + wide * direction[c])
            residual_next[c] = masked(residual[c]) - wide * total


def swapped_across(half):
    count = lax.axis_size("orbit")
    assert count % 2 == 0
    return lax.ppermute(half, "orbit", [(i, (i + 2 * (i % 2) - 1) % count) for i in range(count)])


def swapped_within(half):
    return lax.ppermute(half, "orbit", [(i, i ^ 1) for i in range(lax.axis_size("orbit"))])


def sum_steps(devices):
    assert devices >= 8 and devices & (devices - 1) == 0
    return [1 << b for b in range(1, devices.bit_length() - 2)] + [1 | devices // 2]


def partner(array, bit):
    return lax.ppermute(array, "orbit", [(i, i ^ bit) for i in range(lax.axis_size("orbit"))])


def from_group(array, bits):
    devices = range(lax.axis_size("orbit"))
    groups = [[i for i in devices if i & ~bits == low] for low in devices if low & bits == 0]
    wide = jnp.broadcast_to(array[None], (len(groups[0]),) + array.shape)
    return lax.all_to_all(wide, "orbit", 0, 0, axis_index_groups=groups)


def local(
    solution, residual, direction, jacobian, crossing, tile_count, sightline_weight,
    length_class, smooth_weight,
):
    cols, species, probes, width = direction.shape
    assert REACH <= cols
    rim = cols // 2
    slots = crossing.shape[0]
    early = early_slots(slots)
    f32, bf16 = jnp.float32, jnp.bfloat16
    shape = jax.ShapeDtypeStruct
    column = (species, probes, width)
    elements = direction.size
    dot_flops = 2 * jacobian.size * probes
    near = shape((rim,) + column, bf16)
    whole = shape(direction.shape, f32)
    small = shape((probes, width), f32)

    held, across, within = call(
        rounding_kernel,
        (whole, near, near),
        [HBM()],
        2 * elements,
        10 * elements,
        [pltpu.SemaphoreType.DMA((2,))],
    )(in_hbm(direction))
    from_across, from_within = swapped_across(across), swapped_within(within)

    begun, faced, norm, curved, rows, jac, crossing, length_class, live = call(
        inner_kernel,
        (
            shape((2 * cols,) + column, f32), shape((2, rim) + column, f32), small, small,
            shape(sightline_weight.shape, f32), shape((early,) + jacobian.shape[1:], bf16),
            pltpu.SMEM(crossing.shape, jnp.int32), pltpu.SMEM(length_class.shape, jnp.int32),
            pltpu.SMEM((8,), jnp.int32),
        ),
        [VMEM(), SMEM()] + [HBM()] * 6,
        60 * elements,
        4 * jacobian.size,
        [
            pltpu.VMEM(direction.shape, f32),
            pltpu.VMEM(smooth_weight.shape, f32),
            pltpu.VMEM(sightline_weight.shape, f32),
            pltpu.SemaphoreType.DMA((5 + len(slot_groups(early)),)),
        ],
        [VMEM()] * 6 + [SMEM()] * 3,
    )(
        held, tile_count,
        *map(in_hbm, (
            residual, length_class, smooth_weight, sightline_weight, crossing, jacobian,
        )),
    )

    devices = lax.axis_size("orbit")
    peers = devices // 2
    weighted, sums, late = call(
        forward_kernel,
        (
            shape((slots, probes, width), bf16), shape((probes // 2, width), f32),
            shape((slots - early,) + jacobian.shape[1:], bf16),
        ),
        [SMEM()] * 2 + [VMEM()] * 9 + [HBM()],
        dot_flops,
        2 * jacobian.size,
        [
            pltpu.VMEM((2 * cols * species, probes, width), bf16),
            pltpu.VMEM((probes, width), f32),
            pltpu.SemaphoreType.DMA,
        ],
    )(
        crossing, live, rows, across, within, from_across, from_within, faced, norm, curved, jac,
        in_hbm(jacobian),
    )
    *steps, last_bits = sum_steps(devices)
    held = [sums, partner(sums, steps[0])]

    image, across, within = call(
        backward_kernel,
        (whole, near, near),
        [SMEM()] * 3 + [VMEM()] * 7,
        dot_flops,
        2 * jacobian.size,
        [
            pltpu.VMEM((2 * cols * species, probes, width), f32),
            pltpu.VMEM((2, rim) + column, f32),
        ],
    )(crossing, length_class, live, smooth_weight, weighted, jac, late, begun, from_across, from_within)
    from_across = swapped_across(across)
    for step in steps[1:] + [None]:
        within, *held = lax.optimization_barrier((within, *held))
        sums = held[0] + held[1]
        if step is not None:
            held = [sums, partner(sums, step)]
    from_within = swapped_within(within)
    held = from_group(sums, last_bits)

    solution_next, residual_next, step_length = call(
        final_kernel,
        (whole, whole, shape((1, probes), f32)),
        [VMEM()] * 7,
        8 * elements,
        28 * elements,
    )(solution, residual, direction, image, from_across, from_within, held)
    return solution_next, residual_next, step_length.reshape(probes)


def solution(mesh):
    wide = P(("grp", "orbit"), None, None, None)
    placed = (
        wide, wide, wide, wide,
        P(("grp", "orbit"), None),
        P(("grp", "orbit")),
        P(("grp", "orbit"), None),
        P("grp"),
        P(),
    )
    return jax.shard_map(
        local, mesh=mesh, in_specs=placed, out_specs=(wide, wide, P("grp")), check_vma=False
    )
```

```python
import functools

import jax
import jax.numpy as jnp
from jax import lax
from jax.experimental import pallas as pl
from jax.experimental.pallas import tpu as pltpu
from jax.sharding import PartitionSpec as P

LEVELS = 120
CLASSES = 4
REACH = 8
EPSILON = 1e-06
GROUP = 2
VMEM_LIMIT = 24 * 1024 * 1024

SMEM = functools.partial(pl.BlockSpec, memory_space=pltpu.SMEM)
VMEM = functools.partial(pl.BlockSpec, memory_space=pltpu.VMEM)
HBM = functools.partial(pl.BlockSpec, memory_space=pltpu.HBM)


def in_hbm(array):
    return pltpu.with_memory_space_constraint(array, pltpu.HBM)


def live_lanes(shape):
    return lax.broadcasted_iota(jnp.int32, shape, len(shape) - 1) < LEVELS


def masked(values):
    return jnp.where(live_lanes(values.shape), values, 0.0)


def call(kernel, out_shape, in_specs, flops, moved, scratch=(), out_specs=None):
    return pl.pallas_call(
        kernel,
        out_shape=out_shape,
        in_specs=in_specs,
        out_specs=tuple(out_specs or [VMEM()] * len(out_shape)),
        scratch_shapes=list(scratch),
        compiler_params=pltpu.CompilerParams(vmem_limit_bytes=VMEM_LIMIT),
        cost_estimate=pl.CostEstimate(flops=flops, bytes_accessed=moved, transcendentals=0),
    )


def parity():
    return lax.rem(lax.axis_index("orbit"), 2)


def rounding_kernel(direction_hbm, direction, across, within, sems):
    rim = across.shape[0]
    odd = parity()
    halves = ((odd, across), (1 - odd, within))
    copies = []
    for k, (place, _) in enumerate(halves):
        half = pl.ds(place * rim, rim)
        copies.append(
            pltpu.make_async_copy(direction_hbm.at[half], direction.at[half], sems.at[k])
        )
        copies[-1].start()
    for copy, (place, half) in zip(copies, halves):
        copy.wait()
        for c in range(rim):
            half[c] = masked(direction[place * rim + c]).astype(jnp.bfloat16)


def coupling(classes, cols, columns):
    total = classes.shape[0]
    first = lax.axis_index("orbit") * cols
    table = {}
    for c in columns:
        length = (classes[lax.rem(first + c + total, total)] + 1) * REACH // CLASSES
        for k in range(1, REACH + 1):
            table[c, k] = jnp.where(k <= length, jnp.float32(1.0 / (k * k)), jnp.float32(0.0))
    return table


def pull(table, to, values):
    result = None
    for c, value in values.items():
        if c != to and abs(c - to) <= REACH:
            term = table[min(c, to), abs(c - to)] * value
            result = term if result is None else result + term
    return 0.0 if result is None else -result


def slot_groups(slots):
    return [range(i, min(i + GROUP, slots)) for i in range(0, slots, GROUP)]


def early_slots(slots):
    return slot_groups(slots)[-1][0] if slots > GROUP else slots


def slot_tiles(jac, late, i):
    part, row = (jac, i) if i < jac.shape[0] else (late, i - jac.shape[0])
    return jnp.concatenate([part[row, j] for j in range(part.shape[1])], axis=1)


def if_live(count, group, work):
    if group[0] == 0:
        work()
    else:
        pl.when(group[0] < count)(work)


def inner_kernel(
    direction, count, residual_hbm, classes_hbm, smooth_hbm, sight_hbm, crossing_hbm, jac_hbm,
    begun, faced, norm, curved, rows, jac, crossing, classes, live, residual, smooth, sight, sems,
):
    pairs = (
        (classes_hbm, classes), (smooth_hbm, smooth), (sight_hbm, sight),
        (residual_hbm, residual), (crossing_hbm, crossing),
    )
    copies = [pltpu.make_async_copy(*pair, sems.at[i]) for i, pair in enumerate(pairs)]
    for copy in copies:
        copy.start()

    def load(group):
        part = pl.ds(group[0], len(group))
        return pltpu.make_async_copy(
            jac_hbm.at[part], jac.at[part], sems.at[len(pairs) + group[0] // GROUP]
        )

    early = slot_groups(jac.shape[0])
    for group in early:
        if_live(count[0], group, lambda: load(group).start())
    live[0] = count[0]
    copies[0].wait()
    copies[1].wait()
    cols = direction.shape[0]
    rim = cols // 2
    table = coupling(classes, cols, range(-REACH, cols))
    weight = smooth[...][:, None, :]
    total = jnp.zeros(norm.shape, jnp.float32)
    values = {c: masked(direction[c]) for c in range(cols)}
    rests = {c: v - v.astype(jnp.bfloat16).astype(jnp.float32) for c, v in values.items()}
    for c in range(cols):
        centre = jnp.float32(1.0)
        for k in range(1, REACH + 1):
            centre = centre + (table[c, k] + table[c - k, k])
        result = weight * (centre * values[c] + pull(table, c, values))
        begun[rim + c] = result
        total = total + jnp.sum(values[c] * result, axis=0)
    low = {c: values[c] for c in range(rim)}
    high = {c: values[c] for c in range(rim, cols)}
    low_rests = {c: rests[c] for c in range(rim)}
    high_rests = {c: rests[c] for c in range(rim, cols)}
    for q in range(rim):
        facing = weight * pull(table, q - rim, high)
        faced[0, q] = facing
        begun[q] = facing + weight * pull(table, q - rim, low_rests)
        facing = weight * pull(table, q + cols, low)
        faced[1, q] = facing + weight * pull(table, q + cols, high)
        begun[rim + cols + q] = facing + weight * pull(table, q + cols, high_rests)
    curved[...] = total
    copies[2].wait()
    slot = lax.broadcasted_iota(jnp.int32, rows.shape, 0)
    rows[...] = jnp.where(slot < count[0], sight[...], 0.0)
    copies[3].wait()
    squares = jnp.zeros(norm.shape, jnp.float32)
    for c in range(cols):
        mres = masked(residual[c])
        squares = squares + jnp.sum(mres * mres, axis=0)
    norm[...] = squares
    copies[4].wait()
    for group in early:
        if_live(count[0], group, lambda: load(group).wait())


def forward_kernel(
    crossing, live, rows, across, within, from_across, from_within, faced, norm, curved, jac, jac_hbm,
    weighted, sums, late, window, total, sem,
):
    slots, crossings = crossing.shape
    last = slot_groups(slots)[-1]
    load = pltpu.make_async_copy(jac_hbm.at[pl.ds(last[0], len(last))], late, sem)
    if_live(live[0], last, load.start)
    rim, species = across.shape[:2]
    span = rim * species
    odd = parity()
    places = (1 + odd, across), (2 - odd, within), (3 * odd, from_across), (3 - 3 * odd, from_within)
    for place, part in places:
        window[pl.ds(place * span, span)] = part[...].reshape(span, *part.shape[2:])
    edges = curved[...]
    for q in range(rim):
        for side, part in (odd, from_across), (1 - odd, from_within):
            edges = edges + 2.0 * jnp.sum(faced[side, q] * part[q].astype(jnp.float32), axis=0)
    total[...] = edges

    def project(group):
        if group == last:
            load.wait()
        added = jnp.zeros(total.shape, jnp.float32)
        for i in group:
            picked = jnp.concatenate([window[crossing[i, j]] for j in range(crossings)], axis=1)
            tiles = slot_tiles(jac, late, i)
            integrals = lax.dot_general(
                picked, tiles, (((1,), (1,)), ((), ())), preferred_element_type=jnp.float32
            )
            product = (rows[pl.ds(i, 1), :] * integrals).astype(jnp.bfloat16)
            weighted[i] = product
            added = added + product.astype(jnp.float32) * integrals
        total[...] += added

    for group in slot_groups(slots):
        if_live(live[0], group, lambda: project(group))
    half = sums.shape[0]
    parts = [jnp.sum(x, axis=1, keepdims=True) for x in (norm[...], total[...])]
    parts = [part[h * half : (h + 1) * half] for h in range(2) for part in parts]
    lane = lax.broadcasted_iota(jnp.int32, sums.shape, 1)
    block = jnp.zeros(sums.shape, jnp.float32)
    for k, part in enumerate(parts):
        block = jnp.where(lane == k, part, block)
    sums[...] = block


def backward_kernel(
    crossing, classes, live, smooth, weighted, jac, late, begun, from_across, from_within,
    image, across, within, sums, near,
):
    slots, crossings = crossing.shape
    cols, species, probes, tile = image.shape
    rim = across.shape[0]
    span = rim * species
    odd = parity()
    near[odd] = from_across[...].astype(jnp.float32)
    near[1 - odd] = from_within[...].astype(jnp.float32)
    table = coupling(classes, cols, range(-rim, cols))
    weight = smooth[...][:, None, :]
    beside = {q - rim: near[0, q] for q in range(rim)} | {q + cols: near[1, q] for q in range(rim)}
    for c in range(cols):
        place = pl.ds(span + c * species, species)
        sums[place] = begun[rim + c] + weight * pull(table, c, beside)
    sums[pl.ds(0, span)] = begun[pl.ds(0, rim)].reshape(span, probes, tile)
    sums[pl.ds(3 * span, span)] = begun[pl.ds(rim + cols, rim)].reshape(span, probes, tile)

    def project(group):
        for i in group:
            tiles = slot_tiles(jac, late, i)
            terms = jnp.dot(weighted[i], tiles, preferred_element_type=jnp.float32)
            for j in range(crossings):
                sums[crossing[i, j]] += terms[:, j * tile : (j + 1) * tile]

    for group in slot_groups(slots):
        if_live(live[0], group, lambda: project(group))
    for part, place in (across, 3 * odd), (within, 3 - 3 * odd):
        part[...] = sums[pl.ds(place * span, span)].astype(part.dtype).reshape(part.shape)
    image[...] = sums[pl.ds(span, 2 * span)].reshape(image.shape)


def final_kernel(
    solution, residual, direction, image, from_across, from_within, *rest
):
    *held, solution_next, residual_next, step_length = rest
    whole = tree_sum([part[...] for part in held])
    norm = jnp.concatenate([whole[:, 0:1], whole[:, 2:3]], axis=0)
    curvature = jnp.concatenate([whole[:, 1:2], whole[:, 3:4]], axis=0)
    step = norm / (curvature + EPSILON)
    rim = from_across.shape[0]
    wide = jnp.broadcast_to(step, direction.shape[2:])
    step_length[...] = jnp.transpose(wide)[0:1]
    wide = wide[None]
    odd = parity()
    for q in range(rim):
        for c, part in (odd * rim + q, from_across), ((1 - odd) * rim + q, from_within):
            total = masked(image[c] + part[q].astype(jnp.float32))
            solution_next[c] = masked(solution[c] + wide * direction[c])
            residual_next[c] = masked(residual[c]) - wide * total


def swapped_across(half):
    count = lax.axis_size("orbit")
    assert count % 2 == 0
    return lax.ppermute(half, "orbit", [(i, (i + 2 * (i % 2) - 1) % count) for i in range(count)])


def swapped_within(half):
    return lax.ppermute(half, "orbit", [(i, i ^ 1) for i in range(lax.axis_size("orbit"))])


def sum_steps(devices):
    assert devices >= 8 and devices & (devices - 1) == 0
    return [[1 << b] for b in range(1, devices.bit_length() - 2)] + [[1, devices // 2]]


def partners(array, bits):
    devices = range(lax.axis_size("orbit"))
    masks = [sum(bit for k, bit in enumerate(bits) if m >> k & 1) for m in range(1, 1 << len(bits))]
    found = {
        mask: lax.ppermute(array, "orbit", [(i, i ^ mask) for i in devices]) for mask in masks[::-1]
    }
    return [found[mask] for mask in masks[::-1]]


def tree_sum(parts):
    while len(parts) > 1:
        parts = [parts[k] + parts[k + 1] for k in range(0, len(parts), 2)]
    return parts[0]


def local(
    solution, residual, direction, jacobian, crossing, tile_count, sightline_weight,
    length_class, smooth_weight,
):
    cols, species, probes, width = direction.shape
    assert REACH <= cols
    rim = cols // 2
    slots = crossing.shape[0]
    early = early_slots(slots)
    f32, bf16 = jnp.float32, jnp.bfloat16
    shape = jax.ShapeDtypeStruct
    column = (species, probes, width)
    elements = direction.size
    dot_flops = 2 * jacobian.size * probes
    near = shape((rim,) + column, bf16)
    whole = shape(direction.shape, f32)
    small = shape((probes, width), f32)

    held, across, within = call(
        rounding_kernel,
        (whole, near, near),
        [HBM()],
        2 * elements,
        10 * elements,
        [pltpu.SemaphoreType.DMA((2,))],
    )(in_hbm(direction))
    from_across, from_within = swapped_across(across), swapped_within(within)

    begun, faced, norm, curved, rows, jac, crossing, length_class, live = call(
        inner_kernel,
        (
            shape((2 * cols,) + column, f32), shape((2, rim) + column, f32), small, small,
            shape(sightline_weight.shape, f32), shape((early,) + jacobian.shape[1:], bf16),
            pltpu.SMEM(crossing.shape, jnp.int32), pltpu.SMEM(length_class.shape, jnp.int32),
            pltpu.SMEM((8,), jnp.int32),
        ),
        [VMEM(), SMEM()] + [HBM()] * 6,
        60 * elements,
        4 * jacobian.size,
        [
            pltpu.VMEM(direction.shape, f32),
            pltpu.VMEM(smooth_weight.shape, f32),
            pltpu.VMEM(sightline_weight.shape, f32),
            pltpu.SemaphoreType.DMA((5 + len(slot_groups(early)),)),
        ],
        [VMEM()] * 6 + [SMEM()] * 3,
    )(
        held, tile_count,
        *map(in_hbm, (
            residual, length_class, smooth_weight, sightline_weight, crossing, jacobian,
        )),
    )

    devices = lax.axis_size("orbit")
    peers = devices // 2
    weighted, sums, late = call(
        forward_kernel,
        (
            shape((slots, probes, width), bf16), shape((probes // 2, width), f32),
            shape((slots - early,) + jacobian.shape[1:], bf16),
        ),
        [SMEM()] * 2 + [VMEM()] * 9 + [HBM()],
        dot_flops,
        2 * jacobian.size,
        [
            pltpu.VMEM((2 * cols * species, probes, width), bf16),
            pltpu.VMEM((probes, width), f32),
            pltpu.SemaphoreType.DMA,
        ],
    )(
        crossing, live, rows, across, within, from_across, from_within, faced, norm, curved, jac,
        in_hbm(jacobian),
    )
    near_step, *far_steps = sum_steps(devices)
    held = [sums] + partners(sums, near_step)

    image, across, within = call(
        backward_kernel,
        (whole, near, near),
        [SMEM()] * 3 + [VMEM()] * 7,
        dot_flops,
        2 * jacobian.size,
        [
            pltpu.VMEM((2 * cols * species, probes, width), f32),
            pltpu.VMEM((2, rim) + column, f32),
        ],
    )(crossing, length_class, live, smooth_weight, weighted, jac, late, begun, from_across, from_within)
    from_across = swapped_across(across)
    within, *held = lax.optimization_barrier((within, *held))
    sums = tree_sum(held)
    held = [sums] + partners(sums, far_steps[0])
    within, *held = lax.optimization_barrier((within, *held))
    from_within = swapped_within(within)
    for step in far_steps[1:]:
        sums = tree_sum(held)
        held = [sums] + partners(sums, step)

    solution_next, residual_next, step_length = call(
        final_kernel,
        (whole, whole, shape((1, probes), f32)),
        [VMEM()] * (6 + len(held)),
        8 * elements,
        28 * elements,
    )(solution, residual, direction, image, from_across, from_within, *held)
    return solution_next, residual_next, step_length.reshape(probes)


def solution(mesh):
    wide = P(("grp", "orbit"), None, None, None)
    placed = (
        wide, wide, wide, wide,
        P(("grp", "orbit"), None),
        P(("grp", "orbit")),
        P(("grp", "orbit"), None),
        P("grp"),
        P(),
    )
    return jax.shard_map(
        local, mesh=mesh, in_specs=placed, out_specs=(wide, wide, P("grp")), check_vma=False
    )
```

```python
import functools

import jax
import jax.numpy as jnp
from jax import lax
from jax.experimental import pallas as pl
from jax.experimental.pallas import tpu as pltpu
from jax.sharding import PartitionSpec as P

LEVELS = 120
CLASSES = 4
REACH = 8
EPSILON = 1e-06
GROUP = 2
VMEM_LIMIT = 24 * 1024 * 1024

SMEM = functools.partial(pl.BlockSpec, memory_space=pltpu.SMEM)
VMEM = functools.partial(pl.BlockSpec, memory_space=pltpu.VMEM)
HBM = functools.partial(pl.BlockSpec, memory_space=pltpu.HBM)


def in_hbm(array):
    return pltpu.with_memory_space_constraint(array, pltpu.HBM)


def live_lanes(shape):
    return lax.broadcasted_iota(jnp.int32, shape, len(shape) - 1) < LEVELS


def masked(values):
    return jnp.where(live_lanes(values.shape), values, 0.0)


def call(kernel, out_shape, in_specs, flops, moved, scratch=(), out_specs=None):
    return pl.pallas_call(
        kernel,
        out_shape=out_shape,
        in_specs=in_specs,
        out_specs=tuple(out_specs or [VMEM()] * len(out_shape)),
        scratch_shapes=list(scratch),
        compiler_params=pltpu.CompilerParams(vmem_limit_bytes=VMEM_LIMIT),
        cost_estimate=pl.CostEstimate(flops=flops, bytes_accessed=moved, transcendentals=0),
    )


def parity():
    return lax.rem(lax.axis_index("orbit"), 2)


def rounding_kernel(direction_hbm, direction, across, within, sems):
    rim = across.shape[0]
    odd = parity()
    halves = ((odd, across), (1 - odd, within))
    copies = []
    for k, (place, _) in enumerate(halves):
        half = pl.ds(place * rim, rim)
        copies.append(
            pltpu.make_async_copy(direction_hbm.at[half], direction.at[half], sems.at[k])
        )
        copies[-1].start()
    for copy, (place, half) in zip(copies, halves):
        copy.wait()
        for c in range(rim):
            half[c] = masked(direction[place * rim + c]).astype(jnp.bfloat16)


def coupling(classes, cols, columns):
    total = classes.shape[0]
    first = lax.axis_index("orbit") * cols
    table = {}
    for c in columns:
        length = (classes[lax.rem(first + c + total, total)] + 1) * REACH // CLASSES
        for k in range(1, REACH + 1):
            table[c, k] = jnp.where(k <= length, jnp.float32(1.0 / (k * k)), jnp.float32(0.0))
    return table


def pull(table, to, values):
    result = None
    for c, value in values.items():
        if c != to and abs(c - to) <= REACH:
            term = table[min(c, to), abs(c - to)] * value
            result = term if result is None else result + term
    return 0.0 if result is None else -result


def slot_groups(slots):
    return [range(i, min(i + GROUP, slots)) for i in range(0, slots, GROUP)]


def if_live(count, group, work):
    if group[0] == 0:
        work()
    else:
        pl.when(group[0] < count)(work)


def inner_kernel(
    direction, count, residual_hbm, classes_hbm, smooth_hbm, sight_hbm, crossing_hbm, jac_hbm,
    begun, faced, norm, curved, rows, jac, crossing, classes, live, residual, smooth, sight, sems,
):
    pairs = (
        (classes_hbm, classes), (smooth_hbm, smooth), (sight_hbm, sight),
        (residual_hbm, residual), (crossing_hbm, crossing),
    )
    copies = [pltpu.make_async_copy(*pair, sems.at[i]) for i, pair in enumerate(pairs)]
    for copy in copies:
        copy.start()

    def load(group):
        part = pl.ds(group[0], len(group))
        return pltpu.make_async_copy(
            jac_hbm.at[part], jac.at[part], sems.at[len(pairs) + group[0] // GROUP]
        )

    for group in slot_groups(jac.shape[0]):
        if_live(count[0], group, lambda: load(group).start())
    live[0] = count[0]
    copies[0].wait()
    copies[1].wait()
    cols = direction.shape[0]
    rim = cols // 2
    table = coupling(classes, cols, range(-REACH, cols))
    weight = smooth[...][:, None, :]
    total = jnp.zeros(norm.shape, jnp.float32)
    values = {c: masked(direction[c]) for c in range(cols)}
    rests = {c: v - v.astype(jnp.bfloat16).astype(jnp.float32) for c, v in values.items()}
    for c in range(cols):
        centre = jnp.float32(1.0)
        for k in range(1, REACH + 1):
            centre = centre + (table[c, k] + table[c - k, k])
        result = weight * (centre * values[c] + pull(table, c, values))
        begun[rim + c] = result
        total = total + jnp.sum(values[c] * result, axis=0)
    low = {c: values[c] for c in range(rim)}
    high = {c: values[c] for c in range(rim, cols)}
    low_rests = {c: rests[c] for c in range(rim)}
    high_rests = {c: rests[c] for c in range(rim, cols)}
    for q in range(rim):
        facing = weight * pull(table, q - rim, high)
        faced[0, q] = facing
        begun[q] = facing + weight * pull(table, q - rim, low_rests)
        facing = weight * pull(table, q + cols, low)
        faced[1, q] = facing + weight * pull(table, q + cols, high)
        begun[rim + cols + q] = facing + weight * pull(table, q + cols, high_rests)
    curved[...] = total
    copies[2].wait()
    slot = lax.broadcasted_iota(jnp.int32, rows.shape, 0)
    rows[...] = jnp.where(slot < count[0], sight[...], 0.0)
    copies[3].wait()
    squares = jnp.zeros(norm.shape, jnp.float32)
    for c in range(cols):
        mres = masked(residual[c])
        squares = squares + jnp.sum(mres * mres, axis=0)
    norm[...] = squares
    copies[4].wait()
    for group in slot_groups(jac.shape[0]):
        if_live(count[0], group, lambda: load(group).wait())


def forward_kernel(
    crossing, live, rows, across, within, from_across, from_within, faced, norm, curved, jac,
    weighted, sums, window, total,
):
    slots, crossings = crossing.shape
    rim, species = across.shape[:2]
    span = rim * species
    odd = parity()
    places = (1 + odd, across), (2 - odd, within), (3 * odd, from_across), (3 - 3 * odd, from_within)
    for place, part in places:
        window[pl.ds(place * span, span)] = part[...].reshape(span, *part.shape[2:])
    edges = curved[...]
    for q in range(rim):
        for side, part in (odd, from_across), (1 - odd, from_within):
            edges = edges + 2.0 * jnp.sum(faced[side, q] * part[q].astype(jnp.float32), axis=0)
    total[...] = edges

    def project(group):
        added = jnp.zeros(total.shape, jnp.float32)
        for i in group:
            picked = jnp.concatenate([window[crossing[i, j]] for j in range(crossings)], axis=1)
            tiles = jnp.concatenate([jac[i, j] for j in range(crossings)], axis=1)
            integrals = lax.dot_general(
                picked, tiles, (((1,), (1,)), ((), ())), preferred_element_type=jnp.float32
            )
            product = (rows[pl.ds(i, 1), :] * integrals).astype(jnp.bfloat16)
            weighted[i] = product
            added = added + product.astype(jnp.float32) * integrals
        total[...] += added

    for group in slot_groups(slots):
        if_live(live[0], group, lambda: project(group))
    half = sums.shape[0]
    parts = [jnp.sum(x, axis=1, keepdims=True) for x in (norm[...], total[...])]
    parts = [part[h * half : (h + 1) * half] for h in range(2) for part in parts]
    lane = lax.broadcasted_iota(jnp.int32, sums.shape, 1)
    block = jnp.zeros(sums.shape, jnp.float32)
    for k, part in enumerate(parts):
        block = jnp.where(lane == k, part, block)
    sums[...] = block


def backward_kernel(
    crossing, classes, live, smooth, weighted, jac, begun, from_across, from_within,
    image, across, within, sums, near,
):
    slots, crossings = crossing.shape
    cols, species, probes, tile = image.shape
    rim = across.shape[0]
    span = rim * species
    odd = parity()
    near[odd] = from_across[...].astype(jnp.float32)
    near[1 - odd] = from_within[...].astype(jnp.float32)
    table = coupling(classes, cols, range(-rim, cols))
    weight = smooth[...][:, None, :]
    beside = {q - rim: near[0, q] for q in range(rim)} | {q + cols: near[1, q] for q in range(rim)}
    for c in range(cols):
        place = pl.ds(span + c * species, species)
        sums[place] = begun[rim + c] + weight * pull(table, c, beside)
    sums[pl.ds(0, span)] = begun[pl.ds(0, rim)].reshape(span, probes, tile)
    sums[pl.ds(3 * span, span)] = begun[pl.ds(rim + cols, rim)].reshape(span, probes, tile)

    def project(group):
        for i in group:
            tiles = jnp.concatenate([jac[i, j] for j in range(crossings)], axis=1)
            terms = jnp.dot(weighted[i], tiles, preferred_element_type=jnp.float32)
            for j in range(crossings):
                sums[crossing[i, j]] += terms[:, j * tile : (j + 1) * tile]

    for group in slot_groups(slots):
        if_live(live[0], group, lambda: project(group))
    for part, place in (across, 3 * odd), (within, 3 - 3 * odd):
        part[...] = sums[pl.ds(place * span, span)].astype(part.dtype).reshape(part.shape)
    image[...] = sums[pl.ds(span, 2 * span)].reshape(image.shape)


def final_kernel(
    solution, residual, direction, image, from_across, from_within, *rest
):
    *held, solution_next, residual_next, step_length = rest
    whole = tree_sum([part[...] for part in held])
    norm = jnp.concatenate([whole[:, 0:1], whole[:, 2:3]], axis=0)
    curvature = jnp.concatenate([whole[:, 1:2], whole[:, 3:4]], axis=0)
    step = norm / (curvature + EPSILON)
    rim = from_across.shape[0]
    wide = jnp.broadcast_to(step, direction.shape[2:])
    step_length[...] = jnp.transpose(wide)[0:1]
    wide = wide[None]
    odd = parity()
    for q in range(rim):
        for c, part in (odd * rim + q, from_across), ((1 - odd) * rim + q, from_within):
            total = masked(image[c] + part[q].astype(jnp.float32))
            solution_next[c] = masked(solution[c] + wide * direction[c])
            residual_next[c] = masked(residual[c]) - wide * total


def swapped_across(half):
    count = lax.axis_size("orbit")
    assert count % 2 == 0
    return lax.ppermute(half, "orbit", [(i, (i + 2 * (i % 2) - 1) % count) for i in range(count)])


def swapped_within(half):
    return lax.ppermute(half, "orbit", [(i, i ^ 1) for i in range(lax.axis_size("orbit"))])


def sum_steps(devices):
    assert devices >= 8 and devices & (devices - 1) == 0
    return [[2]] + [[1 << b] for b in range(devices.bit_length() - 2, 2, -1)] + [[1, 4]]


def partners(array, bits):
    devices = range(lax.axis_size("orbit"))
    masks = [sum(bit for k, bit in enumerate(bits) if m >> k & 1) for m in range(1, 1 << len(bits))]
    found = {
        mask: lax.ppermute(array, "orbit", [(i, i ^ mask) for i in devices]) for mask in masks[::-1]
    }
    return [found[mask] for mask in masks]


def tree_sum(parts):
    while len(parts) > 1:
        parts = [parts[k] + parts[k + 1] for k in range(0, len(parts), 2)]
    return parts[0]


def local(
    solution, residual, direction, jacobian, crossing, tile_count, sightline_weight,
    length_class, smooth_weight,
):
    cols, species, probes, width = direction.shape
    assert REACH <= cols
    rim = cols // 2
    slots = crossing.shape[0]
    f32, bf16 = jnp.float32, jnp.bfloat16
    shape = jax.ShapeDtypeStruct
    column = (species, probes, width)
    elements = direction.size
    dot_flops = 2 * jacobian.size * probes
    near = shape((rim,) + column, bf16)
    whole = shape(direction.shape, f32)
    small = shape((probes, width), f32)

    held, across, within = call(
        rounding_kernel,
        (whole, near, near),
        [HBM()],
        2 * elements,
        10 * elements,
        [pltpu.SemaphoreType.DMA((2,))],
    )(in_hbm(direction))
    from_across, from_within = swapped_across(across), swapped_within(within)

    begun, faced, norm, curved, rows, jac, crossing, length_class, live = call(
        inner_kernel,
        (
            shape((2 * cols,) + column, f32), shape((2, rim) + column, f32), small, small,
            shape(sightline_weight.shape, f32), shape(jacobian.shape, bf16),
            pltpu.SMEM(crossing.shape, jnp.int32), pltpu.SMEM(length_class.shape, jnp.int32),
            pltpu.SMEM((8,), jnp.int32),
        ),
        [VMEM(), SMEM()] + [HBM()] * 6,
        60 * elements,
        4 * jacobian.size,
        [
            pltpu.VMEM(direction.shape, f32),
            pltpu.VMEM(smooth_weight.shape, f32),
            pltpu.VMEM(sightline_weight.shape, f32),
            pltpu.SemaphoreType.DMA((5 + len(slot_groups(slots)),)),
        ],
        [VMEM()] * 6 + [SMEM()] * 3,
    )(
        held, tile_count,
        *map(in_hbm, (
            residual, length_class, smooth_weight, sightline_weight, crossing, jacobian,
        )),
    )

    devices = lax.axis_size("orbit")
    peers = devices // 2
    weighted, sums = call(
        forward_kernel,
        (shape((slots, probes, width), bf16), shape((probes // 2, width), f32)),
        [SMEM()] * 2 + [VMEM()] * 9,
        dot_flops,
        2 * jacobian.size,
        [pltpu.VMEM((2 * cols * species, probes, width), bf16), pltpu.VMEM((probes, width), f32)],
    )(crossing, live, rows, across, within, from_across, from_within, faced, norm, curved, jac)
    near_step, *far_steps = sum_steps(devices)
    held = [sums] + partners(sums, near_step)

    image, across, within = call(
        backward_kernel,
        (whole, near, near),
        [SMEM()] * 3 + [VMEM()] * 6,
        dot_flops,
        2 * jacobian.size,
        [
            pltpu.VMEM((2 * cols * species, probes, width), f32),
            pltpu.VMEM((2, rim) + column, f32),
        ],
    )(crossing, length_class, live, smooth_weight, weighted, jac, begun, from_across, from_within)
    from_across = swapped_across(across)
    within, *held = lax.optimization_barrier((within, *held))
    sums = tree_sum(held)
    held = [sums] + partners(sums, far_steps[0])
    within, *held = lax.optimization_barrier((within, *held))
    from_within = swapped_within(within)
    for step in far_steps[1:]:
        sums = tree_sum(held)
        held = [sums] + partners(sums, step)

    solution_next, residual_next, step_length = call(
        final_kernel,
        (whole, whole, shape((1, probes), f32)),
        [VMEM()] * (6 + len(held)),
        8 * elements,
        28 * elements,
    )(solution, residual, direction, image, from_across, from_within, *held)
    return solution_next, residual_next, step_length.reshape(probes)


def solution(mesh):
    wide = P(("grp", "orbit"), None, None, None)
    placed = (
        wide, wide, wide, wide,
        P(("grp", "orbit"), None),
        P(("grp", "orbit")),
        P(("grp", "orbit"), None),
        P("grp"),
        P(),
    )
    return jax.shard_map(
        local, mesh=mesh, in_specs=placed, out_specs=(wide, wide, P("grp")), check_vma=False
    )
```

```python
import functools

import jax
import jax.numpy as jnp
from jax import lax
from jax.experimental import pallas as pl
from jax.experimental.pallas import tpu as pltpu
from jax.sharding import PartitionSpec as P

LEVELS = 120
CLASSES = 4
REACH = 8
EPSILON = 1e-06
GROUP = 2
VMEM_LIMIT = 24 * 1024 * 1024

SMEM = functools.partial(pl.BlockSpec, memory_space=pltpu.SMEM)
VMEM = functools.partial(pl.BlockSpec, memory_space=pltpu.VMEM)
HBM = functools.partial(pl.BlockSpec, memory_space=pltpu.HBM)


def in_hbm(array):
    return pltpu.with_memory_space_constraint(array, pltpu.HBM)


def live_lanes(shape):
    return lax.broadcasted_iota(jnp.int32, shape, len(shape) - 1) < LEVELS


def masked(values):
    return jnp.where(live_lanes(values.shape), values, 0.0)


def call(kernel, out_shape, in_specs, flops, moved, scratch=(), out_specs=None):
    return pl.pallas_call(
        kernel,
        out_shape=out_shape,
        in_specs=in_specs,
        out_specs=tuple(out_specs or [VMEM()] * len(out_shape)),
        scratch_shapes=list(scratch),
        compiler_params=pltpu.CompilerParams(vmem_limit_bytes=VMEM_LIMIT),
        cost_estimate=pl.CostEstimate(flops=flops, bytes_accessed=moved, transcendentals=0),
    )


def parity():
    return lax.rem(lax.axis_index("orbit"), 2)


def rounding_kernel(direction_hbm, direction, across, within, sems):
    rim = across.shape[0]
    odd = parity()
    halves = ((odd, across), (1 - odd, within))
    copies = []
    for k, (place, _) in enumerate(halves):
        half = pl.ds(place * rim, rim)
        copies.append(
            pltpu.make_async_copy(direction_hbm.at[half], direction.at[half], sems.at[k])
        )
        copies[-1].start()
    for copy, (place, half) in zip(copies, halves):
        copy.wait()
        for c in range(rim):
            half[c] = masked(direction[place * rim + c]).astype(jnp.bfloat16)


def coupling(classes, cols, columns):
    total = classes.shape[0]
    first = lax.axis_index("orbit") * cols
    table = {}
    for c in columns:
        length = (classes[lax.rem(first + c + total, total)] + 1) * REACH // CLASSES
        for k in range(1, REACH + 1):
            table[c, k] = jnp.where(k <= length, jnp.float32(1.0 / (k * k)), jnp.float32(0.0))
    return table


def pull(table, to, values):
    result = None
    for c, value in values.items():
        if c != to and abs(c - to) <= REACH:
            term = table[min(c, to), abs(c - to)] * value
            result = term if result is None else result + term
    return 0.0 if result is None else -result


def slot_groups(slots):
    ends = [end for end in (GROUP, 2 * GROUP) if end < slots] + [slots]
    return [range(begin, end) for begin, end in zip([0] + ends, ends)]


def if_live(count, group, work):
    if group[0] == 0:
        work()
    else:
        pl.when(group[0] < count)(work)


def inner_kernel(
    direction, count, residual_hbm, classes_hbm, smooth_hbm, sight_hbm, crossing_hbm, jac_hbm,
    begun, faced, norm, curved, rows, jac, crossing, classes, live, residual, smooth, sight, sems,
):
    pairs = (
        (classes_hbm, classes), (smooth_hbm, smooth), (sight_hbm, sight),
        (residual_hbm, residual), (crossing_hbm, crossing),
    )
    copies = [pltpu.make_async_copy(*pair, sems.at[i]) for i, pair in enumerate(pairs)]
    for copy in copies:
        copy.start()

    def load(group):
        part = pl.ds(group[0], len(group))
        return pltpu.make_async_copy(
            jac_hbm.at[part], jac.at[part], sems.at[len(pairs) + group[0] // GROUP]
        )

    for group in slot_groups(jac.shape[0]):
        if_live(count[0], group, lambda: load(group).start())
    live[0] = count[0]
    copies[0].wait()
    copies[1].wait()
    cols = direction.shape[0]
    rim = cols // 2
    table = coupling(classes, cols, range(-REACH, cols))
    weight = smooth[...][:, None, :]
    total = jnp.zeros(norm.shape, jnp.float32)
    values = {c: masked(direction[c]) for c in range(cols)}
    rests = {c: v - v.astype(jnp.bfloat16).astype(jnp.float32) for c, v in values.items()}
    for c in range(cols):
        centre = jnp.float32(1.0)
        for k in range(1, REACH + 1):
            centre = centre + (table[c, k] + table[c - k, k])
        result = weight * (centre * values[c] + pull(table, c, values))
        begun[rim + c] = result
        total = total + jnp.sum(values[c] * result, axis=0)
    low = {c: values[c] for c in range(rim)}
    high = {c: values[c] for c in range(rim, cols)}
    low_rests = {c: rests[c] for c in range(rim)}
    high_rests = {c: rests[c] for c in range(rim, cols)}
    for q in range(rim):
        facing = weight * pull(table, q - rim, high)
        faced[0, q] = facing
        begun[q] = facing + weight * pull(table, q - rim, low_rests)
        facing = weight * pull(table, q + cols, low)
        faced[1, q] = facing + weight * pull(table, q + cols, high)
        begun[rim + cols + q] = facing + weight * pull(table, q + cols, high_rests)
    curved[...] = total
    copies[2].wait()
    slot = lax.broadcasted_iota(jnp.int32, rows.shape, 0)
    rows[...] = jnp.where(slot < count[0], sight[...], 0.0)
    copies[3].wait()
    squares = jnp.zeros(norm.shape, jnp.float32)
    for c in range(cols):
        mres = masked(residual[c])
        squares = squares + jnp.sum(mres * mres, axis=0)
    norm[...] = squares
    copies[4].wait()
    for group in slot_groups(jac.shape[0]):
        if_live(count[0], group, lambda: load(group).wait())


def forward_kernel(
    crossing, live, rows, across, within, from_across, from_within, faced, norm, curved, jac,
    weighted, sums, window, total,
):
    slots, crossings = crossing.shape
    rim, species = across.shape[:2]
    span = rim * species
    odd = parity()
    places = (1 + odd, across), (2 - odd, within), (3 * odd, from_across), (3 - 3 * odd, from_within)
    for place, part in places:
        window[pl.ds(place * span, span)] = part[...].reshape(span, *part.shape[2:])
    edges = curved[...]
    for q in range(rim):
        for side, part in (odd, from_across), (1 - odd, from_within):
            edges = edges + 2.0 * jnp.sum(faced[side, q] * part[q].astype(jnp.float32), axis=0)
    total[...] = edges

    def project(group):
        added = jnp.zeros(total.shape, jnp.float32)
        for i in group:
            picked = jnp.concatenate([window[crossing[i, j]] for j in range(crossings)], axis=1)
            tiles = jnp.concatenate([jac[i, j] for j in range(crossings)], axis=1)
            integrals = lax.dot_general(
                picked, tiles, (((1,), (1,)), ((), ())), preferred_element_type=jnp.float32
            )
            product = (rows[pl.ds(i, 1), :] * integrals).astype(jnp.bfloat16)
            weighted[i] = product
            added = added + product.astype(jnp.float32) * integrals
        total[...] += added

    for group in slot_groups(slots):
        if_live(live[0], group, lambda: project(group))
    half = sums.shape[0]
    parts = [jnp.sum(x, axis=1, keepdims=True) for x in (norm[...], total[...])]
    parts = [part[h * half : (h + 1) * half] for h in range(2) for part in parts]
    lane = lax.broadcasted_iota(jnp.int32, sums.shape, 1)
    block = jnp.zeros(sums.shape, jnp.float32)
    for k, part in enumerate(parts):
        block = jnp.where(lane == k, part, block)
    sums[...] = block


def backward_kernel(
    crossing, classes, live, smooth, weighted, jac, begun, from_across, from_within,
    image, across, within, sums, near,
):
    slots, crossings = crossing.shape
    cols, species, probes, tile = image.shape
    rim = across.shape[0]
    span = rim * species
    odd = parity()
    near[odd] = from_across[...].astype(jnp.float32)
    near[1 - odd] = from_within[...].astype(jnp.float32)
    table = coupling(classes, cols, range(-rim, cols))
    weight = smooth[...][:, None, :]
    beside = {q - rim: near[0, q] for q in range(rim)} | {q + cols: near[1, q] for q in range(rim)}
    for c in range(cols):
        place = pl.ds(span + c * species, species)
        sums[place] = begun[rim + c] + weight * pull(table, c, beside)
    sums[pl.ds(0, span)] = begun[pl.ds(0, rim)].reshape(span, probes, tile)
    sums[pl.ds(3 * span, span)] = begun[pl.ds(rim + cols, rim)].reshape(span, probes, tile)

    def project(group):
        for i in group:
            tiles = jnp.concatenate([jac[i, j] for j in range(crossings)], axis=1)
            terms = jnp.dot(weighted[i], tiles, preferred_element_type=jnp.float32)
            for j in range(crossings):
                sums[crossing[i, j]] += terms[:, j * tile : (j + 1) * tile]

    for group in slot_groups(slots):
        if_live(live[0], group, lambda: project(group))
    for part, place in (across, 3 * odd), (within, 3 - 3 * odd):
        part[...] = sums[pl.ds(place * span, span)].astype(part.dtype).reshape(part.shape)
    image[...] = sums[pl.ds(span, 2 * span)].reshape(image.shape)


def final_kernel(
    solution, residual, direction, image, from_across, from_within, *rest
):
    *held, solution_next, residual_next, step_length = rest
    whole = tree_sum([part[...] for part in held])
    norm = jnp.concatenate([whole[:, 0:1], whole[:, 2:3]], axis=0)
    curvature = jnp.concatenate([whole[:, 1:2], whole[:, 3:4]], axis=0)
    step = norm / (curvature + EPSILON)
    rim = from_across.shape[0]
    wide = jnp.broadcast_to(step, direction.shape[2:])
    step_length[...] = jnp.transpose(wide)[0:1]
    wide = wide[None]
    odd = parity()
    for q in range(rim):
        for c, part in (odd * rim + q, from_across), ((1 - odd) * rim + q, from_within):
            total = masked(image[c] + part[q].astype(jnp.float32))
            solution_next[c] = masked(solution[c] + wide * direction[c])
            residual_next[c] = masked(residual[c]) - wide * total


def swapped_across(half):
    count = lax.axis_size("orbit")
    assert count % 2 == 0
    return lax.ppermute(half, "orbit", [(i, (i + 2 * (i % 2) - 1) % count) for i in range(count)])


def swapped_within(half):
    return lax.ppermute(half, "orbit", [(i, i ^ 1) for i in range(lax.axis_size("orbit"))])


def sum_steps(devices):
    assert devices >= 8 and devices & (devices - 1) == 0
    return [[2]] + [[1 << b] for b in range(devices.bit_length() - 2, 2, -1)] + [[1, 4]]


def partners(array, bits):
    devices = range(lax.axis_size("orbit"))
    masks = [sum(bit for k, bit in enumerate(bits) if m >> k & 1) for m in range(1, 1 << len(bits))]
    found = {
        mask: lax.ppermute(array, "orbit", [(i, i ^ mask) for i in devices]) for mask in masks[::-1]
    }
    return [found[mask] for mask in masks]


def tree_sum(parts):
    while len(parts) > 1:
        parts = [parts[k] + parts[k + 1] for k in range(0, len(parts), 2)]
    return parts[0]


def local(
    solution, residual, direction, jacobian, crossing, tile_count, sightline_weight,
    length_class, smooth_weight,
):
    cols, species, probes, width = direction.shape
    assert REACH <= cols
    rim = cols // 2
    slots = crossing.shape[0]
    f32, bf16 = jnp.float32, jnp.bfloat16
    shape = jax.ShapeDtypeStruct
    column = (species, probes, width)
    elements = direction.size
    dot_flops = 2 * jacobian.size * probes
    near = shape((rim,) + column, bf16)
    whole = shape(direction.shape, f32)
    small = shape((probes, width), f32)

    held, across, within = call(
        rounding_kernel,
        (whole, near, near),
        [HBM()],
        2 * elements,
        10 * elements,
        [pltpu.SemaphoreType.DMA((2,))],
    )(in_hbm(direction))
    from_across, from_within = swapped_across(across), swapped_within(within)

    begun, faced, norm, curved, rows, jac, crossing, length_class, live = call(
        inner_kernel,
        (
            shape((2 * cols,) + column, f32), shape((2, rim) + column, f32), small, small,
            shape(sightline_weight.shape, f32), shape(jacobian.shape, bf16),
            pltpu.SMEM(crossing.shape, jnp.int32), pltpu.SMEM(length_class.shape, jnp.int32),
            pltpu.SMEM((8,), jnp.int32),
        ),
        [VMEM(), SMEM()] + [HBM()] * 6,
        60 * elements,
        4 * jacobian.size,
        [
            pltpu.VMEM(direction.shape, f32),
            pltpu.VMEM(smooth_weight.shape, f32),
            pltpu.VMEM(sightline_weight.shape, f32),
            pltpu.SemaphoreType.DMA((5 + len(slot_groups(slots)),)),
        ],
        [VMEM()] * 6 + [SMEM()] * 3,
    )(
        held, tile_count,
        *map(in_hbm, (
            residual, length_class, smooth_weight, sightline_weight, crossing, jacobian,
        )),
    )

    devices = lax.axis_size("orbit")
    peers = devices // 2
    weighted, sums = call(
        forward_kernel,
        (shape((slots, probes, width), bf16), shape((probes // 2, width), f32)),
        [SMEM()] * 2 + [VMEM()] * 9,
        dot_flops,
        2 * jacobian.size,
        [pltpu.VMEM((2 * cols * species, probes, width), bf16), pltpu.VMEM((probes, width), f32)],
    )(crossing, live, rows, across, within, from_across, from_within, faced, norm, curved, jac)
    near_step, *far_steps = sum_steps(devices)
    held = [sums] + partners(sums, near_step)

    image, across, within = call(
        backward_kernel,
        (whole, near, near),
        [SMEM()] * 3 + [VMEM()] * 6,
        dot_flops,
        2 * jacobian.size,
        [
            pltpu.VMEM((2 * cols * species, probes, width), f32),
            pltpu.VMEM((2, rim) + column, f32),
        ],
    )(crossing, length_class, live, smooth_weight, weighted, jac, begun, from_across, from_within)
    from_across = swapped_across(across)
    within, *held = lax.optimization_barrier((within, *held))
    sums = tree_sum(held)
    held = [sums] + partners(sums, far_steps[0])
    within, *held = lax.optimization_barrier((within, *held))
    from_within = swapped_within(within)
    for step in far_steps[1:]:
        sums = tree_sum(held)
        held = [sums] + partners(sums, step)

    solution_next, residual_next, step_length = call(
        final_kernel,
        (whole, whole, shape((1, probes), f32)),
        [VMEM()] * (6 + len(held)),
        8 * elements,
        28 * elements,
    )(solution, residual, direction, image, from_across, from_within, *held)
    return solution_next, residual_next, step_length.reshape(probes)


def solution(mesh):
    wide = P(("grp", "orbit"), None, None, None)
    placed = (
        wide, wide, wide, wide,
        P(("grp", "orbit"), None),
        P(("grp", "orbit")),
        P(("grp", "orbit"), None),
        P("grp"),
        P(),
    )
    return jax.shard_map(
        local, mesh=mesh, in_specs=placed, out_specs=(wide, wide, P("grp")), check_vma=False
    )
```
